32 devices in a mesh: dp: 8 (over z, y), mp: 4 (over x, core).
Axes of the slice: x: 2, y: 2, z: 4, core: 2. Of those that a mesh axis runs over, the one named last changes fastest.
Arguments:
- hidden_in: float32 [15360, 768], P('dp'), may hold values from -6 to 6
- roi: float32 [3072, 768], P('dp'), may hold values from -135 to 135, as said below
- bn_gain: float32 [768], replicated, may hold values from 0.1 to 1.9
- bn_bias: float32 [768], replicated, may hold values from -3 to 3
- w_qkv: float32 [3, 768, 768], P(None, None, 'mp'), may hold values from -0.21875 to 0.21875
- bias_qv: float32 [2, 768], P(None, 'mp'), may hold values from -3 to 3
- w_out: float32 [768, 768], P('mp'), may hold values from -0.875 to 0.875
- bias_out: float32 [768], replicated, may hold values from -3 to 3
- ln1_gain: float32 [768], replicated, may hold values from 0.1 to 1.9
- ln1_bias: float32 [768], replicated, may hold values from -3 to 3
- w_in: float32 [768, 3072], P(None, 'mp'), may hold values from -0.21875 to 0.21875
- bias_in: float32 [3072], P('mp'), may hold values from -3 to 3
- w_back: float32 [3072, 768], P('mp'), may hold values from -0.109375 to 0.109375
- bias_back: float32 [768], replicated, may hold values from -3 to 3
- ln2_gain: float32 [768], replicated, may hold values from 0.1 to 1.9
- ln2_bias: float32 [768], replicated, may hold values from -3 to 3
- pair_w: float32 [2, 768, 768], P(None, 'mp'), may hold values from -0.15625 to 0.15625
- pair_bias: float32 [768], replicated, may hold values from -3 to 3
- dir_w: float32 [768, 8], replicated, may hold values from -0.21875 to 0.21875
- text_len: int32 [24], P('dp'), may hold values from 30 to 512, as said below
- owner_order: int32 [8, 384], P('dp'), may hold values from 0 to 383, each once within a row
- pair_index: int32 [2048, 2], P('dp'), may hold values from 0 to 384, as said below
- cot_out: float32 [15360, 768], P('dp'), may hold values from -6 to 6
- cot_logits: float32 [2048, 8], P('dp'), may hold values from -6 to 6
Outputs:
- out: float32 [15360, 768], P('dp')
- logits: float32 [2048, 8], P('dp')
- grad_hidden: float32 [15360, 768], P('dp')
- grad_roi: float32 [3072, 768], P('dp')
- grad_bn_gain: float32 [768], replicated
- grad_bn_bias: float32 [768], replicated
- grad_w_qkv: float32 [3, 768, 768], P(None, None, 'mp')
- grad_bias_qv: float32 [2, 768], P(None, 'mp')
- grad_w_out: float32 [768, 768], P('mp')
- grad_bias_out: float32 [768], replicated
- grad_ln1_gain: float32 [768], replicated
- grad_ln1_bias: float32 [768], replicated
- grad_w_in: float32 [768, 3072], P(None, 'mp')
- grad_bias_in: float32 [3072], P('mp')
- grad_w_back: float32 [3072, 768], P('mp')
- grad_bias_back: float32 [768], replicated
- grad_ln2_gain: float32 [768], replicated
- grad_ln2_bias: float32 [768], replicated
- grad_pair_w: float32 [2, 768, 768], P(None, 'mp')
- grad_pair_bias: float32 [768], replicated
- grad_dir_w: float32 [768, 8], replicated
The draws below stay inside these ranges and needn't reach their ends.
Inputs may be any that keep to these rules, and one draw needn't show every extreme that they name: Document d's first text_len[d] text slots hold text, the rest of its text slots are padding. One document has exactly 512 true text slots, another exactly 30. `owner_order`: row i is a permutation of the 384 segment rows of index i of dp; the k-th entry is sent to owner k // 48. `pair_index`: rows e * 256 to (e + 1) * 256 - 1 are the pair slots of owner e, indexing its received rows; 384 marks an empty slot. Each owner has 192 or more used slots first, then one or more empty ones. `roi`: visual features of the segment rows.
All inputs are finite; a program needn't handle non-finite values.
Results may differ from the reference program's by a relative error of at most 0.0003.
Values sent between devices are 32-bit elements; how exact they have to be, the bound alone decides.
No kernel may reach another device: no remote copies, remote signals or barrier semaphores. Data moves between devices by JAX's collectives and lax.ppermute only.
A program may use at most 192 MiB of HBM per device.

```python
import math
import jax
import jax.numpy as jnp
from jax import lax

D = 768
HEADS = 12
HEAD_DIM = 64
FF = 3072
TEXT = 512
SEGS = 128
DIRS = 8
PAIR_DEV = 256
DOCS = 24
TOKENS = 15360
SEG_DEV = 384
SEND = 48
SEGS_ALL = 3072
NPAIRS = 2048
N_DP = 8


def draw_roi(key, part):
    key = jax.random.fold_in(key, 3)
    key_base, key_scale, key_shift = jax.random.split(key, 3)
    column_scale = jnp.exp(jax.random.uniform(key_scale, (1, D), jnp.float32, 0.0, math.log(10.0)))
    column_shift = jax.random.uniform(key_shift, (1, D), jnp.float32, -0.5, 0.5)
    row_place = lax.broadcasted_iota(jnp.float32, (SEGS_ALL, 1), 0)
    row_scale = 1.0 + 2.0 * row_place / (SEGS_ALL - 1)
    base = jnp.clip(jax.random.normal(key_base, (SEGS_ALL, D), jnp.float32), -4.0, 4.0)
    return ((base + column_shift) * column_scale * row_scale).astype(jnp.float32)


def draw_text_len(key, part):
    key = jax.random.fold_in(key, 5)
    key_len, key_order = jax.random.split(key)
    shortest = min(30, TEXT // 2)
    lengths = jax.random.randint(key_len, (DOCS,), shortest, TEXT + 1)
    ranking = jax.random.permutation(key_order, DOCS)
    lengths = jnp.where(ranking == 0, TEXT, lengths)
    lengths = jnp.where(ranking == 1, shortest, lengths)
    return lengths.astype(jnp.int32)


def draw_pair_index(key, part):
    key = jax.random.fold_in(key, 7)
    key_pick, key_count = jax.random.split(key)
    picks = jax.random.randint(key_pick, (N_DP, PAIR_DEV, 2), 0, SEG_DEV)
    used = jax.random.randint(key_count, (N_DP, 1, 1), 3 * PAIR_DEV // 4, PAIR_DEV)
    slot_place = lax.broadcasted_iota(jnp.int32, (N_DP, PAIR_DEV, 2), 1)
    return jnp.where(slot_place < used, picks, SEG_DEV).reshape(NPAIRS, 2).astype(jnp.int32)


def block_levels(stream_key, shape, cuts, least, high):
    factor_of, own = 1.0, jax.random.fold_in(stream_key, 6)
    for dim, shards_of in cuts:
        steps = jnp.exp(jax.random.uniform(jax.random.fold_in(own, dim), (shards_of,), jnp.float32, least / len(cuts), high / len(cuts)))
        factor_of = factor_of * jnp.repeat(steps, shape[dim] // shards_of).reshape([-1 if axis == dim else 1 for axis in range(len(shape))])
    return factor_of


def scatter_about(rng, shape, deviation, bound, pieces=(), kind=jnp.bfloat16):
    level = block_levels(rng, shape, pieces, -0.22, 0.18) if pieces else 1.0
    drawn = jax.random.normal(rng, shape, jnp.float32) * deviation * level
    return jnp.minimum(jnp.maximum(drawn, -bound), bound).astype(kind)


def setup_inputs(seed: int = 0) -> dict:
    keys = jax.random.split(jax.random.key(seed), 25)
    return {
        "hidden_in": scatter_about(keys[0], (TOKENS, D), 1.0, 6.0, ((0, 8),), jnp.float32),
        "roi": draw_roi(jax.random.fold_in(keys[24], 71), 0),
        "bn_gain": jnp.clip(1.0 + 0.18 * jax.random.normal(keys[2], (D,), jnp.float32), 0.1, 1.9),
        "bn_bias": scatter_about(keys[3], (D,), 0.5, 3.0, (), jnp.float32),
        "w_qkv": scatter_about(keys[4], (3, D, D), D ** -0.5, 0.21875, ((2, 4),), jnp.float32),
        "bias_qv": scatter_about(keys[5], (2, D), 0.5, 3.0, ((1, 4),), jnp.float32),
        "w_out": scatter_about(keys[6], (D, D), (D // 16) ** -0.5, 0.875, ((0, 4),), jnp.float32),
        "bias_out": scatter_about(keys[7], (D,), 0.5, 3.0, (), jnp.float32),
        "ln1_gain": jnp.clip(1.0 + 0.18 * jax.random.normal(keys[8], (D,), jnp.float32), 0.1, 1.9),
        "ln1_bias": scatter_about(keys[9], (D,), 0.5, 3.0, (), jnp.float32),
        "w_in": scatter_about(keys[10], (D, FF), D ** -0.5, 0.21875, ((1, 4),), jnp.float32),
        "bias_in": scatter_about(keys[11], (FF,), 0.5, 3.0, ((0, 4),), jnp.float32),
        "w_back": scatter_about(keys[12], (FF, D), FF ** -0.5, 0.109375, ((0, 4),), jnp.float32),
        "bias_back": scatter_about(keys[13], (D,), 0.5, 3.0, (), jnp.float32),
        "ln2_gain": jnp.clip(1.0 + 0.18 * jax.random.normal(keys[14], (D,), jnp.float32), 0.1, 1.9),
        "ln2_bias": scatter_about(keys[15], (D,), 0.5, 3.0, (), jnp.float32),
        "pair_w": scatter_about(keys[16], (2, D, D), (2 * D) ** -0.5, 0.15625, ((1, 4),), jnp.float32),
        "pair_bias": scatter_about(keys[17], (D,), 0.5, 3.0, (), jnp.float32),
        "dir_w": scatter_about(keys[18], (D, DIRS), D ** -0.5, 0.21875, (), jnp.float32),
        "text_len": draw_text_len(jax.random.fold_in(keys[24], 71), 0),
        "owner_order": jax.vmap(lambda own: jax.random.permutation(own, SEG_DEV))(jax.random.split(keys[20], N_DP)).reshape((N_DP, SEG_DEV)).astype(jnp.int32),
        "pair_index": draw_pair_index(jax.random.fold_in(keys[24], 71), 0),
        "cot_out": scatter_about(keys[22], (TOKENS, D), 1.0, 6.0, ((0, 8),), jnp.float32),
        "cot_logits": scatter_about(keys[23], (NPAIRS, DIRS), 1.0, 6.0, ((0, 8),), jnp.float32),
    }


EPSILON = 1e-05
HIGHEST = lax.Precision.HIGHEST

@jax.custom_vjp
def low(v):
    return lax.optimization_barrier(v.astype(jnp.bfloat16)).astype(jnp.float32)

@jax.custom_vjp
def low_back(v):
    return v

def low_keep(v):
    return (low(v), None)

def low_pass(kept, grad):
    return (grad,)

def back_keep(v):
    return (v, None)

def back_low(kept, grad):
    return (low(grad),)
low.defvjp(low_keep, low_pass)
low_back.defvjp(back_keep, back_low)

def product(operand, other):
    return jnp.dot(operand, other, precision=HIGHEST, preferred_element_type=jnp.float32)

def normalize(values, gain, bias):
    center = values - lax.optimization_barrier(jnp.mean(values, axis=-1, keepdims=True))
    return center * lax.rsqrt(lax.optimization_barrier(jnp.mean(center * center, axis=-1, keepdims=True)) + EPSILON) * gain + bias

def split_heads(tensor):
    return tensor.reshape(tensor.shape[0], HEADS, HEAD_DIM)

def doc_attention(doc_group):
    query_rows, key_rows, value_rows, key_live = doc_group
    scores = jnp.einsum('qhd,khd->hqk', split_heads(query_rows), split_heads(key_rows), precision=HIGHEST) * HEAD_DIM ** (-0.5)
    scores = jnp.where(key_live[None, None, :], scores, -1e+30)
    weights = jax.nn.softmax(scores, axis=-1)
    context = jnp.einsum('hqk,khd->qhd', weights, split_heads(value_rows), precision=HIGHEST)
    return context.reshape(query_rows.shape)

def forward(hidden_in, roi, bn_gain, bn_bias, w_qkv, bias_qv, w_out, bias_out, ln1_gain, ln1_bias, w_in, bias_in, w_back, bias_back, ln2_gain, ln2_bias, pair_w, pair_bias, dir_w, text_len, owner_order, pair_index):
    roi_mean = lax.optimization_barrier(jnp.mean(roi, axis=0))
    roi_center = roi - roi_mean
    roi_var = lax.optimization_barrier(jnp.mean(roi_center * roi_center, axis=0))
    roi_out = roi_center * lax.rsqrt(roi_var + EPSILON) * bn_gain + bn_bias
    slot_count = TEXT + SEGS
    doc_blocks = hidden_in.reshape(DOCS, slot_count, D)
    doc_blocks = jnp.concatenate([doc_blocks[:, :TEXT], doc_blocks[:, TEXT:] + roi_out.reshape(DOCS, SEGS, D)], axis=1)
    layer_input = doc_blocks.reshape(TOKENS, D)
    position = jnp.arange(slot_count, dtype=jnp.int32)
    key_live = (position[None, :] < text_len[:, None]) | (position[None, :] >= TEXT)
    query_rows = product(layer_input, w_qkv[0]) + bias_qv[0]
    key_rows = product(layer_input, w_qkv[1])
    value_rows = product(layer_input, w_qkv[2]) + bias_qv[1]
    context = lax.map(jax.checkpoint(doc_attention), (query_rows.reshape(DOCS, slot_count, D), key_rows.reshape(DOCS, slot_count, D), value_rows.reshape(DOCS, slot_count, D), key_live))
    context = context.reshape(TOKENS, D)
    hidden_one = normalize(layer_input + product(context, w_out) + bias_out, ln1_gain, ln1_bias)
    inner_act = jax.nn.gelu(product(hidden_one, w_in) + bias_in, approximate=False)
    output = normalize(hidden_one + product(inner_act, w_back) + bias_back, ln2_gain, ln2_bias)
    segments = output.reshape(DOCS, slot_count, D)[:, TEXT:].reshape(N_DP, SEG_DEV, D)
    ordered = jnp.take_along_axis(segments, owner_order[:, :, None].astype(jnp.int32), axis=1)
    received = ordered.reshape(N_DP, N_DP, SEND, D).transpose(1, 0, 2, 3).reshape(N_DP, SEG_DEV, D)
    candidates = jnp.arange(SEG_DEV, dtype=jnp.int32)
    pairs = pair_index.reshape(N_DP, PAIR_DEV, 2)
    pick_left = (pairs[:, :, 0:1] == candidates[None, None, :]).astype(jnp.float32)
    pick_right = (pairs[:, :, 1:2] == candidates[None, None, :]).astype(jnp.float32)
    left_rows = jnp.einsum('eps,esd->epd', pick_left, received, precision=HIGHEST).reshape(NPAIRS, D)
    right_rows = jnp.einsum('eps,esd->epd', pick_right, received, precision=HIGHEST).reshape(NPAIRS, D)
    pair_pre = product(left_rows, pair_w[0]) + product(right_rows, pair_w[1]) + pair_bias
    logits = product(jax.nn.gelu(pair_pre, approximate=False), dir_w)
    return (output, logits)

def reference(hidden_in, roi, bn_gain, bn_bias, w_qkv, bias_qv, w_out, bias_out, ln1_gain, ln1_bias, w_in, bias_in, w_back, bias_back, ln2_gain, ln2_bias, pair_w, pair_bias, dir_w, text_len, owner_order, pair_index, cot_out, cot_logits):

    def apply(hidden_in, roi, bn_gain, bn_bias, w_qkv, bias_qv, w_out, bias_out, ln1_gain, ln1_bias, w_in, bias_in, w_back, bias_back, ln2_gain, ln2_bias, pair_w, pair_bias, dir_w):
        return forward(hidden_in, roi, bn_gain, bn_bias, w_qkv, bias_qv, w_out, bias_out, ln1_gain, ln1_bias, w_in, bias_in, w_back, bias_back, ln2_gain, ln2_bias, pair_w, pair_bias, dir_w, text_len, owner_order, pair_index)
    (output, logits), pull = jax.vjp(apply, hidden_in, roi, bn_gain, bn_bias, w_qkv, bias_qv, w_out, bias_out, ln1_gain, ln1_bias, w_in, bias_in, w_back, bias_back, ln2_gain, ln2_bias, pair_w, pair_bias, dir_w)
    grad_hidden, grad_roi, grad_bn_gain, grad_bn_bias, grad_w_qkv, grad_bias_qv, grad_w_out, grad_bias_out, grad_ln1_gain, grad_ln1_bias, grad_w_in, grad_bias_in, grad_w_back, grad_bias_back, grad_ln2_gain, grad_ln2_bias, grad_pair_w, grad_pair_bias, grad_dir_w = pull((cot_out, cot_logits))
    return (output, logits, grad_hidden, grad_roi, grad_bn_gain, grad_bn_bias, grad_w_qkv, grad_bias_qv, grad_w_out, grad_bias_out, grad_ln1_gain, grad_ln1_bias, grad_w_in, grad_bias_in, grad_w_back, grad_bias_back, grad_ln2_gain, grad_ln2_bias, grad_pair_w, grad_pair_bias, grad_dir_w)
```

```python
import functools

import jax
import jax.numpy as jnp
from jax import lax
from jax.experimental import pallas as pl
from jax.experimental.pallas import tpu as pltpu
from jax.sharding import PartitionSpec as P

HEAD_DIM = 64
TEXT = 512
EPSILON = 1e-05
NEGATIVE = -1e30
ROOT_HALF = 0.7071067811865476
DENSITY = 0.3989422804014327
HIGH = lax.Precision.HIGH
F32 = jnp.float32
BF16 = jnp.bfloat16
VMEM_LIMIT = 56 << 20


def product(operand, other, dims=((1,), (0,))):
    return lax.dot_general(
        operand, other, (dims, ((), ())), precision=HIGH, preferred_element_type=F32
    )


def halves(x):
    hi = x.astype(BF16)
    return hi, (x - hi.astype(F32)).astype(BF16)


def dot(a, b, dims=((1,), (0,))):
    return lax.dot_general(a, b, (dims, ((), ())), preferred_element_type=F32)


ROWS_BY_ROWS = ((1,), (1,))
COLS_BY_COLS = ((0,), (0,))


def dot3(a, b, dims=((1,), (0,))):
    return dot(a[0], b[0], dims) + dot(a[1], b[0], dims) + dot(a[0], b[1], dims)


def gelu_parts(v):
    density = jnp.exp(-0.5 * v * v)
    t = 1.0 / (1.0 + (0.3275911 * ROOT_HALF) * jnp.abs(v))
    poly = t * (
        0.127414796
        + t * (-0.142248368 + t * (0.7107068705 + t * (-0.7265760135 + t * 0.5307027145)))
    )
    tail = poly * density
    phi = jnp.where(v >= 0, 1.0 - tail, tail)
    return v * phi, phi + v * density * DENSITY


def normalize_rows(y):
    center = y - jnp.mean(y, axis=-1, keepdims=True)
    factor = lax.rsqrt(jnp.mean(center * center, axis=-1, keepdims=True) + EPSILON)
    return center * factor, factor


def normalize_rows_back(upstream, normed, factor):
    return factor * (
        upstream
        - jnp.mean(upstream, axis=-1, keepdims=True)
        - normed * jnp.mean(upstream * normed, axis=-1, keepdims=True)
    )


def colsum(x):
    return jnp.sum(x, axis=0, keepdims=True)


def lane_is(rows, width, lane):
    return lax.broadcasted_iota(jnp.int32, (rows, width), 1) == lane


def batch_normed(roi, bn):
    return (roi - bn[0:1]) * bn[1:2]


def split_pieces(pieces, where_hi, where_lo, shift, rows):
    if len(pieces) == 1:
        where_hi[:rows], where_lo[:rows] = halves(pieces[0][...])
    else:
        half = rows // 2
        for piece, place in zip(pieces, (shift, 1 - shift)):
            at = pl.ds(pl.multiple_of(place * half, half), half)
            where_hi[at], where_lo[at] = halves(piece[...])


def attn_fwd_kernel(n_pieces, with_rows, segs, heads, *refs):
    place, lens, hid, roi, bn, bias = refs[:6]
    pieces = refs[6 : 6 + n_pieces]
    refs = refs[6 + n_pieces :]
    qkv, lse, cm_seg, cm_txt, ct_seg, ct_txt = refs[:6]
    refs = refs[6:]
    if with_rows:
        xm_seg, xm_txt = refs[:2]
        refs = refs[2:]
    w_hi, w_lo, x_seg, ctx = refs
    doc = pl.program_id(0)
    c = place[0]
    width = heads * HEAD_DIM
    slots = TEXT + segs

    @pl.when(doc == 0)
    def _():
        split_pieces(pieces, w_hi, w_lo, place[1], w_hi.shape[0])

    x_seg[...] = hid[TEXT:, :] + batch_normed(roi[...], bn) * bn[2:3] + bn[3:4]
    w = (w_hi[...], w_lo[...])
    half = TEXT // 2
    for start in (0, half):
        qkv[start : start + half, :] = dot3(halves(hid[start : start + half, :]), w) + bias[0:1]
    qkv[TEXT:, :] = dot3(halves(x_seg[...]), w) + bias[0:1]

    position = lax.broadcasted_iota(jnp.int32, (slots, HEAD_DIM), 0)
    first = lane_is(slots, HEAD_DIM, 0)
    dead = (position >= lens[doc]) & (position < TEXT)
    key_extra = jnp.where(first & dead, NEGATIVE, 0.0).astype(BF16)
    ones = jnp.where(first, 1.0, 0.0).astype(BF16)
    step = 128
    for h in range(heads):
        at = h * HEAD_DIM
        q_hi, q_lo = halves(qkv[:, at : at + HEAD_DIM] * HEAD_DIM**-0.5)
        k_hi, k_lo = halves(qkv[:, width + at : width + at + HEAD_DIM])
        v_hi, v_lo = halves(qkv[:, 2 * width + at : 2 * width + at + HEAD_DIM])
        q_pack = jnp.concatenate([q_hi, q_lo, q_hi, ones], axis=1)
        k_pack = jnp.concatenate([k_hi, k_hi, k_lo, key_extra], axis=1)
        v_pack = jnp.concatenate([v_hi, v_lo, ones, jnp.zeros_like(ones)], axis=1)
        for start in range(0, slots, step):
            rows = slice(start, start + step)
            scores = dot(q_pack[rows], k_pack, ROWS_BY_ROWS)
            top = jnp.max(scores, axis=-1, keepdims=True)
            p_hi, p_lo = halves(jnp.exp(scores - top))
            mixed = dot(p_hi, v_pack) + dot(p_lo, v_pack)
            total = mixed[:, 2 * HEAD_DIM : 2 * HEAD_DIM + 1]
            ctx[rows, at : at + HEAD_DIM] = (
                mixed[:, :HEAD_DIM] + mixed[:, HEAD_DIM : 2 * HEAD_DIM]
            ) / total
            logsum = top + jnp.log(total)
            if h == 0:
                lse[rows, :] = jnp.broadcast_to(logsum, (step, 128))
            else:
                lse[rows, :] = jnp.where(lane_is(step, 128, h), logsum, lse[rows, :])
    half_seg = segs // 2
    for seg, txt, side in ((cm_seg, cm_txt, c), (ct_seg, ct_txt, 1 - c)):
        seg[...] = ctx[pl.ds(pl.multiple_of(TEXT + side * half_seg, half_seg), half_seg), :]
        txt[...] = ctx[pl.ds(pl.multiple_of(side * half, half), half), :]
    if with_rows:
        xm_seg[...] = x_seg[pl.ds(pl.multiple_of(c * half_seg, half_seg), half_seg), :]
        xm_txt[...] = hid[pl.ds(pl.multiple_of(c * half, half), half), :]


def smem():
    return pl.BlockSpec(memory_space=pltpu.SMEM)


def whole(shape):
    return pl.BlockSpec(shape, lambda *_: (0,) * len(shape))


def attn_fwd(place, lens, hidden, roi, bn, bias, pieces, with_rows):
    docs = lens.shape[0]
    slots, width = hidden.shape[0] // docs, hidden.shape[1]
    segs = slots - TEXT
    cols = pieces[0].shape[1]
    part = cols // 3
    heads = part // HEAD_DIM
    out_rows = [
        (slots, cols),
        (slots, 128),
        (segs // 2, part),
        (TEXT // 2, part),
        (segs // 2, part),
        (TEXT // 2, part),
    ]
    if with_rows:
        out_rows += [(segs // 2, width), (TEXT // 2, width)]
    by_doc = lambda shape: pl.BlockSpec(shape, lambda d: (d, 0))
    return pl.pallas_call(
        functools.partial(attn_fwd_kernel, len(pieces), with_rows, segs, heads),
        grid=(docs,),
        in_specs=[smem(), smem(), by_doc((slots, width)), by_doc((segs, width)), whole(bn.shape), whole(bias.shape)]
        + [whole(p.shape) for p in pieces],
        out_specs=[by_doc(s) for s in out_rows],
        out_shape=[jax.ShapeDtypeStruct((docs * s[0], s[1]), F32) for s in out_rows],
        scratch_shapes=[
            pltpu.VMEM((width, cols), BF16),
            pltpu.VMEM((width, cols), BF16),
            pltpu.VMEM((segs, width), F32),
            pltpu.VMEM((slots, part), F32),
        ],
        compiler_params=pltpu.CompilerParams(vmem_limit_bytes=VMEM_LIMIT),
        name="attn_fwd",
    )(place, lens, hidden, roi, bn, bias, *pieces)


def attn_bwd_kernel(segs, heads, doc, *refs):
    (place, lens, hid, roi, bn) = refs[:5]
    pieces = (refs[5:6], refs[6:8])
    qkvs, lses = refs[8:10], refs[10:12]
    ctxs = (refs[12:16], refs[16:20])
    gcm_seg, gcm_txt, gct_seg, gct_txt = refs[20:24]
    w_sum, b_sum = refs[24:26]
    gx, w_out, b_out = refs[26:29]
    w_hi, w_lo, o_all, g_all, gq, x_all = refs[29:]
    c = place[0]
    width = heads * HEAD_DIM
    slots = TEXT + segs
    half, half_seg = TEXT // 2, segs // 2
    model = hid.shape[1]
    for s in range(2):
        at = s * model
        split_pieces(
            pieces[s], w_hi.at[at : at + model], w_lo.at[at : at + model], place[1], model
        )

    def place_rows(dst, lanes, seg, txt, side):
        dst[pl.ds(pl.multiple_of(TEXT + side * half_seg, half_seg), half_seg), lanes] = seg
        dst[pl.ds(pl.multiple_of(side * half, half), half), lanes] = txt

    for s in range(2):
        lanes = slice(s * width, (s + 1) * width)
        seg_m, txt_m, seg_t, txt_t = ctxs[s]
        place_rows(o_all.at[s], slice(0, width), seg_m[...], txt_m[...], c)
        place_rows(o_all.at[s], slice(0, width), seg_t[...], txt_t[...], 1 - c)
        place_rows(g_all.at[s], slice(0, width), gcm_seg[:, lanes], gcm_txt[:, lanes], c)
        place_rows(g_all.at[s], slice(0, width), gct_seg[:, lanes], gct_txt[:, lanes], 1 - c)
    x_all[:TEXT, :] = hid[:TEXT, :]
    x_all[TEXT:, :] = hid[TEXT:, :] + batch_normed(roi[...], bn) * bn[2:3] + bn[3:4]

    position = lax.broadcasted_iota(jnp.int32, (slots, HEAD_DIM), 0)
    lane = lax.broadcasted_iota(jnp.int32, (slots, HEAD_DIM), 1)
    dead = (position >= lens[doc]) & (position < TEXT)
    key_extra = jnp.where(
        lane == 3, jnp.where(dead, NEGATIVE, 0.0), jnp.where(lane < 3, 1.0, 0.0)
    ).astype(BF16)
    val_extra = jnp.where(lane < 3, 1.0, 0.0).astype(BF16)

    def column_extra(col, last):
        hi = (-col).astype(BF16)
        rest = -col - hi.astype(F32)
        mid = rest.astype(BF16)
        low = (rest - mid.astype(F32)).astype(BF16)
        return jnp.where(
            lane == 0,
            hi.astype(F32),
            jnp.where(
                lane == 1,
                mid.astype(F32),
                jnp.where(lane == 2, low.astype(F32), jnp.where(lane == 3, last, 0.0)),
            ),
        ).astype(BF16)

    step = 128
    scale = HEAD_DIM**-0.5
    for s in range(2):
        qkv = qkvs[s]
        for h in range(heads):
            at = h * HEAD_DIM
            q_hi, q_lo = halves(qkv[:, at : at + HEAD_DIM] * scale)
            k_hi, k_lo = halves(qkv[:, width + at : width + at + HEAD_DIM])
            v_hi, v_lo = halves(qkv[:, 2 * width + at : 2 * width + at + HEAD_DIM])
            g = g_all[s, :, at : at + HEAD_DIM]
            g_hi, g_lo = halves(g)
            inner = jnp.sum(g * o_all[s, :, at : at + HEAD_DIM], axis=-1, keepdims=True)
            q_pack = jnp.concatenate(
                [q_hi, q_lo, q_hi, column_extra(lses[s][:, h : h + 1], 1.0)], axis=1
            )
            k_pack = jnp.concatenate([k_hi, k_hi, k_lo, key_extra], axis=1)
            g_pack = jnp.concatenate([g_hi, g_lo, g_hi, column_extra(inner, 0.0)], axis=1)
            v_pack = jnp.concatenate([v_hi, v_hi, v_lo, val_extra], axis=1)
            q_two = jnp.concatenate([q_hi, q_lo], axis=1)
            k_two = jnp.concatenate([k_hi, k_lo], axis=1)
            g_two = jnp.concatenate([g_hi, g_lo], axis=1)
            grad_q = jnp.zeros((slots, 2 * HEAD_DIM), F32)
            for start in range(0, slots, step):
                rows = slice(start, start + step)
                weights = jnp.exp(dot(k_pack[rows], q_pack, ROWS_BY_ROWS))
                grads = weights * dot(v_pack[rows], g_pack, ROWS_BY_ROWS)
                w_two = halves(weights)
                s_two = halves(grads)
                grad_v = dot(w_two[0], g_two) + dot(w_two[1], g_two)
                grad_k = dot(s_two[0], q_two) + dot(s_two[1], q_two)
                gq[rows, width + at : width + at + HEAD_DIM] = (
                    grad_k[:, :HEAD_DIM] + grad_k[:, HEAD_DIM:]
                )
                gq[rows, 2 * width + at : 2 * width + at + HEAD_DIM] = (
                    grad_v[:, :HEAD_DIM] + grad_v[:, HEAD_DIM:]
                )
                grad_q = (
                    grad_q
                    + dot(s_two[0], k_two[rows], COLS_BY_COLS)
                    + dot(s_two[1], k_two[rows], COLS_BY_COLS)
                )
            gq[:, at : at + HEAD_DIM] = (grad_q[:, :HEAD_DIM] + grad_q[:, HEAD_DIM:]) * scale
        w = (w_hi[s * model : (s + 1) * model, :], w_lo[s * model : (s + 1) * model, :])
        for start in range(0, slots, 2 * step):
            rows = slice(start, min(slots, start + 2 * step))
            part = dot3(halves(gq[rows, :]), w, ROWS_BY_ROWS)
            if s == 0:
                gx[rows, :] = part
            else:
                gx[rows, :] += part
        if s == 0:
            b_out[...] = b_sum[...] + colsum(gq[...])
            w_out[...] = w_sum[...] + dot3(halves(gq[...]), halves(x_all[...]), COLS_BY_COLS)


def attn_bwd(doc, place, lens, hidden, roi, bn, own, other, qkvs, lses, ctxs, grads, w_sum, b_sum):
    docs = lens.shape[0]
    slots, width = hidden.shape[0] // docs, hidden.shape[1]
    segs = slots - TEXT
    cols = own[0].shape[1]
    part = cols // 3
    heads = part // HEAD_DIM
    by_doc = lambda rows, lanes: pl.BlockSpec((rows, lanes), lambda i: (doc, 0))
    half, half_seg = TEXT // 2, segs // 2
    return pl.pallas_call(
        functools.partial(attn_bwd_kernel, segs, heads, doc),
        grid=(1,),
        in_specs=[smem(), smem(), by_doc(slots, width), by_doc(segs, width), whole(bn.shape)]
        + [whole(p.shape) for p in (*own, *other)]
        + [by_doc(slots, cols)] * 2
        + [by_doc(slots, 128)] * 2
        + [by_doc(half_seg, part), by_doc(half, part)] * 4
        + [by_doc(half_seg, 2 * part), by_doc(half, 2 * part)] * 2
        + [whole((cols, width)), whole((1, cols))],
        out_specs=[whole((slots, width)), whole((cols, width)), whole((1, cols))],
        out_shape=[
            jax.ShapeDtypeStruct((slots, width), F32),
            jax.ShapeDtypeStruct((cols, width), F32),
            jax.ShapeDtypeStruct((1, cols), F32),
        ],
        scratch_shapes=[
            pltpu.VMEM((2 * width, cols), BF16),
            pltpu.VMEM((2 * width, cols), BF16),
            pltpu.VMEM((2, slots, part), F32),
            pltpu.VMEM((2, slots, part), F32),
            pltpu.VMEM((slots, cols), F32),
            pltpu.VMEM((slots, width), F32),
        ],
        compiler_params=pltpu.CompilerParams(vmem_limit_bytes=VMEM_LIMIT),
        name="attn_bwd",
    )(place, lens, hidden, roi, bn, *own, *other, *qkvs, *lses, *ctxs[0], *ctxs[1], *grads, w_sum, b_sum)


BIAS_OUT, LN1_GAIN, LN1_BIAS, BIAS_BACK, LN2_GAIN, LN2_BIAS = range(6)
PIECE_SHARDS = (0, 1, 2, 2, 3, 3)


def row_chunks(rows, most=256):
    step = min(rows, most)
    return [slice(start, start + step) for start in range(0, rows, step)]


def piece_place(i, rows, shift):
    if i < 2:
        return 0
    half = rows // 2
    return pl.multiple_of((shift if i % 2 == 0 else 1 - shift) * half, half)


def ffn_fwd_kernel(split, *refs):
    place = refs[0]
    ctx = refs[1:5]
    xres, vec, bias_in = refs[5:8]
    refs = refs[8:]
    if split:
        wo_pieces, wi_pieces, wb_pieces = refs[:6], refs[6:12], refs[12:18]
        refs = refs[18:]
    else:
        wo_ref, wt_ref = refs[:2]
        refs = refs[2:]
    out, n1, f1, n2, f2, act, slope = refs[:7]
    refs = refs[7:]
    if split:
        wo_ref, wt_ref = refs[:2]
        refs = refs[2:]
        wbuf, sems = refs[-2:]
        refs = refs[:-2]
    h_hi, h_lo, acc = refs
    t = pl.program_id(0)
    tiles = 4
    rows = xres.shape[0]
    head_rows = ctx[0].shape[1]
    width = xres.shape[1]

    if split:
        shift = place[1]

        def copies(tile):
            found = []
            for i in range(6):
                if PIECE_SHARDS[i] != tile:
                    continue
                for k, pieces in enumerate((wi_pieces, wb_pieces)):
                    ref = pieces[i]
                    at = piece_place(i, width, shift)
                    found.append(
                        pltpu.make_async_copy(
                            ref, wbuf.at[k, pl.ds(at, ref.shape[0]), :], sems.at[len(found)]
                        )
                    )
            return found

        @pl.when(t == 0)
        def _():
            for copy in copies(0):
                copy.start()
            for i in range(6):
                at = PIECE_SHARDS[i] * head_rows + piece_place(i, head_rows, shift)
                where = pl.ds(at, wo_pieces[i].shape[0])
                wo_ref[0, where, :], wo_ref[1, where, :] = halves(wo_pieces[i][...])

        for tile in range(tiles):

            @pl.when(t == tile)
            def _():
                for copy in copies(tile):
                    copy.wait()

        wt_ref[0, 0], wt_ref[0, 1] = halves(wbuf[0])
        wt_ref[0, 2], wt_ref[0, 3] = halves(wbuf[1])
        for tile in range(tiles - 1):

            @pl.when(t == tile)
            def _():
                for copy in copies(tile + 1):
                    copy.start()

    @pl.when(t == 0)
    def _():
        for r in row_chunks(rows):
            y = xres[r, :] + vec[BIAS_OUT : BIAS_OUT + 1]
            for s in range(4):
                at = slice(s * head_rows, (s + 1) * head_rows)
                y = y + dot3(halves(ctx[s][r, :]), (wo_ref[0, at, :], wo_ref[1, at, :]))
            normed, factor = normalize_rows(y)
            n1[r, :] = normed
            f1[r, :] = jnp.broadcast_to(factor, (factor.shape[0], 128))
            h = normed * vec[LN1_GAIN : LN1_GAIN + 1] + vec[LN1_BIAS : LN1_BIAS + 1]
            h_hi[r, :], h_lo[r, :] = halves(h)
            acc[r, :] = h + vec[BIAS_BACK : BIAS_BACK + 1]

    w_in = (wt_ref[0, 0], wt_ref[0, 1])
    w_back = (wt_ref[0, 2], wt_ref[0, 3])
    bias = bias_in[pl.ds(t, 1), :]
    for r in row_chunks(rows):
        pre = dot3((h_hi[r, :], h_lo[r, :]), w_in) + bias
        value, rise = gelu_parts(pre)
        slope[0, r, :] = rise

        @pl.when(t < 2)
        def _():
            act[0, r, :] = value

        acc[r, :] += dot3(halves(value), w_back)

    @pl.when(t == tiles - 1)
    def _():
        for r in row_chunks(rows):
            normed, factor = normalize_rows(acc[r, :])
            n2[r, :] = normed
            f2[r, :] = jnp.broadcast_to(factor, (factor.shape[0], 128))
            out[r, :] = normed * vec[LN2_GAIN : LN2_GAIN + 1] + vec[LN2_BIAS : LN2_BIAS + 1]


def ffn_fwd(place, ctx, xres, vec, bias_in, wo, wt=None):
    rows, width = xres.shape
    split = wt is None
    f32 = lambda *shape: jax.ShapeDtypeStruct(shape, F32)
    out_shape = [
        f32(rows, width),
        f32(rows, width),
        f32(rows, 128),
        f32(rows, width),
        f32(rows, 128),
        f32(2, rows, width),
        f32(4, rows, width),
    ]
    tile = lambda shape, clip=3: pl.BlockSpec(
        shape, lambda t: (jnp.minimum(t, clip),) + (0,) * (len(shape) - 1)
    )
    out_specs = [whole(s.shape) for s in out_shape[:5]] + [
        tile((1, rows, width), 1),
        tile((1, rows, width)),
    ]
    in_specs = [smem()] + [whole(a.shape) for a in (*ctx, xres, vec, bias_in)]
    scratch = [
        pltpu.VMEM((rows, width), BF16),
        pltpu.VMEM((rows, width), BF16),
        pltpu.VMEM((rows, width), F32),
    ]
    if split:
        w_out, w_in, w_back = wo
        weights = (*w_out, *w_in, *w_back)
        in_specs += [whole(w.shape) for w in w_out] + [pl.BlockSpec(memory_space=pl.ANY)] * 12
        inner = w_in[0].shape[1]
        out_shape += [
            jax.ShapeDtypeStruct((2, width, width), BF16),
            jax.ShapeDtypeStruct((4, 4, width, inner), BF16),
        ]
        out_specs += [whole((2, width, width)), tile((1, 4, width, inner))]
        scratch += [pltpu.VMEM((2, width, inner), F32), pltpu.SemaphoreType.DMA((4,))]
    else:
        weights = (wo, wt)
        in_specs += [whole(wo.shape), tile((1, *wt.shape[1:]))]
    return pl.pallas_call(
        functools.partial(ffn_fwd_kernel, split),
        grid=(4,),
        in_specs=in_specs,
        out_specs=out_specs,
        out_shape=out_shape,
        scratch_shapes=scratch,
        compiler_params=pltpu.CompilerParams(vmem_limit_bytes=VMEM_LIMIT),
        name="ffn_fwd",
    )(place, *ctx, xres, vec, bias_in, *weights)


def ffn_bwd_kernel(*refs):
    gout, n1, f1, n2, f2, slope, vec, wo_ref, wt_ref = refs[:9]
    gs, gi, gf, gcm, gct, sums = refs[9:15]
    s_hi, s_lo, acc = refs[15:]
    t = pl.program_id(0)
    rows = gout.shape[0]
    head_rows = wo_ref.shape[1] // 4
    chunks = row_chunks(rows)

    @pl.when(t == 0)
    def _():
        sums[...] = jnp.zeros_like(sums)
        for r in chunks:
            g = gout[r, :]
            sums[0:1, :] += colsum(g * n2[r, :])
            sums[1:2, :] += colsum(g)
            back = normalize_rows_back(g * vec[LN2_GAIN : LN2_GAIN + 1], n2[r, :], f2[r, 0:1])
            sums[2:3, :] += colsum(back)
            gs[r, :] = back
            acc[r, :] = back
            s_hi[r, :], s_lo[r, :] = halves(back)

    w_in = (wt_ref[0, 0], wt_ref[0, 1])
    w_back = (wt_ref[0, 2], wt_ref[0, 3])
    for r in chunks:
        grad_inner = dot3((s_hi[r, :], s_lo[r, :]), w_back, ROWS_BY_ROWS) * slope[0, r, :]

        @pl.when(t < 2)
        def _():
            gi[0, r, :] = grad_inner
            sums[pl.ds(6 + t, 1), :] += colsum(grad_inner)

        acc[r, :] += dot3(halves(grad_inner), w_in, ROWS_BY_ROWS)

    @pl.when(t == 3)
    def _():
        for r in chunks:
            g = acc[r, :]
            sums[3:4, :] += colsum(g * n1[r, :])
            sums[4:5, :] += colsum(g)
            back = normalize_rows_back(g * vec[LN1_GAIN : LN1_GAIN + 1], n1[r, :], f1[r, 0:1])
            sums[5:6, :] += colsum(back)
            gf[r, :] = back
            two = halves(back)
            for s, (dst, lanes) in enumerate(
                (
                    (gcm, slice(0, head_rows)),
                    (gct, slice(0, head_rows)),
                    (gcm, slice(head_rows, 2 * head_rows)),
                    (gct, slice(head_rows, 2 * head_rows)),
                )
            ):
                at = slice(s * head_rows, (s + 1) * head_rows)
                dst[r, lanes] = dot3(two, (wo_ref[0, at, :], wo_ref[1, at, :]), ROWS_BY_ROWS)


def ffn_bwd(gout, n1, f1, n2, f2, slope, vec, wo, wt):
    rows, width = gout.shape
    f32 = lambda *shape: jax.ShapeDtypeStruct(shape, F32)
    tile = lambda shape, clip=3: pl.BlockSpec(
        shape, lambda t: (jnp.minimum(t, clip),) + (0,) * (len(shape) - 1)
    )
    return pl.pallas_call(
        ffn_bwd_kernel,
        grid=(4,),
        in_specs=[whole(a.shape) for a in (gout, n1, f1, n2, f2)]
        + [tile((1, rows, width)), whole(vec.shape), whole(wo.shape), tile((1, *wt.shape[1:]))],
        out_specs=[
            whole((rows, width)),
            tile((1, rows, width), 1),
            whole((rows, width)),
            whole((rows, width // 2)),
            whole((rows, width // 2)),
            whole((8, width)),
        ],
        out_shape=[
            f32(rows, width),
            f32(2, rows, width),
            f32(rows, width),
            f32(rows, width // 2),
            f32(rows, width // 2),
            f32(8, width),
        ],
        scratch_shapes=[
            pltpu.VMEM((rows, width), BF16),
            pltpu.VMEM((rows, width), BF16),
            pltpu.VMEM((rows, width), F32),
        ],
        compiler_params=pltpu.CompilerParams(vmem_limit_bytes=VMEM_LIMIT),
        name="ffn_bwd",
    )(gout, n1, f1, n2, f2, slope, vec, wo, wt)


def join_kernel(segs, place, ms, mt, ts, tt, out):
    c = place[0]
    half, half_seg = TEXT // 2, segs // 2
    for seg, txt, side in ((ms, mt, c), (ts, tt, 1 - c)):
        out[pl.ds(pl.multiple_of(TEXT + side * half_seg, half_seg), half_seg), :] = seg[...]
        out[pl.ds(pl.multiple_of(side * half, half), half), :] = txt[...]


def join_rows(docs, segs, place, ms, mt, ts, tt):
    width = ms.shape[1]
    slots = TEXT + segs
    by_doc = lambda rows: pl.BlockSpec((rows, width), lambda d: (d, 0))
    return pl.pallas_call(
        functools.partial(join_kernel, segs),
        grid=(docs,),
        in_specs=[smem()] + [by_doc(segs // 2), by_doc(TEXT // 2)] * 2,
        out_specs=by_doc(slots),
        out_shape=jax.ShapeDtypeStruct((docs * slots, width), F32),
        name="join_rows",
    )(place, ms, mt, ts, tt)


def final_kernel(segs, n_parts, *refs):
    place = refs[0]
    mine, theirs = refs[1 : 1 + n_parts], refs[1 + n_parts : 1 + 2 * n_parts]
    ms, mt, ts, tt, roi, bn, out, sums = refs[1 + 2 * n_parts :]
    d = pl.program_id(0)
    join_kernel(segs, place, ms, mt, ts, tt, out)
    for i in range(n_parts):

        @pl.when(d == i)
        def _():
            out[...] += mine[i][...] + theirs[i][...]

    @pl.when(d == 0)
    def _():
        sums[...] = jnp.zeros_like(sums)

    g = out[TEXT:, :]
    sums[0:1, :] += colsum(g)
    sums[1:2, :] += colsum(g * batch_normed(roi[...], bn))


def final_rows(docs, segs, place, mine, theirs, ms, mt, ts, tt, roi, bn):
    width = ms.shape[1]
    slots = TEXT + segs
    by_doc = lambda rows: pl.BlockSpec((rows, width), lambda d: (d, 0))
    return pl.pallas_call(
        functools.partial(final_kernel, segs, len(mine)),
        grid=(docs,),
        in_specs=[smem()]
        + [whole((slots, width))] * (2 * len(mine))
        + [by_doc(segs // 2), by_doc(TEXT // 2)] * 2
        + [by_doc(segs), whole(bn.shape)],
        out_specs=[by_doc(slots), whole((8, width))],
        out_shape=[
            jax.ShapeDtypeStruct((docs * slots, width), F32),
            jax.ShapeDtypeStruct((8, width), F32),
        ],
        compiler_params=pltpu.CompilerParams(vmem_limit_bytes=VMEM_LIMIT),
        name="final_rows",
    )(place, *mine, *theirs, ms, mt, ts, tt, roi, bn)


def swap(x, axis, bit):
    n = lax.axis_size(axis)
    return lax.ppermute(x, axis, [(i, i ^ bit) for i in range(n)])


def butterfly(x, merge):
    bit = 1
    while bit < lax.axis_size("dp"):
        x = merge(x, swap(x, "dp", bit), bit)
        bit *= 2
    return x


def ring_sum(parts):
    n = lax.axis_size("dp")
    order = list(range(0, n, 2)) + list(range(n - 1, 0, -2))
    me = lax.axis_index("dp")
    place = jnp.where(me % 2 == 0, me // 2, n - 1 - me // 2)

    def chunk(i, k):
        sign = 1 if i % 2 == 0 else -1
        size = parts[i].shape[0] // n
        return ((sign * place - k) % n) * size, size

    def take(i, k):
        at, size = chunk(i, k)
        return lax.dynamic_slice_in_dim(parts[i], at, size, 0)

    def send(i, x):
        sign = 1 if i % 2 == 0 else -1
        return lax.ppermute(x, "dp", [(order[k], order[(k + sign) % n]) for k in range(n)])

    count = len(parts)
    held = [take(i, 0) for i in range(count)]
    for step in range(1, n):
        held = [send(i, held[i]) + take(i, step) for i in range(count)]
    total = []
    for i in range(count):
        total.append(lax.dynamic_update_slice_in_dim(parts[i], held[i], chunk(i, -1)[0], 0))
    for step in range(n - 1):
        held = [send(i, held[i]) for i in range(count)]
        for i in range(count):
            total[i] = lax.dynamic_update_slice_in_dim(total[i], held[i], chunk(i, step)[0], 0)
    return total


def per_device(
    hidden_in,
    roi,
    bn_gain,
    bn_bias,
    w_qkv,
    bias_qv,
    w_out,
    bias_out,
    ln1_gain,
    ln1_bias,
    w_in,
    bias_in,
    w_back,
    bias_back,
    ln2_gain,
    ln2_bias,
    pair_w,
    pair_bias,
    dir_w,
    text_len,
    owner_order,
    pair_index,
    cot_out,
    cot_logits,
):
    docs = text_len.shape[0]
    slots = hidden_in.shape[0] // docs
    width = hidden_in.shape[1]
    segs = slots - TEXT
    seg_rows = roi.shape[0]
    n_dp = lax.axis_size("dp")
    all_rows = seg_rows * n_dp
    half, half_seg = TEXT // 2, segs // 2
    m = lax.axis_index("mp")
    c = m % 2
    shift = lax.axis_index("dp") % 2
    place = jnp.stack([c, shift]).astype(jnp.int32)
    part = w_qkv.shape[2]

    def fetch(w):
        size = w.shape[0] // 2
        near = swap(lax.dynamic_slice_in_dim(w, shift * size, size, 0), "mp", 2)
        return near, swap(near, "dp", 1)

    qkv_own = jnp.transpose(w_qkv, (1, 0, 2)).reshape(width, 3 * part)
    qkv_other = fetch(qkv_own)
    small = jnp.zeros((8, width), F32)
    small = small.at[0].set(bias_in)
    small = small.at[1, :part].set(bias_qv[0]).at[2, :part].set(bias_qv[1])

    mean = jnp.mean(roi, axis=0)
    stats = jnp.stack([mean, jnp.sum((roi - mean) ** 2, axis=0)])

    def merge(one, two, count):
        gap = one[0] - two[0]
        return jnp.stack(
            [
                0.5 * (one[0] + two[0]),
                one[1] + two[1] + gap * gap * (0.5 * seg_rows * count),
            ]
        )

    stats = butterfly(stats, merge)
    roi_factor = lax.rsqrt(stats[1] / all_rows + EPSILON)
    bn = jnp.zeros((8, width), F32)
    bn = bn.at[0].set(stats[0]).at[1].set(roi_factor).at[2].set(bn_gain).at[3].set(bn_bias)

    small_x = swap(small, "mp", 2)
    out_own = w_out
    out_x = fetch(w_out)
    in_x = fetch(w_in)
    back_x = fetch(w_back)

    def four(own, far):
        return (own, swap(own, "mp", 1), *far, *(swap(f, "mp", 1) for f in far))

    def qkv_bias(rows):
        return jnp.concatenate([rows[1:2, :part], jnp.zeros((1, part), F32), rows[2:3, :part]], axis=1)

    qkv_a, lse_a, cm_seg_a, cm_txt_a, ct_seg_a, ct_txt_a, x_seg, x_txt = attn_fwd(
        place, text_len, hidden_in, roi, bn, qkv_bias(small), (qkv_own,), True
    )
    qkv_b, lse_b, cm_seg_b, cm_txt_b, ct_seg_b, ct_txt_b = attn_fwd(
        place, text_len, hidden_in, roi, bn, qkv_bias(small_x), qkv_other, False
    )
    from_sib = lambda x: swap(x, "mp", 1)
    ctx_seg = (cm_seg_a, from_sib(ct_seg_a), cm_seg_b, from_sib(ct_seg_b))
    ctx_txt = (cm_txt_a, from_sib(ct_txt_a), cm_txt_b, from_sib(ct_txt_b))
    vec = jnp.stack([bias_out, ln1_gain, ln1_bias, bias_back, ln2_gain, ln2_bias, ln2_bias, ln2_bias])
    bias_rows = jnp.concatenate(
        [small[0:1], from_sib(small)[0:1], small_x[0:1], from_sib(small_x)[0:1]], axis=0
    )
    out_seg, n1_seg, f1_seg, n2_seg, f2_seg, act_seg, slope_seg, wo, wt = ffn_fwd(
        place, ctx_seg, x_seg, vec, bias_rows,
        (four(out_own, out_x), four(w_in, in_x), four(w_back, back_x)),
    )
    out_txt, n1_txt, f1_txt, n2_txt, f2_txt, act_txt, slope_txt = ffn_fwd(
        place, ctx_txt, x_txt, vec, bias_rows, wo, wt
    )

    share = width // lax.axis_size("mp")
    cols = lambda x, who: lax.dynamic_slice_in_dim(x, who * share, share, 1)
    mine, theirs = cols(out_seg, m), from_sib(cols(out_seg, m ^ 1))
    by_core = lambda a, b: (jnp.where(c == 0, a, b), jnp.where(c == 0, b, a))
    columns = jnp.stack(
        [p.reshape(docs, half_seg, share) for p in by_core(mine, theirs)], axis=1
    ).reshape(seg_rows, share)
    ordering = owner_order[0]
    received = lax.all_to_all(
        jnp.take(columns, ordering, axis=0), "dp", split_axis=0, concat_axis=0, tiled=True
    )
    candidates = jnp.arange(seg_rows, dtype=jnp.int32)[None, :]
    pick_left = (pair_index[:, 0:1] == candidates).astype(F32)
    pick_right = (pair_index[:, 1:2] == candidates).astype(F32)
    sides = jnp.concatenate([product(pick_left, received), product(pick_right, received)], axis=1)
    pair_w2 = pair_w.reshape(2 * share, width)
    pair_part = product(sides, pair_w2)
    pair_part = pair_part + from_sib(pair_part)
    pairs_half = pair_part.shape[0] // 2
    piece = lax.dynamic_slice_in_dim(pair_part, c * pairs_half, pairs_half, 0)
    piece = piece + swap(piece, "mp", 2)
    pair_pre = jnp.concatenate(by_core(piece, from_sib(piece)), axis=0) + pair_bias
    root = 0.5 * (1.0 + lax.erf(pair_pre * ROOT_HALF))
    pair_act = pair_pre * root
    logits = product(pair_act, dir_w)
    grad_dir_w = product(cot_logits, pair_act, ((0,), (0,)))
    grad_pair_pre = product(cot_logits, dir_w, ((1,), (1,))) * (
        root + pair_pre * jnp.exp(-0.5 * pair_pre * pair_pre) * DENSITY
    )
    grad_pair_bias = jnp.sum(grad_pair_pre, axis=0)
    grad_pair_w = product(sides, grad_pair_pre, ((0,), (0,)))
    grad_sides = product(grad_pair_pre, pair_w2, ((1,), (1,)))
    grad_received = product(pick_left, grad_sides[:, :share], ((0,), (0,))) + product(
        pick_right, grad_sides[:, share:], ((0,), (0,))
    )
    grad_sent = lax.all_to_all(grad_received, "dp", split_axis=0, concat_axis=0, tiled=True)
    back_order = jnp.zeros_like(ordering).at[ordering].set(jnp.arange(seg_rows, dtype=jnp.int32))
    grad_cols = jnp.take(grad_sent, back_order, axis=0).reshape(docs, 2, half_seg, share)
    rows_of = lambda who: lax.dynamic_index_in_dim(grad_cols, who, 1, keepdims=False).reshape(
        docs * half_seg, share
    )
    grad_mine, grad_theirs = rows_of(c), from_sib(rows_of(1 - c))
    chip_cols = jnp.concatenate(by_core(grad_mine, grad_theirs), axis=1)
    far_cols = swap(chip_cols, "mp", 2)
    low_x = m < 2
    grad_seg = jnp.concatenate(
        [jnp.where(low_x, chip_cols, far_cols), jnp.where(low_x, far_cols, chip_cols)], axis=1
    )

    cot = cot_out.reshape(docs, slots, width)
    cot_seg = lax.dynamic_slice_in_dim(cot, TEXT + c * half_seg, half_seg, 1).reshape(
        docs * half_seg, width
    )
    cot_txt = lax.dynamic_slice_in_dim(cot, c * half, half, 1).reshape(docs * half, width)
    gs_txt, gi_txt, gf_txt, gcm_txt, gct_txt, sums_txt = ffn_bwd(
        cot_txt, n1_txt, f1_txt, n2_txt, f2_txt, slope_txt, vec, wo, wt
    )
    gs_seg, gi_seg, gf_seg, gcm_seg, gct_seg, sums_seg = ffn_bwd(
        cot_seg + grad_seg, n1_seg, f1_seg, n2_seg, f2_seg, slope_seg, vec, wo, wt
    )

    tall = ((0,), (0,))
    h_seg = n1_seg * ln1_gain + ln1_bias
    h_txt = n1_txt * ln1_gain + ln1_bias
    grad_back = [
        product(act_txt[k], gs_txt, tall) + product(act_seg[k], gs_seg, tall) for k in (0, 1)
    ]
    grad_in = [product(h_txt, gi_txt[k], tall) + product(h_seg, gi_seg[k], tall) for k in (0, 1)]
    grad_back_own = grad_back[0] + from_sib(grad_back[1])
    grad_in_own = grad_in[0] + from_sib(grad_in[1])
    sum_w_in, sum_w_back = ring_sum([grad_in_own, grad_back_own])

    grads = (gcm_seg, gcm_txt, from_sib(gct_seg), from_sib(gct_txt))
    ctx_a = (cm_seg_a, cm_txt_a, ct_seg_a, ct_txt_a)
    ctx_b = (cm_seg_b, cm_txt_b, ct_seg_b, ct_txt_b)
    w_sum = jnp.zeros((3 * part, width), F32)
    b_sum = jnp.zeros((1, 3 * part), F32)
    gx = []
    for doc in range(docs):
        gx_doc, w_sum, b_sum = attn_bwd(
            doc, place, text_len, hidden_in, roi, bn, (qkv_own,), qkv_other,
            (qkv_a, qkv_b), (lse_a, lse_b), (ctx_a, ctx_b), grads, w_sum, b_sum,
        )
        gx.append(gx_doc)
    gx_sib = [from_sib(g) for g in gx]
    grad_hidden, bn_sums = final_rows(
        docs, segs, place, gx, gx_sib, gf_seg, gf_txt, from_sib(gf_seg), from_sib(gf_txt), roi, bn
    )

    def out_grad(first):
        return jnp.concatenate(
            [
                product(ctx_txt[first], gf_txt, tall) + product(ctx_seg[first], gf_seg, tall)
            ],
            axis=0,
        )

    grad_out_own = out_grad(0) + from_sib(out_grad(1))
    sum_qkv, sum_rest = ring_sum([w_sum, jnp.concatenate([grad_pair_w, grad_out_own], axis=0)])

    rows = sums_txt + sums_seg
    rows = jnp.concatenate([rows[:6], rows[6:7]]) + from_sib(jnp.concatenate([rows[:6], rows[7:8]]))
    pad = lambda v: jnp.pad(v, (0, width - v.shape[0]))[None]
    vectors = jnp.concatenate(
        [
            rows,
            grad_pair_bias[None],
            grad_dir_w,
            pad(b_sum[0, :part]),
            pad(b_sum[0, 2 * part :]),
            bn_sums[0:2],
        ],
        axis=0,
    )
    vectors = butterfly(vectors, lambda one, two, _: one + two)
    n_dirs = dir_w.shape[1]
    sum_dir_w = vectors[8 : 8 + n_dirs].T
    tail = vectors[8 + n_dirs :]
    sum_bias_qv = tail[0:2, :part]
    grad_bn_bias, grad_bn_gain = tail[2], tail[3]
    grad_roi_out = grad_hidden.reshape(docs, slots, width)[:, TEXT:].reshape(seg_rows, width)
    roi_normed = (roi - bn[0]) * roi_factor
    grad_roi = (
        bn_gain
        * roi_factor
        * (grad_roi_out - grad_bn_bias / all_rows - roi_normed * grad_bn_gain / all_rows)
    )
    output = join_rows(
        docs, segs, place, out_seg, out_txt, from_sib(out_seg), from_sib(out_txt)
    )
    return (
        output,
        logits,
        grad_hidden,
        grad_roi,
        grad_bn_gain,
        grad_bn_bias,
        jnp.transpose(sum_qkv.reshape(3, part, width), (0, 2, 1)),
        sum_bias_qv,
        sum_rest[2 * share :],
        vectors[5],
        vectors[3],
        vectors[4],
        sum_w_in,
        vectors[6],
        sum_w_back,
        vectors[2],
        vectors[0],
        vectors[1],
        sum_rest[: 2 * share].reshape(2, share, width),
        vectors[7],
        sum_dir_w,
    )


def solution(mesh):
    placed = (
        P("dp", None),
        P("dp", None),
        P(),
        P(),
        P(None, None, "mp"),
        P(None, "mp"),
        P("mp", None),
        P(),
        P(),
        P(),
        P(None, "mp"),
        P("mp"),
        P("mp", None),
        P(),
        P(),
        P(),
        P(None, "mp", None),
        P(),
        P(),
        P("dp"),
        P("dp", None),
        P("dp", None),
        P("dp", None),
        P("dp", None),
    )
    return jax.shard_map(
        per_device,
        mesh=mesh,
        in_specs=placed,
        out_specs=(
            P("dp", None),
            P("dp", None),
            P("dp", None),
            P("dp", None),
            P(),
            P(),
            P(None, None, "mp"),
            P(None, "mp"),
            P("mp", None),
            P(),
            P(),
            P(),
            P(None, "mp"),
            P("mp"),
            P("mp", None),
            P(),
            P(),
            P(),
            P(None, "mp", None),
            P(),
            P(),
        ),
        check_vma=False,
    )
```

```python
import functools

import jax
import jax.numpy as jnp
from jax import lax
from jax.experimental import pallas as pl
from jax.experimental.pallas import tpu as pltpu
from jax.sharding import PartitionSpec as P

HEAD_DIM = 64
TEXT = 512
EPSILON = 1e-05
NEGATIVE = -1e30
ROOT_HALF = 0.7071067811865476
DENSITY = 0.3989422804014327
HIGH = lax.Precision.HIGH
QUERY_STEP = 256
VMEM_LIMIT = 60 << 20
F32 = jnp.float32
BF16 = jnp.bfloat16


def product(operand, other, dims=((1,), (0,))):
    return lax.dot_general(
        operand, other, (dims, ((), ())), precision=HIGH, preferred_element_type=F32
    )


def halves(x):
    hi = x.astype(BF16)
    return hi, (x - hi.astype(F32)).astype(BF16)


def dot(a, b, dims=((1,), (0,))):
    return lax.dot_general(a, b, (dims, ((), ())), preferred_element_type=F32)


ROWS_BY_ROWS = ((1,), (1,))
COLS_BY_COLS = ((0,), (0,))


def dot3_apart(a, b, dims=((1,), (0,))):
    return dot(a[0], b[0], dims) + dot(a[1], b[0], dims) + dot(a[0], b[1], dims)


def dot3(a, b, dims=((1,), (0,))):
    ka, kb = dims[0][0], dims[1][0]
    return dot(jnp.concatenate([a[0], a[1], a[0]], ka), jnp.concatenate([b[0], b[0], b[1]], kb), dims)


def gelu_parts(v):
    phi = 0.5 + 0.5 * lax.erf(v * ROOT_HALF)
    return v * phi, phi + v * jnp.exp(-0.5 * v * v) * DENSITY


def normalize_rows(y):
    center = y - jnp.mean(y, axis=-1, keepdims=True)
    factor = lax.rsqrt(jnp.mean(center * center, axis=-1, keepdims=True) + EPSILON)
    return center * factor, factor


def normalize_rows_back(upstream, normed, factor):
    return factor * (
        upstream
        - jnp.mean(upstream, axis=-1, keepdims=True)
        - normed * jnp.mean(upstream * normed, axis=-1, keepdims=True)
    )


def colsum(x):
    return jnp.sum(x, axis=0, keepdims=True)


def lane_is(rows, width, lane):
    return lax.broadcasted_iota(jnp.int32, (rows, width), 1) == lane


def cost(products, moved):
    return pl.CostEstimate(flops=6 * products, bytes_accessed=moved, transcendentals=0)


def smem():
    return pl.BlockSpec(memory_space=pltpu.SMEM)


def whole(shape):
    return pl.BlockSpec(shape, lambda *_: (0,) * len(shape), pipeline_mode=pl.Buffered(1))


def sds(*shape):
    return jax.ShapeDtypeStruct(shape, F32)


def batch_normed(roi, stats, rows):
    return (roi - stats[0:1]) * lax.rsqrt(stats[1:2] / rows + EPSILON)


def segment_rows(roi, stats, rows, gain, shift):
    return batch_normed(roi[...], stats, rows) * gain[...][None, :] + shift[...][None, :]


def side_rows(ref, side, half, half_seg):
    return (
        ref.at[pl.ds(pl.multiple_of(TEXT + side * half_seg, half_seg), half_seg)],
        ref.at[pl.ds(pl.multiple_of(side * half, half), half)],
    )


def split_qkv(w, w_hi, w_lo):
    part = w.shape[2]
    for i in range(3):
        lanes = slice(i * part, (i + 1) * part)
        w_hi[:, lanes], w_lo[:, lanes] = halves(w[i])


def attn_fwd_kernel(all_rows, *refs):
    place, lens, hid, roi, stats, gain, shift, w, bias = refs[:9]
    qkv, lse, both_seg, both_txt, xm_seg, xm_txt = refs[9:15]
    w_hi, w_lo, x_seg, ctx, ctx_t = refs[15:]
    doc = pl.program_id(0)
    c = place[0]
    width = w.shape[2]
    heads = width // HEAD_DIM
    slots = hid.shape[0]
    half, half_seg = TEXT // 2, (slots - TEXT) // 2

    @pl.when(doc == 0)
    def _():
        split_qkv(w, w_hi, w_lo)

    x_seg[...] = hid[TEXT:, :] + segment_rows(roi, stats, all_rows, gain, shift)
    wide = (w_hi[...], w_lo[...])
    added = jnp.concatenate([bias[0:1, :], jnp.zeros((1, width), F32), bias[1:2, :]], axis=1)
    for start in (0, half):
        qkv[start : start + half, :] = dot3(halves(hid[start : start + half, :]), wide) + added
    qkv[TEXT:, :] = dot3(halves(x_seg[...]), wide) + added

    position = lax.broadcasted_iota(jnp.int32, (slots, HEAD_DIM), 0)
    first = lane_is(slots, HEAD_DIM, 0)
    dead = (position >= lens[doc]) & (position < TEXT)
    key_extra = jnp.where(first & dead, NEGATIVE, 0.0).astype(BF16)
    ones = jnp.where(first, 1.0, 0.0).astype(BF16)
    one_rows = jnp.ones((16, slots), BF16)
    values = jnp.transpose(qkv[:, 2 * width :])
    for h in range(heads):
        at = h * HEAD_DIM
        q_hi, q_lo = halves(qkv[:, at : at + HEAD_DIM] * HEAD_DIM**-0.5)
        k_hi, k_lo = halves(qkv[:, width + at : width + at + HEAD_DIM])
        v_two = jnp.concatenate([*halves(values[at : at + HEAD_DIM, :]), one_rows], axis=0)
        q_pack = jnp.concatenate([q_hi, q_lo, q_hi, ones], axis=1)
        k_pack = jnp.concatenate([k_hi, k_hi, k_lo, key_extra], axis=1)
        for start in range(0, slots, QUERY_STEP):
            cols = slice(start, min(slots, start + QUERY_STEP))
            scores = dot(k_pack, q_pack[cols], ROWS_BY_ROWS)
            top = jnp.max(scores, axis=0, keepdims=True)
            p_hi, p_lo = halves(jnp.exp(scores - top))
            mixed = dot(v_two, p_hi) + dot(v_two, p_lo)
            total = mixed[2 * HEAD_DIM : 2 * HEAD_DIM + 1]
            ctx_t[at : at + HEAD_DIM, cols] = (
                mixed[:HEAD_DIM] + mixed[HEAD_DIM : 2 * HEAD_DIM]
            ) / total
            lse[h : h + 1, cols] = top + jnp.log(total)
    ctx[...] = jnp.transpose(ctx_t[...])
    for lanes, side in ((slice(0, width), c), (slice(width, 2 * width), 1 - c)):
        at_seg, at_txt = side_rows(ctx, side, half, half_seg)
        both_seg[:, lanes] = at_seg[...]
        both_txt[:, lanes] = at_txt[...]
    xm_seg[...] = x_seg[pl.ds(pl.multiple_of(c * half_seg, half_seg), half_seg), :]
    xm_txt[...] = hid[pl.ds(pl.multiple_of(c * half, half), half), :]


def by_doc(rows, lanes):
    return pl.BlockSpec((rows, lanes), lambda d: (d, 0))


def attn_fwd(all_rows, place, lens, hidden, roi, stats, gain, shift, w, bias):
    docs = lens.shape[0]
    slots, width = hidden.shape[0] // docs, hidden.shape[1]
    segs = slots - TEXT
    part = w.shape[2]
    out_rows = [
        (slots, 3 * part),
        (8, slots),
        (segs // 2, 2 * part),
        (TEXT // 2, 2 * part),
        (segs // 2, width),
        (TEXT // 2, width),
    ]
    return pl.pallas_call(
        functools.partial(attn_fwd_kernel, all_rows),
        grid=(docs,),
        in_specs=[smem(), smem(), by_doc(slots, width), by_doc(segs, width)]
        + [whole(a.shape) for a in (stats, gain, shift, w, bias)],
        out_specs=[by_doc(*s) for s in out_rows],
        out_shape=[sds(docs * s[0], s[1]) for s in out_rows],
        scratch_shapes=[
            pltpu.VMEM((width, 3 * part), BF16),
            pltpu.VMEM((width, 3 * part), BF16),
            pltpu.VMEM((segs, width), F32),
            pltpu.VMEM((slots, part), F32),
            pltpu.VMEM((part, slots), F32),
        ],
        compiler_params=pltpu.CompilerParams(vmem_limit_bytes=VMEM_LIMIT),
        cost_estimate=cost(docs * slots, slots),
        name="attn_fwd",
    )(place, lens, hidden, roi, stats, gain, shift, w, bias)


def attn_bwd_kernel(doc, *refs):
    place, lens, qkv, lse, ctx_seg, ctx_txt, gm_seg, gm_txt, gt_seg, gt_txt, b_sum = refs[:11]
    gq, b_out, o_all, g_all, gq_t = refs[11:]
    c = place[0]
    width = qkv.shape[1] // 3
    heads = width // HEAD_DIM
    slots = qkv.shape[0]
    half, half_seg = TEXT // 2, (slots - TEXT) // 2
    near, far = slice(0, width), slice(width, 2 * width)
    for dst, mine, theirs in (
        (o_all, (ctx_seg, ctx_txt), (ctx_seg, ctx_txt)),
        (g_all, (gm_seg, gm_txt), (gt_seg, gt_txt)),
    ):
        for side, sources, lanes in ((c, mine, near), (1 - c, theirs, far)):
            for place_at, source in zip(side_rows(dst, side, half, half_seg), sources):
                place_at[...] = source[:, lanes]

    position = lax.broadcasted_iota(jnp.int32, (slots, HEAD_DIM), 0)
    first = lane_is(slots, HEAD_DIM, 0)
    dead = (position >= lens[doc]) & (position < TEXT)
    key_extra = jnp.where(first & dead, NEGATIVE, 0.0).astype(BF16)
    ones = jnp.where(first, 1.0, 0.0).astype(BF16)
    none = jnp.zeros_like(ones)
    head_of = lax.broadcasted_iota(jnp.int32, (16, width), 1) // HEAD_DIM
    pick_head = jnp.where(
        head_of == lax.broadcasted_iota(jnp.int32, (16, width), 0), 1.0, 0.0
    ).astype(BF16)
    scale = HEAD_DIM**-0.5
    product_hi, product_lo = halves(g_all[...] * o_all[...])
    inner = dot(pick_head, product_hi, ROWS_BY_ROWS) + dot(pick_head, product_lo, ROWS_BY_ROWS)
    keys_t = jnp.transpose(qkv[:, width : 2 * width])
    for h in range(heads):
        at = h * HEAD_DIM
        q_hi, q_lo = halves(qkv[:, at : at + HEAD_DIM] * scale)
        k_hi, k_lo = halves(qkv[:, width + at : width + at + HEAD_DIM])
        v_hi, v_lo = halves(qkv[:, 2 * width + at : 2 * width + at + HEAD_DIM])
        g_hi, g_lo = halves(g_all[:, at : at + HEAD_DIM])
        k_rows = jnp.concatenate(halves(keys_t[at : at + HEAD_DIM, :]), axis=0)
        q_pack = jnp.concatenate([q_hi, q_lo, q_hi, ones], axis=1)
        k_pack = jnp.concatenate([k_hi, k_hi, k_lo, key_extra], axis=1)
        g_pack = jnp.concatenate([g_hi, g_lo, g_hi, none], axis=1)
        v_pack = jnp.concatenate([v_hi, v_hi, v_lo, none], axis=1)
        q_two = jnp.concatenate([q_hi, q_lo], axis=1)
        g_two = jnp.concatenate([g_hi, g_lo], axis=1)
        weights = jnp.exp(dot(k_pack, q_pack, ROWS_BY_ROWS) - lse[h : h + 1, :])
        grads = weights * (dot(v_pack, g_pack, ROWS_BY_ROWS) - inner[h : h + 1, :])
        w_two = halves(weights)
        s_two = halves(grads)
        grad_v = dot(w_two[0], g_two) + dot(w_two[1], g_two)
        grad_k = dot(s_two[0], q_two) + dot(s_two[1], q_two)
        grad_q = dot(k_rows, s_two[0]) + dot(k_rows, s_two[1])
        gq[:, width + at : width + at + HEAD_DIM] = grad_k[:, :HEAD_DIM] + grad_k[:, HEAD_DIM:]
        gq[:, 2 * width + at : 2 * width + at + HEAD_DIM] = (
            grad_v[:, :HEAD_DIM] + grad_v[:, HEAD_DIM:]
        )
        gq_t[at : at + HEAD_DIM, :] = (grad_q[:HEAD_DIM] + grad_q[HEAD_DIM:]) * scale
    gq[:, :width] = jnp.transpose(gq_t[...])
    b_out[...] = b_sum[...] + colsum(gq[...])


def attn_bwd(doc, place, lens, qkv, lse, ctx, mine, theirs, b_sum):
    docs = lens.shape[0]
    slots, cols = qkv.shape[0] // docs, qkv.shape[1]
    segs = slots - TEXT
    part = cols // 3
    of_doc = lambda rows, lanes: pl.BlockSpec((rows, lanes), lambda i: (doc, 0))
    rows = [of_doc(segs // 2, 2 * part), of_doc(TEXT // 2, 2 * part)]
    return pl.pallas_call(
        functools.partial(attn_bwd_kernel, doc),
        grid=(1,),
        in_specs=[smem(), smem(), of_doc(slots, cols), of_doc(8, slots)] + rows * 3 + [whole((1, cols))],
        out_specs=[whole((slots, cols)), whole((1, cols))],
        out_shape=[sds(slots, cols), sds(1, cols)],
        scratch_shapes=[
            pltpu.VMEM((slots, part), F32),
            pltpu.VMEM((slots, part), F32),
            pltpu.VMEM((part, slots), F32),
        ],
        compiler_params=pltpu.CompilerParams(vmem_limit_bytes=VMEM_LIMIT),
        cost_estimate=cost(slots * part * 16 * slots, 8 * slots * cols),
        name="attn_bwd",
    )(place, lens, qkv, lse, *ctx, *mine, *theirs, b_sum)


def qkv_bwd_kernel(all_rows, *refs):
    place, hid, roi, stats, gain, shift, w, gq, w_sum = refs[:9]
    gx_mine, gx_theirs, w_out = refs[9:12]
    w_hi, w_lo, x_all, gx = refs[12:]
    c = place[0]
    slots = hid.shape[0]
    half, half_seg = TEXT // 2, (slots - TEXT) // 2
    split_qkv(w, w_hi, w_lo)
    x_all[:TEXT, :] = hid[:TEXT, :]
    x_all[TEXT:, :] = hid[TEXT:, :] + segment_rows(roi, stats, all_rows, gain, shift)
    wide = (w_hi[...], w_lo[...])
    for start in range(0, slots, 320):
        rows = slice(start, min(slots, start + 320))
        gx[rows, :] = dot3_apart(halves(gq[rows, :]), wide, ROWS_BY_ROWS)
    w_out[...] = w_sum[...] + dot3_apart(halves(gq[...]), halves(x_all[...]), COLS_BY_COLS)
    for dst, side in ((gx_mine, c), (gx_theirs, 1 - c)):
        at_seg, at_txt = side_rows(gx, side, half, half_seg)
        dst[:half_seg, :] = at_seg[...]
        dst[half_seg:, :] = at_txt[...]


def qkv_bwd(all_rows, doc, docs, place, hidden, roi, stats, gain, shift, w, gq, w_sum):
    slots, width = hidden.shape[0] // docs, hidden.shape[1]
    cols = gq.shape[1]
    of_doc = lambda rows, lanes: pl.BlockSpec((rows, lanes), lambda i: (doc, 0))
    return pl.pallas_call(
        functools.partial(qkv_bwd_kernel, all_rows),
        grid=(1,),
        in_specs=[smem(), of_doc(slots, width), of_doc(slots - TEXT, width)]
        + [whole(a.shape) for a in (stats, gain, shift, w, gq, w_sum)],
        out_specs=[whole((slots // 2, width)), whole((slots // 2, width)), whole((cols, width))],
        out_shape=[sds(slots // 2, width), sds(slots // 2, width), sds(cols, width)],
        scratch_shapes=[
            pltpu.VMEM((width, cols), BF16),
            pltpu.VMEM((width, cols), BF16),
            pltpu.VMEM((slots, width), F32),
            pltpu.VMEM((slots, width), F32),
        ],
        compiler_params=pltpu.CompilerParams(vmem_limit_bytes=VMEM_LIMIT),
        cost_estimate=cost(slots * cols * 2 * width, 12 * slots * width),
        name="qkv_bwd",
    )(place, hidden, roi, stats, gain, shift, w, gq, w_sum)


VECTORS = ("bias_out", "ln1_gain", "ln1_bias", "bias_back", "ln2_gain", "ln2_bias")
TILES = 4
PIECE_SHARDS = (0, 1, 2, 2, 3, 3)


def piece_place(i, rows, shift):
    if i < 2:
        return 0
    half = rows // 2
    return pl.multiple_of((shift if i % 2 == 0 else 1 - shift) * half, half)


def ffn_kernel(forward, backward, names, *refs):
    ref = dict(zip(names, refs))
    place, stage, sems = ref["place"], ref["stage"], ref["sems"]
    wts, acc, a_hi, a_lo = ref["wts"], ref["acc"], ref["a_hi"], ref["a_lo"]
    wo = ref["wo"]
    resident = wts.shape[0] == TILES
    c = place[0]
    shifts = {"wo": place[1], "wi": place[1], "wb": place[2]}
    width = acc.shape[1]
    rows = acc.shape[0]
    part = wo.shape[1] // 4
    row = lambda name: ref[name][...][None, :]

    def two_shards(one, two):
        lane = lax.broadcasted_iota(jnp.int32, (rows, 2 * part), 1)
        return jnp.where(lane < part, ref[one][...], ref[two][...])

    def copies(tile):
        found = []
        for i in range(6):
            if PIECE_SHARDS[i] == tile:
                for k, kind in enumerate(("wi", "wb")):
                    piece = ref[f"{kind}{i}"]
                    if kind == "wi" and i > 1:
                        piece = piece.at[pl.ds(part // 2, width // 2)]
                    at = pl.ds(piece_place(i, width, shifts[kind]), piece.shape[0])
                    found.append(
                        pltpu.make_async_copy(piece, stage.at[k, at, :], sems.at[len(found)])
                    )
        return found

    def start_tile(tile):
        for copy in copies(tile):
            copy.start()

    def ready(tile):
        for copy in copies(tile):
            copy.wait()
        slot = tile if resident else 0
        wts[slot, 0], wts[slot, 1] = halves(stage[0])
        wts[slot, 2], wts[slot, 3] = halves(stage[1])
        if tile + 1 < TILES:
            start_tile(tile + 1)

    def load_wo(count):
        for i in range(count):
            at = PIECE_SHARDS[i] * part + piece_place(i, part, shifts["wo"])
            where = pl.ds(at, ref[f"wo{i}"].shape[0])
            wo[0, where, :], wo[1, where, :] = halves(ref[f"wo{i}"][...])

    def run_forward(loading):
        y = ref["xres"][...] + row("bias_out")
        for one, two, at in (
            ("ctx_own", "ctx_sib", slice(0, 2 * part)),
            ("ctx_far", "ctx_farsib", slice(2 * part, 4 * part)),
        ):
            y = y + dot3(halves(two_shards(one, two)), (wo[0, at, :], wo[1, at, :]))
        normed, factor = normalize_rows(y)
        ref["n1"][...] = normed
        ref["f1"][...] = jnp.broadcast_to(factor, (rows, 128))
        h = normed * row("ln1_gain") + row("ln1_bias")
        ref["h1"][...] = h
        a_hi[...], a_lo[...] = halves(h)
        acc[...] = h + row("bias_back")
        for t in range(TILES):
            if loading:
                ready(t)
            slot = t if resident else 0
            pre = dot3((a_hi[...], a_lo[...]), (wts[slot, 0], wts[slot, 1]))
            value, rise = gelu_parts(pre + row(f"bias_in{t}"))
            ref["slope"][t] = rise
            if t < 2:
                ref[f"act{t}"][...] = value
            acc[...] += dot3(halves(value), (wts[slot, 2], wts[slot, 3]))
        normed, factor = normalize_rows(acc[...])
        ref["n2"][...] = normed
        ref["f2"][...] = jnp.broadcast_to(factor, (rows, 128))
        ref["out"][...] = normed * row("ln2_gain") + row("ln2_bias")

    def run_backward(loading):
        sums = ref["sums"]
        if forward:
            g = ref["gout"][pl.ds(pl.multiple_of(c * rows, rows), rows), :]
        else:
            g = ref["gout"][...]
        n2 = ref["n2"][...]
        sums[0:1, :] += colsum(g * n2)
        sums[1:2, :] += colsum(g)
        back = normalize_rows_back(g * row("ln2_gain"), n2, ref["f2"][:, 0:1])
        sums[2:3, :] += colsum(back)
        ref["gs"][...] = back
        acc[...] = back
        a_hi[...], a_lo[...] = halves(back)
        for t in range(TILES):
            if loading:
                ready(t)
            slot = t if resident else 0
            grad = dot3((a_hi[...], a_lo[...]), (wts[slot, 2], wts[slot, 3]), ROWS_BY_ROWS)
            grad = grad * ref["slope"][t]
            if t < 2:
                ref[f"gi{t}"][...] = grad
                sums[6 + t : 7 + t, :] += colsum(grad)
            acc[...] += dot3(halves(grad), (wts[slot, 0], wts[slot, 1]), ROWS_BY_ROWS)
        g, n1 = acc[...], ref["n1"][...]
        sums[3:4, :] += colsum(g * n1)
        sums[4:5, :] += colsum(g)
        back = normalize_rows_back(g * row("ln1_gain"), n1, ref["f1"][:, 0:1])
        sums[5:6, :] += colsum(back)
        ref["gf"][...] = back
        two = halves(back)
        at = slice(0, 2 * part)
        ref["gb"][...] = dot3(two, (wo[0, at, :], wo[1, at, :]), ROWS_BY_ROWS)
        ref["gwo"][...] = dot3_apart(halves(two_shards("ctx_own", "ctx_sib")), two, COLS_BY_COLS)

    def begin():
        start_tile(0)
        load_wo(6 if forward else 2)
        if backward:
            ref["sums"][...] = jnp.zeros_like(ref["sums"])

    if forward and backward:

        @pl.when(pl.program_id(0) == 0)
        def _():
            begin()
            run_forward(True)
            run_backward(False)

        @pl.when(pl.program_id(0) > 0)
        def _():
            run_forward(False)
            run_backward(False)
    else:
        begin()
        if forward:
            run_forward(True)
        if backward:
            run_backward(True)


def ffn(place, vectors, bias_in, weights, block, offset, total, saved, *, ctx=None, xres=None, gout=None, into=None, start=0, count=None):
    forward, backward = xres is not None, gout is not None
    both = forward and backward
    width = vectors[0].shape[0]
    rows = ctx[0].shape[0]
    blocks = rows // block
    part = width // 4
    w_out, w_in, w_back = weights
    first = offset // block + start
    local = lambda lanes: pl.BlockSpec((block, lanes), lambda r: (start + r, 0))
    shared = pl.BlockSpec((block, width), lambda r: (first + r, 0))
    anywhere = pl.BlockSpec(memory_space=pltpu.HBM)
    names, specs, args = [], [], []

    def take(name, spec, arg):
        names.append(name)
        specs.append(spec)
        args.append(arg)

    take("place", smem(), place)
    for name, a in zip(VECTORS, vectors):
        take(name, whole(a.shape), a)
    for name, a in zip(("ctx_own", "ctx_sib", "ctx_far", "ctx_farsib"), ctx):
        take(name, local(a.shape[1]), a)
    if forward:
        for t in range(TILES):
            take(f"bias_in{t}", whole(bias_in[t].shape), bias_in[t])
        take("xres", local(width), xres)
    if backward:
        if both:
            slots = gout.shape[0] // blocks
            take("gout", pl.BlockSpec((slots, width), lambda r: (start + r, 0)), gout)
        else:
            take("gout", local(width), gout)
    kept = (
        ("n1", (block, width)),
        ("f1", (block, 128)),
        ("n2", (block, width)),
        ("f2", (block, 128)),
        ("slope", (TILES, block, width)),
    )
    if backward and not forward:
        for (name, shape), a in zip(kept, saved):
            take(name, whole(shape), a)
    for i in range(6 if forward else 2):
        piece, height = (w_out[i], part) if i < 2 else (w_in[i], part // 2)
        take(f"wo{i}", whole((height, width)), piece)
    for i in range(6):
        take(f"wi{i}", anywhere, w_in[i])
        take(f"wb{i}", anywhere, w_back[i])
    outs = []
    if forward:
        outs += [("out", local(width), sds(rows, width))]
        outs += [(n, shared, sds(total, width)) for n in ("h1", "act0", "act1")]
        if not backward:
            outs += [(name, whole(shape), sds(*shape)) for name, shape in kept]
    if backward:
        outs += [(n, shared, sds(total, width)) for n in ("gs", "gi0", "gi1", "gf")]
        outs += [("gb", local(2 * part), sds(rows, 2 * part))]
        outs += [("gwo", whole((2 * part, width)), sds(2 * part, width))]
        outs += [("sums", whole((8, width)), sds(8, width))]
    aliases = {}
    if into:
        for k, (name, _, _) in enumerate(outs):
            if name in into:
                aliases[len(args)] = k
                take(name + "_into", anywhere, into[name])
    scratch = [
        ("stage", pltpu.VMEM((2, width, width), F32)),
        ("sems", pltpu.SemaphoreType.DMA((4,))),
        ("wts", pltpu.VMEM((TILES if both else 1, 4, width, width), BF16)),
        ("wo", pltpu.VMEM((2, width, width), BF16)),
        ("acc", pltpu.VMEM((block, width), F32)),
        ("a_hi", pltpu.VMEM((block, width), BF16)),
        ("a_lo", pltpu.VMEM((block, width), BF16)),
    ]
    if both:
        scratch += [(name, pltpu.VMEM(shape, F32)) for name, shape in kept]
    all_names = names + [o[0] for o in outs] + [s[0] for s in scratch]
    passes = (3 if both else 1) * 8
    result = pl.pallas_call(
        functools.partial(ffn_kernel, forward, backward, all_names),
        grid=(count or blocks,),
        in_specs=specs,
        out_specs=[o[1] for o in outs],
        out_shape=[o[2] for o in outs],
        scratch_shapes=[s[1] for s in scratch],
        input_output_aliases=aliases,
        compiler_params=pltpu.CompilerParams(vmem_limit_bytes=VMEM_LIMIT),
        cost_estimate=cost(
            (count or blocks) * block * width * width * (16 if both else 8) + 4 * width**3,
            60 * block * width,
        ),
        name="ffn_" + "fwd" * forward + "bwd" * backward,
    )(*args)
    return {o[0]: r for o, r in zip(outs, result)}


def join_kernel(docs, segs, place, ms, mt, ts, tt, out):
    c = place[0]
    half, half_seg = TEXT // 2, segs // 2
    for seg, txt, side in ((ms, mt, c), (ts, tt, 1 - c)):
        at_seg, at_txt = side_rows(out, side, half, half_seg)
        at_seg[...] = seg[...]
        at_txt[...] = txt[...]


def join_rows(docs, segs, place, ms, mt, ts, tt):
    width = ms.shape[1]
    slots = TEXT + segs
    return pl.pallas_call(
        functools.partial(join_kernel, docs, segs),
        grid=(docs,),
        in_specs=[smem()] + [by_doc(segs // 2, width), by_doc(TEXT // 2, width)] * 2,
        out_specs=by_doc(slots, width),
        out_shape=sds(docs * slots, width),
        cost_estimate=cost(0, 8 * docs * slots * width),
        compiler_params=pltpu.CompilerParams(vmem_limit_bytes=VMEM_LIMIT),
        name="join_rows",
    )(place, ms, mt, ts, tt)


def final_kernel(docs, segs, all_rows, *refs):
    place = refs[0]
    mine, theirs = refs[1 : 1 + docs], refs[1 + docs : 1 + 2 * docs]
    roi, stats, out, sums = refs[1 + 2 * docs :]
    d = pl.program_id(0)
    c = place[0]
    half, half_seg = TEXT // 2, segs // 2

    @pl.when(d == 0)
    def _():
        sums[...] = jnp.zeros_like(sums)

    for i in range(docs):

        @pl.when(d == i)
        def _():
            for source, side in ((mine[i], c), (theirs[i], 1 - c)):
                at_seg, at_txt = side_rows(out, side, half, half_seg)
                at_seg[...] = source[:half_seg, :]
                at_txt[...] = source[half_seg:, :]

    g = out[TEXT:, :]
    sums[0:1, :] += colsum(g)
    sums[1:2, :] += colsum(g * batch_normed(roi[...], stats, all_rows))


def final_rows(all_rows, segs, place, mine, theirs, roi, stats):
    docs = len(mine)
    width = roi.shape[1]
    slots = TEXT + segs
    return pl.pallas_call(
        functools.partial(final_kernel, docs, segs, all_rows),
        grid=(docs,),
        in_specs=[smem()]
        + [whole((slots // 2, width))] * (2 * docs)
        + [by_doc(segs, width), whole(stats.shape)],
        out_specs=[by_doc(slots, width), pl.BlockSpec((8, width), lambda d: (0, 0))],
        out_shape=[sds(docs * slots, width), sds(8, width)],
        compiler_params=pltpu.CompilerParams(vmem_limit_bytes=VMEM_LIMIT),
        cost_estimate=cost(0, 20 * docs * slots * width),
        name="final_rows",
    )(place, *mine, *theirs, roi, stats)


def stats_kernel(roi, stats):
    x = roi[...]
    mean = jnp.mean(x, axis=0, keepdims=True)
    stats[0:1, :] = mean
    stats[1:2, :] = colsum((x - mean) * (x - mean))


def local_stats(roi):
    width = roi.shape[1]
    return pl.pallas_call(
        stats_kernel, out_shape=sds(2, width), name="local_stats"
    )(roi)


def swap(x, axis, bit):
    n = lax.axis_size(axis)
    return lax.ppermute(x, axis, [(i, i ^ bit) for i in range(n)])


def butterfly(x, merge):
    bit = 1
    while bit < lax.axis_size("dp"):
        x = merge(x, swap(x, "dp", bit), bit)
        bit *= 2
    return x


def ring(part, sign):
    n = lax.axis_size("dp")
    order = list(range(0, n, 2)) + list(range(n - 1, 0, -2))
    pairs = [(order[k], order[(k + sign) % n]) for k in range(n)]
    me = lax.axis_index("dp")
    place = sign * jnp.where(me % 2 == 0, me // 2, n - 1 - me // 2)
    size = part.shape[0] // n
    at = lambda k: ((place - k) % n) * size
    held = lax.dynamic_slice_in_dim(part, at(0), size, 0)
    for step in range(1, n):
        got = yield held, "dp", pairs
        held = got + lax.dynamic_slice_in_dim(part, at(step), size, 0)
    pieces = [held]
    for step in range(n - 1):
        held = yield held, "dp", pairs
        pieces.append(held)
    if size % 8 == 0:
        return assemble(jnp.stack([at(k - 1) for k in range(n)]).astype(jnp.int32), pieces)
    total = part
    for k, piece in enumerate(pieces):
        total = lax.dynamic_update_slice_in_dim(total, piece, at(k - 1), 0)
    return total


def assemble_kernel(where, *refs):
    out = refs[-1]
    for k, piece in enumerate(refs[:-1]):
        out[pl.ds(pl.multiple_of(where[k], 8), piece.shape[0]), :] = piece[...]


def assemble(where, pieces):
    size, width = pieces[0].shape
    return pl.pallas_call(
        assemble_kernel,
        in_specs=[smem()] + [pl.BlockSpec(memory_space=pltpu.VMEM)] * len(pieces),
        out_specs=pl.BlockSpec(memory_space=pltpu.VMEM),
        out_shape=sds(size * len(pieces), width),
        compiler_params=pltpu.CompilerParams(vmem_limit_bytes=VMEM_LIMIT),
        cost_estimate=cost(0, 8 * size * len(pieces) * width),
        name="assemble",
    )(where, *pieces)


def halving(part, turn):
    n = lax.axis_size("dp")
    bits = list(range(n.bit_length() - 1))
    bits = bits[turn:] + bits[:turn]
    me = lax.axis_index("dp")
    pairs = lambda bit: [(i, i ^ (1 << bit)) for i in range(n)]
    for bit in bits:
        upper = (me >> bit) % 2
        half = part.shape[0] // 2
        keep, give = (lax.dynamic_slice_in_dim(part, k * half, half, 0) for k in (upper, 1 - upper))
        part = keep + (yield give, "dp", pairs(bit))
    for bit in bits[::-1]:
        upper = (me >> bit) % 2 == 1
        other = yield part, "dp", pairs(bit)
        part = jnp.concatenate(
            [jnp.where(upper, other, part), jnp.where(upper, part, other)], axis=0
        )
    return part


def cube(x):
    n = lax.axis_size("dp")
    bit = 1
    while bit < n:
        x = x + (yield x, "dp", [(i, i ^ bit) for i in range(n)])
        bit *= 2
    return x


class Steps:
    def __init__(self):
        self.active, self.results = {}, {}

    def add(self, name, moves):
        self.active[name] = (moves, next(moves))

    def run(self, work=None, inputs=()):
        names = list(self.active)
        sends = [self.active[name][1][0] for name in names]
        sends, inputs = lax.optimization_barrier((sends, tuple(inputs)))
        got = [lax.ppermute(x, *self.active[name][1][1:]) for name, x in zip(names, sends)]
        done = work(*inputs) if work else ()
        got, done = lax.optimization_barrier((got, done))
        for name, x in zip(names, got):
            moves = self.active.pop(name)[0]
            try:
                self.active[name] = (moves, moves.send(x))
            except StopIteration as stop:
                self.results[name] = stop.value
        return done

    def finish(self):
        while self.active:
            self.run()


def per_device(
    hidden_in,
    roi,
    bn_gain,
    bn_bias,
    w_qkv,
    bias_qv,
    w_out,
    bias_out,
    ln1_gain,
    ln1_bias,
    w_in,
    bias_in,
    w_back,
    bias_back,
    ln2_gain,
    ln2_bias,
    pair_w,
    pair_bias,
    dir_w,
    text_len,
    owner_order,
    pair_index,
    cot_out,
    cot_logits,
):
    docs = text_len.shape[0]
    slots = hidden_in.shape[0] // docs
    width = hidden_in.shape[1]
    segs = slots - TEXT
    seg_rows = roi.shape[0]
    n_dp = lax.axis_size("dp")
    all_rows = seg_rows * n_dp
    half, half_seg = TEXT // 2, segs // 2
    m = lax.axis_index("mp")
    c = m % 2
    dp = lax.axis_index("dp")
    shifts = (dp % 2, dp // 2 % 2)
    place = jnp.stack([c, *shifts]).astype(jnp.int32)
    part = w_qkv.shape[2]
    from_sib = lambda x: swap(x, "mp", 1)
    from_x = lambda x: swap(x, "mp", 2)
    later = lambda w, after: lax.optimization_barrier((w, after))[0]

    def near(k, *arrays):
        parts = []
        for w in arrays:
            size = w.shape[0] // 2
            parts.append(lax.dynamic_slice_in_dim(w, shifts[k] * size, size, 0))
        return from_x(jnp.concatenate(parts, axis=0))

    second = jnp.arange(2, dtype=jnp.int32)[:, None] == 1

    def merge(one, two, count):
        gap = one[0:1] - two[0:1]
        both = one + two
        return jnp.where(second, both + gap * gap * (0.5 * seg_rows * count), 0.5 * both)

    own = (w_out, w_in, w_back)
    close_in = near(0, w_out, w_in)
    close_back = near(1, w_back)
    own_sib = tuple(from_sib(w) for w in own)
    bias_sib, bias_x = from_sib(bias_in), from_x(bias_in)
    bias_xsib = from_sib(bias_x)
    stats = butterfly(local_stats(roi), merge)
    stats, bias_rows = lax.optimization_barrier(
        (stats, (bias_in, bias_sib, bias_x, bias_xsib))
    )
    qkv, lse, both_seg, both_txt, x_seg, x_txt = attn_fwd(
        all_rows, place, text_len, hidden_in, roi, stats, bn_gain, bn_bias, w_qkv, bias_qv
    )

    close, own_sib, both_seg, both_txt = lax.optimization_barrier(
        ((close_in, close_back), own_sib, both_seg, both_txt)
    )
    far = (swap(close[0], "dp", 1), swap(close[1], "dp", 2))
    far_seg, far_txt = from_x(both_seg), from_x(both_txt)
    close_sib = tuple(from_sib(w) for w in close)
    both_sib = (from_sib(both_seg), from_sib(both_txt))
    far, far_seg, far_txt, close_sib, both_sib = lax.optimization_barrier(
        (far, far_seg, far_txt, close_sib, both_sib)
    )
    far_sib = tuple(from_sib(w) for w in far)
    weights = ((w_out, own_sib[0]),) + tuple(
        (own[1 + k], own_sib[1 + k], close[k], far[k], close_sib[k], far_sib[k]) for k in range(2)
    )
    ctx_seg = (both_seg, both_sib[0], far_seg, from_sib(far_seg))
    ctx_txt = (both_txt, both_sib[1], far_txt, from_sib(far_txt))
    vec = (bias_out, ln1_gain, ln1_bias, bias_back, ln2_gain, ln2_bias)
    mine_rows = docs * (half + half_seg)
    txt_rows = docs * half
    seg = ffn(
        place, vec, bias_rows, weights, docs * half_seg, txt_rows, mine_rows, None,
        ctx=ctx_seg, xres=x_seg,
    )

    txt = {name: seg[name] for name in ("h1", "act0", "act1")}
    txt_sums, gwo = [], []

    def text(doc, *first):
        done = ffn(
            place, vec, bias_rows, weights, half, 0, mine_rows, None,
            ctx=ctx_txt, xres=first[0], gout=cot_out, into=txt, start=doc, count=1,
        )
        txt_sums.append(done.pop("sums"))
        gwo.append(done.pop("gwo"))
        txt.update(done)

    share = width // lax.axis_size("mp")
    cols = lambda x, who: lax.dynamic_slice_in_dim(x, who * share, share, 1)
    mine, theirs = cols(seg["out"], m), from_sib(cols(seg["out"], m ^ 1))
    by_core = lambda a, b: (jnp.where(c == 0, a, b), jnp.where(c == 0, b, a))
    columns = jnp.stack(
        [p.reshape(docs, half_seg, share) for p in by_core(mine, theirs)], axis=1
    ).reshape(seg_rows, share)
    ordering = owner_order[0]
    swap_rows = lambda x: lax.all_to_all(x, "dp", split_axis=0, concat_axis=0, tiled=True)
    ordered, x_txt = lax.optimization_barrier((jnp.take(columns, ordering, axis=0), x_txt))
    received = swap_rows(ordered)
    text(0, x_txt)
    received, x_txt = lax.optimization_barrier((received, later(x_txt, txt_sums[0])))
    candidates = jnp.arange(seg_rows, dtype=jnp.int32)[None, :]
    pick_left = (pair_index[:, 0:1] == candidates).astype(F32)
    pick_right = (pair_index[:, 1:2] == candidates).astype(F32)
    sides = jnp.concatenate([product(pick_left, received), product(pick_right, received)], axis=1)
    pair_w2 = pair_w.reshape(2 * share, width)
    pair_part = product(sides, pair_w2)
    pair_part = pair_part + from_sib(pair_part)
    pairs_half = pair_part.shape[0] // 2
    piece = lax.dynamic_slice_in_dim(pair_part, c * pairs_half, pairs_half, 0)
    piece, x_txt = lax.optimization_barrier((piece, x_txt))
    other = from_x(piece)
    if docs > 1:
        text(1, x_txt)
    piece, x_txt = lax.optimization_barrier((piece + later(other, txt_sums[-1]), x_txt))
    pair_pre = jnp.concatenate(by_core(piece, from_sib(piece)), axis=0) + pair_bias
    root = 0.5 * (1.0 + lax.erf(pair_pre * ROOT_HALF))
    pair_act = pair_pre * root
    logits = product(pair_act, dir_w)
    grad_dir_w = product(cot_logits, pair_act, ((0,), (0,)))
    grad_pair_pre = product(cot_logits, dir_w, ((1,), (1,))) * (
        root + pair_pre * jnp.exp(-0.5 * pair_pre * pair_pre) * DENSITY
    )
    grad_pair_bias = jnp.sum(grad_pair_pre, axis=0)
    grad_pair_w = product(sides, grad_pair_pre, ((0,), (0,)))
    grad_sides = product(grad_pair_pre, pair_w2, ((1,), (1,)))
    grad_received = product(pick_left, grad_sides[:, :share], ((0,), (0,))) + product(
        pick_right, grad_sides[:, share:], ((0,), (0,))
    )
    grad_received, x_txt = lax.optimization_barrier((grad_received, x_txt))
    grad_sent = swap_rows(grad_received)
    for doc in range(2, docs):
        text(doc, x_txt)
    grad_sent = later(grad_sent, txt_sums[-1])
    back_order = jnp.zeros_like(ordering).at[ordering].set(jnp.arange(seg_rows, dtype=jnp.int32))
    grad_cols = jnp.take(grad_sent, back_order, axis=0).reshape(docs, 2, half_seg, share)
    rows_of = lambda who: lax.dynamic_index_in_dim(grad_cols, who, 1, keepdims=False).reshape(
        docs * half_seg, share
    )
    grad_mine, grad_theirs = rows_of(c), from_sib(rows_of(1 - c))
    chip_cols = jnp.concatenate(by_core(grad_mine, grad_theirs), axis=1)
    far_cols = from_x(chip_cols)
    low_x = m < 2
    grad_seg = jnp.concatenate(
        [jnp.where(low_x, chip_cols, far_cols), jnp.where(low_x, far_cols, chip_cols)], axis=1
    )
    cot_seg = lax.dynamic_slice_in_dim(
        cot_out.reshape(docs, slots, width), TEXT + c * half_seg, half_seg, 1
    ).reshape(docs * half_seg, width)
    output = join_rows(
        docs, segs, place, seg["out"], txt["out"],
        from_sib(seg["out"]), from_sib(later(txt["out"], grad_cols)),
    )
    grad_seg, output = lax.optimization_barrier((grad_seg, output))
    back = ffn(
        place, vec, bias_rows, weights, docs * half_seg, txt_rows, mine_rows,
        [seg[name] for name in ("n1", "f1", "n2", "f2", "slope")],
        ctx=ctx_seg, gout=cot_seg + grad_seg,
        into={name: txt[name] for name in ("gs", "gi0", "gi1", "gf")},
    )

    tall = ((0,), (0,))
    sib_back = from_sib(product(txt["act1"], back["gs"], tall))
    sib_in = from_sib(product(txt["h1"], back["gi1"], tall))
    grad_back_own = product(txt["act0"], back["gs"], tall) + sib_back
    grad_in_own = product(txt["h1"], back["gi0"], tall) + sib_in
    gf_txt, gf_seg = back["gf"][:txt_rows], back["gf"][txt_rows:]
    gwo = sum(gwo) + back["gwo"]
    grad_out_own = gwo[:part] + from_sib(gwo[part:])

    steps = Steps()
    steps.add("in_out", ring(jnp.concatenate([grad_in_own, grad_out_own], axis=0), 1))
    steps.add("back_pair", ring(jnp.concatenate([grad_back_own, grad_pair_w], axis=0), -1))
    mine = (back["gb"], txt["gb"])
    theirs = tuple(from_sib(g) for g in mine)
    w_sum = jnp.zeros((3 * part, width), F32)
    b_sum = jnp.zeros((1, 3 * part), F32)
    gx = []
    for doc in range(docs):

        def scores(b_sum, doc=doc):
            return attn_bwd(
                doc, place, text_len, qkv, lse, (both_seg, both_txt), mine, theirs, b_sum
            )

        def weights_of(gq, w_sum, doc=doc):
            return qkv_bwd(
                all_rows, doc, docs, place, hidden_in, roi, stats, bn_gain, bn_bias, w_qkv, gq, w_sum
            )

        gq, b_sum = steps.run(scores, (b_sum,))
        gx_mine, gx_theirs, w_sum = steps.run(weights_of, (gq, w_sum))
        chip_sum = gx_mine + from_sib(gx_theirs)
        gx.append((chip_sum, from_x(chip_sum)))
    cut = w_sum.shape[0] * 5 // 9
    steps.add("qkv_low", halving(w_sum[:cut], 0))
    steps.add("qkv_high", halving(w_sum[cut:], 1))
    gh_mine, gh_theirs = [], []
    for doc in range(docs):
        first = jnp.concatenate(
            [gf_seg[doc * half_seg : (doc + 1) * half_seg], gf_txt[doc * half : (doc + 1) * half]],
            axis=0,
        )
        if doc:
            steps.run()
        (far,) = steps.run(lambda x: (x,), (gx[doc][1],))
        gh_mine.append(first + (gx[doc][0] + far))
        gh_theirs.append(from_sib(gh_mine[-1]))
    (gh_theirs[-1],) = steps.run(lambda x: (x,), (gh_theirs[-1],))
    grad_hidden, bn_sums = final_rows(all_rows, segs, place, gh_mine, gh_theirs, roi, stats)

    rows = sum(txt_sums) + back["sums"]
    rows = jnp.concatenate([rows[:6], rows[6:7]]) + from_sib(jnp.concatenate([rows[:6], rows[7:8]]))
    pad = lambda v: jnp.pad(v, (0, width - v.shape[0]))[None]
    vectors = jnp.concatenate(
        [
            rows,
            grad_pair_bias[None],
            grad_dir_w,
            pad(b_sum[0, :part]),
            pad(b_sum[0, 2 * part :]),
            bn_sums[0:2],
        ],
        axis=0,
    )
    steps.add("vectors", cube(vectors))
    steps.finish()
    vectors, in_out, back_pair, low, high = (
        steps.results[name] for name in ("vectors", "in_out", "back_pair", "qkv_low", "qkv_high")
    )
    sum_qkv = jnp.concatenate([low, high], axis=0)
    n_dirs = dir_w.shape[1]
    sum_dir_w = vectors[8 : 8 + n_dirs].T
    tail = vectors[8 + n_dirs :]
    sum_bias_qv = tail[0:2, :part]
    grad_bn_bias, grad_bn_gain = tail[2], tail[3]
    grad_roi_out = grad_hidden.reshape(docs, slots, width)[:, TEXT:].reshape(seg_rows, width)
    roi_factor = lax.rsqrt(stats[1] / all_rows + EPSILON)
    roi_normed = (roi - stats[0]) * roi_factor
    grad_roi = (
        bn_gain
        * roi_factor
        * (grad_roi_out - grad_bn_bias / all_rows - roi_normed * grad_bn_gain / all_rows)
    )
    return (
        output,
        logits,
        grad_hidden,
        grad_roi,
        grad_bn_gain,
        grad_bn_bias,
        jnp.transpose(sum_qkv.reshape(3, part, width), (0, 2, 1)),
        sum_bias_qv,
        in_out[width:],
        vectors[5],
        vectors[3],
        vectors[4],
        in_out[:width],
        vectors[6],
        back_pair[:width],
        vectors[2],
        vectors[0],
        vectors[1],
        back_pair[width:].reshape(2, share, width),
        vectors[7],
        sum_dir_w,
    )


def solution(mesh):
    placed = (
        P("dp", None),
        P("dp", None),
        P(),
        P(),
        P(None, None, "mp"),
        P(None, "mp"),
        P("mp", None),
        P(),
        P(),
        P(),
        P(None, "mp"),
        P("mp"),
        P("mp", None),
        P(),
        P(),
        P(),
        P(None, "mp", None),
        P(),
        P(),
        P("dp"),
        P("dp", None),
        P("dp", None),
        P("dp", None),
        P("dp", None),
    )
    return jax.shard_map(
        per_device,
        mesh=mesh,
        in_specs=placed,
        out_specs=(
            P("dp", None),
            P("dp", None),
            P("dp", None),
            P("dp", None),
            P(),
            P(),
            P(None, None, "mp"),
            P(None, "mp"),
            P("mp", None),
            P(),
            P(),
            P(),
            P(None, "mp"),
            P("mp"),
            P("mp", None),
            P(),
            P(),
            P(),
            P(None, "mp", None),
            P(),
            P(),
        ),
        check_vma=False,
    )
```

```python
import functools

import jax
import jax.numpy as jnp
from jax import lax
from jax.experimental import pallas as pl
from jax.experimental.pallas import tpu as pltpu
from jax.sharding import PartitionSpec as P

HEAD_DIM = 64
TEXT = 512
EPSILON = 1e-05
NEGATIVE = -1e30
ROOT_HALF = 0.7071067811865476
DENSITY = 0.3989422804014327
HIGH = lax.Precision.HIGH
QUERY_STEP = 256
VMEM_LIMIT = 60 << 20
F32 = jnp.float32
BF16 = jnp.bfloat16


def product(operand, other, dims=((1,), (0,))):
    return lax.dot_general(
        operand, other, (dims, ((), ())), precision=HIGH, preferred_element_type=F32
    )


def halves(x):
    hi = x.astype(BF16)
    return hi, (x - hi.astype(F32)).astype(BF16)


def dot(a, b, dims=((1,), (0,))):
    return lax.dot_general(a, b, (dims, ((), ())), preferred_element_type=F32)


ROWS_BY_ROWS = ((1,), (1,))
COLS_BY_COLS = ((0,), (0,))


def dot3_apart(a, b, dims=((1,), (0,))):
    return dot(a[0], b[0], dims) + dot(a[1], b[0], dims) + dot(a[0], b[1], dims)


def dot3(a, b, dims=((1,), (0,))):
    ka, kb = dims[0][0], dims[1][0]
    return dot(jnp.concatenate([a[0], a[1], a[0]], ka), jnp.concatenate([b[0], b[0], b[1]], kb), dims)


def gelu_parts(v):
    phi = 0.5 + 0.5 * lax.erf(v * ROOT_HALF)
    return v * phi, phi + v * jnp.exp(-0.5 * v * v) * DENSITY


def normalize_rows(y):
    center = y - jnp.mean(y, axis=-1, keepdims=True)
    factor = lax.rsqrt(jnp.mean(center * center, axis=-1, keepdims=True) + EPSILON)
    return center * factor, factor


def normalize_rows_back(upstream, normed, factor):
    return factor * (
        upstream
        - jnp.mean(upstream, axis=-1, keepdims=True)
        - normed * jnp.mean(upstream * normed, axis=-1, keepdims=True)
    )


def colsum(x):
    return jnp.sum(x, axis=0, keepdims=True)


def lane_is(rows, width, lane):
    return lax.broadcasted_iota(jnp.int32, (rows, width), 1) == lane


def cost(products, moved):
    return pl.CostEstimate(flops=6 * products, bytes_accessed=moved, transcendentals=0)


def smem():
    return pl.BlockSpec(memory_space=pltpu.SMEM)


def whole(shape):
    return pl.BlockSpec(shape, lambda *_: (0,) * len(shape), pipeline_mode=pl.Buffered(1))


def sds(*shape):
    return jax.ShapeDtypeStruct(shape, F32)


def batch_normed(roi, stats, rows):
    return (roi - stats[0:1]) * lax.rsqrt(stats[1:2] / rows + EPSILON)


def segment_rows(roi, stats, rows, gain, shift):
    return batch_normed(roi[...], stats, rows) * gain[...][None, :] + shift[...][None, :]


def side_rows(ref, side, half, half_seg):
    return (
        ref.at[pl.ds(pl.multiple_of(TEXT + side * half_seg, half_seg), half_seg)],
        ref.at[pl.ds(pl.multiple_of(side * half, half), half)],
    )


def split_qkv(w, w_hi, w_lo):
    part = w.shape[2]
    for i in range(3):
        lanes = slice(i * part, (i + 1) * part)
        w_hi[:, lanes], w_lo[:, lanes] = halves(w[i])


def attn_fwd_kernel(all_rows, *refs):
    place, lens, hid, roi, stats, gain, shift, w, bias = refs[:9]
    qkv, lse, both_seg, both_txt, xm_seg, xm_txt = refs[9:15]
    w_hi, w_lo, x_seg, ctx, ctx_t = refs[15:]
    doc = pl.program_id(0)
    c = place[0]
    width = w.shape[2]
    heads = width // HEAD_DIM
    slots = hid.shape[0]
    half, half_seg = TEXT // 2, (slots - TEXT) // 2

    @pl.when(doc == 0)
    def _():
        split_qkv(w, w_hi, w_lo)

    x_seg[...] = hid[TEXT:, :] + segment_rows(roi, stats, all_rows, gain, shift)
    wide = (w_hi[...], w_lo[...])
    added = jnp.concatenate([bias[0:1, :], jnp.zeros((1, width), F32), bias[1:2, :]], axis=1)
    for start in (0, half):
        qkv[start : start + half, :] = dot3(halves(hid[start : start + half, :]), wide) + added
    qkv[TEXT:, :] = dot3(halves(x_seg[...]), wide) + added

    position = lax.broadcasted_iota(jnp.int32, (slots, HEAD_DIM), 0)
    first = lane_is(slots, HEAD_DIM, 0)
    dead = (position >= lens[doc]) & (position < TEXT)
    key_extra = jnp.where(first & dead, NEGATIVE, 0.0).astype(BF16)
    ones = jnp.where(first, 1.0, 0.0).astype(BF16)
    one_rows = jnp.ones((16, slots), BF16)
    values = jnp.transpose(qkv[:, 2 * width :])
    for h in range(heads):
        at = h * HEAD_DIM
        q_hi, q_lo = halves(qkv[:, at : at + HEAD_DIM] * HEAD_DIM**-0.5)
        k_hi, k_lo = halves(qkv[:, width + at : width + at + HEAD_DIM])
        v_two = jnp.concatenate([*halves(values[at : at + HEAD_DIM, :]), one_rows], axis=0)
        q_pack = jnp.concatenate([q_hi, q_lo, q_hi, ones], axis=1)
        k_pack = jnp.concatenate([k_hi, k_hi, k_lo, key_extra], axis=1)
        for start in range(0, slots, QUERY_STEP):
            cols = slice(start, min(slots, start + QUERY_STEP))
            scores = dot(k_pack, q_pack[cols], ROWS_BY_ROWS)
            top = jnp.max(scores, axis=0, keepdims=True)
            p_hi, p_lo = halves(jnp.exp(scores - top))
            mixed = dot(v_two, p_hi) + dot(v_two, p_lo)
            total = mixed[2 * HEAD_DIM : 2 * HEAD_DIM + 1]
            ctx_t[at : at + HEAD_DIM, cols] = (
                mixed[:HEAD_DIM] + mixed[HEAD_DIM : 2 * HEAD_DIM]
            ) / total
            lse[h : h + 1, cols] = top + jnp.log(total)
    ctx[...] = jnp.transpose(ctx_t[...])
    for lanes, side in ((slice(0, width), c), (slice(width, 2 * width), 1 - c)):
        at_seg, at_txt = side_rows(ctx, side, half, half_seg)
        both_seg[:, lanes] = at_seg[...]
        both_txt[:, lanes] = at_txt[...]
    xm_seg[...] = x_seg[pl.ds(pl.multiple_of(c * half_seg, half_seg), half_seg), :]
    xm_txt[...] = hid[pl.ds(pl.multiple_of(c * half, half), half), :]


def by_doc(rows, lanes):
    return pl.BlockSpec((rows, lanes), lambda d: (d, 0))


def attn_fwd(all_rows, place, lens, hidden, roi, stats, gain, shift, w, bias):
    docs = lens.shape[0]
    slots, width = hidden.shape[0] // docs, hidden.shape[1]
    segs = slots - TEXT
    part = w.shape[2]
    out_rows = [
        (slots, 3 * part),
        (8, slots),
        (segs // 2, 2 * part),
        (TEXT // 2, 2 * part),
        (segs // 2, width),
        (TEXT // 2, width),
    ]
    return pl.pallas_call(
        functools.partial(attn_fwd_kernel, all_rows),
        grid=(docs,),
        in_specs=[smem(), smem(), by_doc(slots, width), by_doc(segs, width)]
        + [whole(a.shape) for a in (stats, gain, shift, w, bias)],
        out_specs=[by_doc(*s) for s in out_rows],
        out_shape=[sds(docs * s[0], s[1]) for s in out_rows],
        scratch_shapes=[
            pltpu.VMEM((width, 3 * part), BF16),
            pltpu.VMEM((width, 3 * part), BF16),
            pltpu.VMEM((segs, width), F32),
            pltpu.VMEM((slots, part), F32),
            pltpu.VMEM((part, slots), F32),
        ],
        compiler_params=pltpu.CompilerParams(vmem_limit_bytes=VMEM_LIMIT),
        cost_estimate=cost(docs * slots, slots),
        name="attn_fwd",
    )(place, lens, hidden, roi, stats, gain, shift, w, bias)


def attn_bwd_kernel(doc, *refs):
    place, lens, qkv, lse, ctx_seg, ctx_txt, gm_seg, gm_txt, gt_seg, gt_txt, b_sum = refs[:11]
    gq, b_out, o_all, g_all, gq_t = refs[11:]
    c = place[0]
    width = qkv.shape[1] // 3
    heads = width // HEAD_DIM
    slots = qkv.shape[0]
    half, half_seg = TEXT // 2, (slots - TEXT) // 2
    near, far = slice(0, width), slice(width, 2 * width)
    for dst, mine, theirs in (
        (o_all, (ctx_seg, ctx_txt), (ctx_seg, ctx_txt)),
        (g_all, (gm_seg, gm_txt), (gt_seg, gt_txt)),
    ):
        for side, sources, lanes in ((c, mine, near), (1 - c, theirs, far)):
            for place_at, source in zip(side_rows(dst, side, half, half_seg), sources):
                place_at[...] = source[:, lanes]

    position = lax.broadcasted_iota(jnp.int32, (slots, HEAD_DIM), 0)
    first = lane_is(slots, HEAD_DIM, 0)
    dead = (position >= lens[doc]) & (position < TEXT)
    key_extra = jnp.where(first & dead, NEGATIVE, 0.0).astype(BF16)
    ones = jnp.where(first, 1.0, 0.0).astype(BF16)
    none = jnp.zeros_like(ones)
    head_of = lax.broadcasted_iota(jnp.int32, (16, width), 1) // HEAD_DIM
    pick_head = jnp.where(
        head_of == lax.broadcasted_iota(jnp.int32, (16, width), 0), 1.0, 0.0
    ).astype(BF16)
    scale = HEAD_DIM**-0.5
    product_hi, product_lo = halves(g_all[...] * o_all[...])
    inner = dot(pick_head, product_hi, ROWS_BY_ROWS) + dot(pick_head, product_lo, ROWS_BY_ROWS)
    keys_t = jnp.transpose(qkv[:, width : 2 * width])
    for h in range(heads):
        at = h * HEAD_DIM
        q_hi, q_lo = halves(qkv[:, at : at + HEAD_DIM] * scale)
        k_hi, k_lo = halves(qkv[:, width + at : width + at + HEAD_DIM])
        v_hi, v_lo = halves(qkv[:, 2 * width + at : 2 * width + at + HEAD_DIM])
        g_hi, g_lo = halves(g_all[:, at : at + HEAD_DIM])
        k_rows = jnp.concatenate(halves(keys_t[at : at + HEAD_DIM, :]), axis=0)
        q_pack = jnp.concatenate([q_hi, q_lo, q_hi, ones], axis=1)
        k_pack = jnp.concatenate([k_hi, k_hi, k_lo, key_extra], axis=1)
        g_pack = jnp.concatenate([g_hi, g_lo, g_hi, none], axis=1)
        v_pack = jnp.concatenate([v_hi, v_hi, v_lo, none], axis=1)
        q_two = jnp.concatenate([q_hi, q_lo], axis=1)
        g_two = jnp.concatenate([g_hi, g_lo], axis=1)
        weights = jnp.exp(dot(k_pack, q_pack, ROWS_BY_ROWS) - lse[h : h + 1, :])
        grads = weights * (dot(v_pack, g_pack, ROWS_BY_ROWS) - inner[h : h + 1, :])
        w_two = halves(weights)
        s_two = halves(grads)
        grad_v = dot(w_two[0], g_two) + dot(w_two[1], g_two)
        grad_k = dot(s_two[0], q_two) + dot(s_two[1], q_two)
        grad_q = dot(k_rows, s_two[0]) + dot(k_rows, s_two[1])
        gq[:, width + at : width + at + HEAD_DIM] = grad_k[:, :HEAD_DIM] + grad_k[:, HEAD_DIM:]
        gq[:, 2 * width + at : 2 * width + at + HEAD_DIM] = (
            grad_v[:, :HEAD_DIM] + grad_v[:, HEAD_DIM:]
        )
        gq_t[at : at + HEAD_DIM, :] = (grad_q[:HEAD_DIM] + grad_q[HEAD_DIM:]) * scale
    gq[:, :width] = jnp.transpose(gq_t[...])
    b_out[...] = b_sum[...] + colsum(gq[...])


def attn_bwd(doc, place, lens, qkv, lse, ctx, mine, theirs, b_sum):
    docs = lens.shape[0]
    slots, cols = qkv.shape[0] // docs, qkv.shape[1]
    segs = slots - TEXT
    part = cols // 3
    of_doc = lambda rows, lanes: pl.BlockSpec((rows, lanes), lambda i: (doc, 0))
    rows = [of_doc(segs // 2, 2 * part), of_doc(TEXT // 2, 2 * part)]
    return pl.pallas_call(
        functools.partial(attn_bwd_kernel, doc),
        grid=(1,),
        in_specs=[smem(), smem(), of_doc(slots, cols), of_doc(8, slots)] + rows * 3 + [whole((1, cols))],
        out_specs=[whole((slots, cols)), whole((1, cols))],
        out_shape=[sds(slots, cols), sds(1, cols)],
        scratch_shapes=[
            pltpu.VMEM((slots, part), F32),
            pltpu.VMEM((slots, part), F32),
            pltpu.VMEM((part, slots), F32),
        ],
        compiler_params=pltpu.CompilerParams(vmem_limit_bytes=32 << 20),
        cost_estimate=cost(slots * part * 16 * slots, 8 * slots * cols),
        name="attn_bwd",
    )(place, lens, qkv, lse, *ctx, *mine, *theirs, b_sum)


def qkv_bwd_kernel(all_rows, *refs):
    place, hid, roi, stats, gain, shift, w, gq, w_sum = refs[:9]
    gx_mine, gx_theirs, w_out = refs[9:12]
    w_hi, w_lo, x_all, gx = refs[12:]
    c = place[0]
    slots = hid.shape[0]
    half, half_seg = TEXT // 2, (slots - TEXT) // 2
    split_qkv(w, w_hi, w_lo)
    x_all[:TEXT, :] = hid[:TEXT, :]
    x_all[TEXT:, :] = hid[TEXT:, :] + segment_rows(roi, stats, all_rows, gain, shift)
    wide = (w_hi[...], w_lo[...])
    for start in range(0, slots, 320):
        rows = slice(start, min(slots, start + 320))
        gx[rows, :] = dot3_apart(halves(gq[rows, :]), wide, ROWS_BY_ROWS)
    w_out[...] = w_sum[...] + dot3_apart(halves(gq[...]), halves(x_all[...]), COLS_BY_COLS)
    for dst, side in ((gx_mine, c), (gx_theirs, 1 - c)):
        at_seg, at_txt = side_rows(gx, side, half, half_seg)
        dst[:half_seg, :] = at_seg[...]
        dst[half_seg:, :] = at_txt[...]


def qkv_bwd(all_rows, doc, docs, place, hidden, roi, stats, gain, shift, w, gq, w_sum):
    slots, width = hidden.shape[0] // docs, hidden.shape[1]
    cols = gq.shape[1]
    of_doc = lambda rows, lanes: pl.BlockSpec((rows, lanes), lambda i: (doc, 0))
    return pl.pallas_call(
        functools.partial(qkv_bwd_kernel, all_rows),
        grid=(1,),
        in_specs=[smem(), of_doc(slots, width), of_doc(slots - TEXT, width)]
        + [whole(a.shape) for a in (stats, gain, shift, w, gq, w_sum)],
        out_specs=[whole((slots // 2, width)), whole((slots // 2, width)), whole((cols, width))],
        out_shape=[sds(slots // 2, width), sds(slots // 2, width), sds(cols, width)],
        scratch_shapes=[
            pltpu.VMEM((width, cols), BF16),
            pltpu.VMEM((width, cols), BF16),
            pltpu.VMEM((slots, width), F32),
            pltpu.VMEM((slots, width), F32),
        ],
        compiler_params=pltpu.CompilerParams(vmem_limit_bytes=32 << 20),
        cost_estimate=cost(slots * cols * 2 * width, 12 * slots * width),
        name="qkv_bwd",
    )(place, hidden, roi, stats, gain, shift, w, gq, w_sum)


VECTORS = ("bias_out", "ln1_gain", "ln1_bias", "bias_back", "ln2_gain", "ln2_bias")
TILES = 4
PIECE_SHARDS = (0, 1, 2, 2, 3, 3)


def piece_place(i, rows, shift):
    if i < 2:
        return 0
    half = rows // 2
    return pl.multiple_of((shift if i % 2 == 0 else 1 - shift) * half, half)


def ffn_kernel(forward, backward, names, *refs):
    ref = dict(zip(names, refs))
    place, stage, sems = ref["place"], ref["stage"], ref["sems"]
    wts, acc, a_hi, a_lo = ref["wts"], ref["acc"], ref["a_hi"], ref["a_lo"]
    wo = ref["wo"]
    resident = wts.shape[0] == TILES
    c = place[0]
    shifts = {"wo": place[1], "wi": place[1], "wb": place[2]}
    width = acc.shape[1]
    rows = acc.shape[0]
    part = wo.shape[1] // 4
    row = lambda name: ref[name][...][None, :]

    def two_shards(one, two):
        lane = lax.broadcasted_iota(jnp.int32, (rows, 2 * part), 1)
        return jnp.where(lane < part, ref[one][...], ref[two][...])

    def copies(tile):
        found = []
        for i in range(6):
            if PIECE_SHARDS[i] == tile:
                for k, kind in enumerate(("wi", "wb")):
                    piece = ref[f"{kind}{i}"]
                    if kind == "wi" and i > 1:
                        piece = piece.at[pl.ds(part // 2, width // 2)]
                    at = pl.ds(piece_place(i, width, shifts[kind]), piece.shape[0])
                    where = stage.at[tile % 2, k, at, :]
                    found.append(
                        pltpu.make_async_copy(piece, where, sems.at[tile % 2, len(found)])
                    )
        return found

    def start_tile(tile):
        for copy in copies(tile):
            copy.start()

    slot_of = lambda tile: tile if resident else tile % 2

    def ready(tile):
        for copy in copies(tile):
            copy.wait()
        slot = slot_of(tile)
        wts[slot, 0], wts[slot, 1] = halves(stage[tile % 2, 0])
        wts[slot, 2], wts[slot, 3] = halves(stage[tile % 2, 1])
        if tile + 2 < TILES:
            start_tile(tile + 2)

    def load_wo(count):
        for i in range(count):
            at = PIECE_SHARDS[i] * part + piece_place(i, part, shifts["wo"])
            where = pl.ds(at, ref[f"wo{i}"].shape[0])
            wo[0, where, :], wo[1, where, :] = halves(ref[f"wo{i}"][...])

    def run_forward(loading):
        y = ref["xres"][...] + row("bias_out")
        for one, two, at in (
            ("ctx_own", "ctx_sib", slice(0, 2 * part)),
            ("ctx_far", "ctx_farsib", slice(2 * part, 4 * part)),
        ):
            y = y + dot3(halves(two_shards(one, two)), (wo[0, at, :], wo[1, at, :]))
        normed, factor = normalize_rows(y)
        ref["n1"][...] = normed
        ref["f1"][...] = jnp.broadcast_to(factor, (rows, 128))
        h = normed * row("ln1_gain") + row("ln1_bias")
        ref["h1"][...] = h
        a_hi[...], a_lo[...] = halves(h)
        acc[...] = h + row("bias_back")
        for t in range(TILES):
            if loading and t == 0:
                ready(0)
            if loading and t + 1 < TILES:
                ready(t + 1)
            slot = slot_of(t)
            pre = dot3((a_hi[...], a_lo[...]), (wts[slot, 0], wts[slot, 1]))
            value, rise = gelu_parts(pre + row(f"bias_in{t}"))
            ref["slope"][t] = rise
            if t < 2:
                ref[f"act{t}"][...] = value
            acc[...] += dot3(halves(value), (wts[slot, 2], wts[slot, 3]))
        normed, factor = normalize_rows(acc[...])
        ref["n2"][...] = normed
        ref["f2"][...] = jnp.broadcast_to(factor, (rows, 128))
        ref["out"][...] = normed * row("ln2_gain") + row("ln2_bias")

    def run_backward(loading):
        sums = ref["sums"]
        if forward:
            g = ref["gout"][pl.ds(pl.multiple_of(c * rows, rows), rows), :]
        else:
            g = ref["gout"][...]
        n2 = ref["n2"][...]
        sums[0:1, :] += colsum(g * n2)
        sums[1:2, :] += colsum(g)
        back = normalize_rows_back(g * row("ln2_gain"), n2, ref["f2"][:, 0:1])
        sums[2:3, :] += colsum(back)
        ref["gs"][...] = back
        acc[...] = back
        a_hi[...], a_lo[...] = halves(back)
        for t in range(TILES):
            if loading and t == 0:
                ready(0)
            if loading and t + 1 < TILES:
                ready(t + 1)
            slot = slot_of(t)
            grad = dot3((a_hi[...], a_lo[...]), (wts[slot, 2], wts[slot, 3]), ROWS_BY_ROWS)
            grad = grad * ref["slope"][t]
            if t < 2:
                ref[f"gi{t}"][...] = grad
                sums[6 + t : 7 + t, :] += colsum(grad)
            acc[...] += dot3(halves(grad), (wts[slot, 0], wts[slot, 1]), ROWS_BY_ROWS)
        g, n1 = acc[...], ref["n1"][...]
        sums[3:4, :] += colsum(g * n1)
        sums[4:5, :] += colsum(g)
        back = normalize_rows_back(g * row("ln1_gain"), n1, ref["f1"][:, 0:1])
        sums[5:6, :] += colsum(back)
        ref["gf"][...] = back
        two = halves(back)
        at = slice(0, 2 * part)
        ref["gb"][...] = dot3(two, (wo[0, at, :], wo[1, at, :]), ROWS_BY_ROWS)
        ref["gwo"][...] = dot3_apart(halves(two_shards("ctx_own", "ctx_sib")), two, COLS_BY_COLS)

    def begin():
        start_tile(0)
        start_tile(1)
        load_wo(6 if forward else 2)
        if backward:
            ref["sums"][...] = jnp.zeros_like(ref["sums"])

    if forward and backward:

        @pl.when(pl.program_id(0) == 0)
        def _():
            begin()
            run_forward(True)
            run_backward(False)

        @pl.when(pl.program_id(0) > 0)
        def _():
            run_forward(False)
            run_backward(False)
    else:
        begin()
        if forward:
            run_forward(True)
        if backward:
            run_backward(True)


def ffn(place, vectors, bias_in, weights, block, offset, total, saved, *, ctx=None, xres=None, gout=None, into=None, start=0, count=None):
    forward, backward = xres is not None, gout is not None
    both = forward and backward
    width = vectors[0].shape[0]
    rows = ctx[0].shape[0]
    blocks = rows // block
    part = width // 4
    w_out, w_in, w_back = weights
    first = offset // block + start
    local = lambda lanes: pl.BlockSpec((block, lanes), lambda r: (start + r, 0))
    shared = pl.BlockSpec((block, width), lambda r: (first + r, 0))
    anywhere = pl.BlockSpec(memory_space=pltpu.HBM)
    names, specs, args = [], [], []

    def take(name, spec, arg):
        names.append(name)
        specs.append(spec)
        args.append(arg)

    take("place", smem(), place)
    for name, a in zip(VECTORS, vectors):
        take(name, whole(a.shape), a)
    for name, a in zip(("ctx_own", "ctx_sib", "ctx_far", "ctx_farsib"), ctx):
        take(name, local(a.shape[1]), a)
    if forward:
        for t in range(TILES):
            take(f"bias_in{t}", whole(bias_in[t].shape), bias_in[t])
        take("xres", local(width), xres)
    if backward:
        if both:
            slots = gout.shape[0] // blocks
            take("gout", pl.BlockSpec((slots, width), lambda r: (start + r, 0)), gout)
        else:
            take("gout", local(width), gout)
    kept = (
        ("n1", (block, width)),
        ("f1", (block, 128)),
        ("n2", (block, width)),
        ("f2", (block, 128)),
        ("slope", (TILES, block, width)),
    )
    if backward and not forward:
        for (name, shape), a in zip(kept, saved):
            take(name, whole(shape), a)
    for i in range(6 if forward else 2):
        piece, height = (w_out[i], part) if i < 2 else (w_in[i], part // 2)
        take(f"wo{i}", whole((height, width)), piece)
    for i in range(6):
        take(f"wi{i}", anywhere, w_in[i])
        take(f"wb{i}", anywhere, w_back[i])
    outs = []
    if forward:
        outs += [("out", local(width), sds(rows, width))]
        outs += [(n, shared, sds(total, width)) for n in ("h1", "act0", "act1")]
        if not backward:
            outs += [(name, whole(shape), sds(*shape)) for name, shape in kept]
    if backward:
        outs += [(n, shared, sds(total, width)) for n in ("gs", "gi0", "gi1", "gf")]
        outs += [("gb", local(2 * part), sds(rows, 2 * part))]
        outs += [("gwo", whole((2 * part, width)), sds(2 * part, width))]
        outs += [("sums", whole((8, width)), sds(8, width))]
    aliases = {}
    if into:
        for k, (name, _, _) in enumerate(outs):
            if name in into:
                aliases[len(args)] = k
                take(name + "_into", anywhere, into[name])
    scratch = [
        ("stage", pltpu.VMEM((2, 2, width, width), F32)),
        ("sems", pltpu.SemaphoreType.DMA((2, 4))),
        ("wts", pltpu.VMEM((TILES if both else 2, 4, width, width), BF16)),
        ("wo", pltpu.VMEM((2, width, width), BF16)),
        ("acc", pltpu.VMEM((block, width), F32)),
        ("a_hi", pltpu.VMEM((block, width), BF16)),
        ("a_lo", pltpu.VMEM((block, width), BF16)),
    ]
    if both:
        scratch += [(name, pltpu.VMEM(shape, F32)) for name, shape in kept]
    all_names = names + [o[0] for o in outs] + [s[0] for s in scratch]
    passes = (3 if both else 1) * 8
    result = pl.pallas_call(
        functools.partial(ffn_kernel, forward, backward, all_names),
        grid=(count or blocks,),
        in_specs=specs,
        out_specs=[o[1] for o in outs],
        out_shape=[o[2] for o in outs],
        scratch_shapes=[s[1] for s in scratch],
        input_output_aliases=aliases,
        compiler_params=pltpu.CompilerParams(vmem_limit_bytes=VMEM_LIMIT),
        cost_estimate=cost(
            (count or blocks) * block * width * width * (16 if both else 8) + 4 * width**3,
            60 * block * width,
        ),
        name="ffn_" + "fwd" * forward + "bwd" * backward,
    )(*args)
    return {o[0]: r for o, r in zip(outs, result)}


def join_kernel(docs, segs, place, ms, mt, ts, tt, out):
    c = place[0]
    half, half_seg = TEXT // 2, segs // 2
    for seg, txt, side in ((ms, mt, c), (ts, tt, 1 - c)):
        at_seg, at_txt = side_rows(out, side, half, half_seg)
        at_seg[...] = seg[...]
        at_txt[...] = txt[...]


def join_rows(docs, segs, place, ms, mt, ts, tt):
    width = ms.shape[1]
    slots = TEXT + segs
    return pl.pallas_call(
        functools.partial(join_kernel, docs, segs),
        grid=(docs,),
        in_specs=[smem()] + [by_doc(segs // 2, width), by_doc(TEXT // 2, width)] * 2,
        out_specs=by_doc(slots, width),
        out_shape=sds(docs * slots, width),
        cost_estimate=cost(0, 8 * docs * slots * width),
        compiler_params=pltpu.CompilerParams(vmem_limit_bytes=VMEM_LIMIT),
        name="join_rows",
    )(place, ms, mt, ts, tt)


def final_kernel(docs, segs, all_rows, *refs):
    place = refs[0]
    mine, theirs = refs[1 : 1 + docs], refs[1 + docs : 1 + 2 * docs]
    roi, stats, out, sums = refs[1 + 2 * docs :]
    d = pl.program_id(0)
    c = place[0]
    half, half_seg = TEXT // 2, segs // 2

    @pl.when(d == 0)
    def _():
        sums[...] = jnp.zeros_like(sums)

    for i in range(docs):

        @pl.when(d == i)
        def _():
            for source, side in ((mine[i], c), (theirs[i], 1 - c)):
                at_seg, at_txt = side_rows(out, side, half, half_seg)
                at_seg[...] = source[:half_seg, :]
                at_txt[...] = source[half_seg:, :]

    g = out[TEXT:, :]
    sums[0:1, :] += colsum(g)
    sums[1:2, :] += colsum(g * batch_normed(roi[...], stats, all_rows))


def final_rows(all_rows, segs, place, mine, theirs, roi, stats):
    docs = len(mine)
    width = roi.shape[1]
    slots = TEXT + segs
    return pl.pallas_call(
        functools.partial(final_kernel, docs, segs, all_rows),
        grid=(docs,),
        in_specs=[smem()]
        + [whole((slots // 2, width))] * (2 * docs)
        + [by_doc(segs, width), whole(stats.shape)],
        out_specs=[by_doc(slots, width), pl.BlockSpec((8, width), lambda d: (0, 0))],
        out_shape=[sds(docs * slots, width), sds(8, width)],
        compiler_params=pltpu.CompilerParams(vmem_limit_bytes=VMEM_LIMIT),
        cost_estimate=cost(0, 20 * docs * slots * width),
        name="final_rows",
    )(place, *mine, *theirs, roi, stats)


def stats_kernel(roi, stats):
    x = roi[...]
    mean = jnp.mean(x, axis=0, keepdims=True)
    stats[0:1, :] = mean
    stats[1:2, :] = colsum((x - mean) * (x - mean))


def local_stats(roi):
    width = roi.shape[1]
    return pl.pallas_call(
        stats_kernel, out_shape=sds(2, width), name="local_stats"
    )(roi)


def swap(x, axis, bit):
    n = lax.axis_size(axis)
    return lax.ppermute(x, axis, [(i, i ^ bit) for i in range(n)])


def butterfly(x, merge):
    bit = 1
    while bit < lax.axis_size("dp"):
        x = merge(x, swap(x, "dp", bit), bit)
        bit *= 2
    return x


def ring(part, sign, cuts):
    n = lax.axis_size("dp")
    order = list(range(0, n, 2)) + list(range(n - 1, 0, -2))
    pairs = [(order[k], order[(k + sign) % n]) for k in range(n)]
    me = lax.axis_index("dp")
    place = sign * jnp.where(me % 2 == 0, me // 2, n - 1 - me // 2)
    size = part.shape[0] // n
    at = lambda k: ((place - k) % n) * size
    held = lax.dynamic_slice_in_dim(part, at(0), size, 0)
    for step in range(1, n):
        got = yield held, "dp", pairs
        held = got + lax.dynamic_slice_in_dim(part, at(step), size, 0)
    pieces = [held]
    for step in range(n - 1):
        held = yield held, "dp", pairs
        pieces.append(held)
    if size % 8 == 0:
        where = jnp.stack([at(k - 1) for k in range(n)]).astype(jnp.int32)
        return assemble(where, pieces, cuts)
    total = part
    for k, piece in enumerate(pieces):
        total = lax.dynamic_update_slice_in_dim(total, piece, at(k - 1), 0)
    return [total[sum(cuts[:i]) : sum(cuts[: i + 1])] for i in range(len(cuts))]


def assemble_kernel(count, where, *refs):
    outs, total = refs[count:-1], refs[-1]
    for k, piece in enumerate(refs[:count]):
        total[pl.ds(pl.multiple_of(where[k], 8), piece.shape[0]), :] = piece[...]
    at = 0
    for out in outs:
        out[...] = total[at : at + out.shape[0], :]
        at += out.shape[0]


def assemble(where, pieces, cuts):
    size, width = pieces[0].shape
    return pl.pallas_call(
        functools.partial(assemble_kernel, len(pieces)),
        in_specs=[smem()] + [pl.BlockSpec(memory_space=pltpu.VMEM)] * len(pieces),
        out_specs=[pl.BlockSpec(memory_space=pltpu.VMEM)] * len(cuts),
        out_shape=[sds(rows, width) for rows in cuts],
        scratch_shapes=[pltpu.VMEM((size * len(pieces), width), F32)],
        compiler_params=pltpu.CompilerParams(vmem_limit_bytes=VMEM_LIMIT),
        cost_estimate=cost(0, 8 * size * len(pieces) * width),
        name="assemble",
    )(where, *pieces)


def halving(part, turn):
    n = lax.axis_size("dp")
    bits = list(range(n.bit_length() - 1))
    bits = bits[turn:] + bits[:turn]
    me = lax.axis_index("dp")
    pairs = lambda bit: [(i, i ^ (1 << bit)) for i in range(n)]
    for bit in bits:
        upper = (me >> bit) % 2
        half = part.shape[0] // 2
        keep, give = (lax.dynamic_slice_in_dim(part, k * half, half, 0) for k in (upper, 1 - upper))
        part = keep + (yield give, "dp", pairs(bit))
    for bit in bits[::-1]:
        upper = (me >> bit) % 2 == 1
        other = yield part, "dp", pairs(bit)
        part = jnp.concatenate(
            [jnp.where(upper, other, part), jnp.where(upper, part, other)], axis=0
        )
    return part


def cube(x):
    n = lax.axis_size("dp")
    bit = 1
    while bit < n:
        x = x + (yield x, "dp", [(i, i ^ bit) for i in range(n)])
        bit *= 2
    return x


class Steps:
    def __init__(self):
        self.active, self.results = {}, {}

    def add(self, name, moves):
        self.active[name] = (moves, next(moves))

    def run(self, work=None, inputs=()):
        names = list(self.active)
        sends = [self.active[name][1][0] for name in names]
        sends, inputs = lax.optimization_barrier((sends, tuple(inputs)))
        got = [lax.ppermute(x, *self.active[name][1][1:]) for name, x in zip(names, sends)]
        done = work(*inputs) if work else ()
        got, done = lax.optimization_barrier((got, done))
        for name, x in zip(names, got):
            moves = self.active.pop(name)[0]
            try:
                self.active[name] = (moves, moves.send(x))
            except StopIteration as stop:
                self.results[name] = stop.value
        return done

    def finish(self):
        while self.active:
            self.run()


def per_device(
    hidden_in,
    roi,
    bn_gain,
    bn_bias,
    w_qkv,
    bias_qv,
    w_out,
    bias_out,
    ln1_gain,
    ln1_bias,
    w_in,
    bias_in,
    w_back,
    bias_back,
    ln2_gain,
    ln2_bias,
    pair_w,
    pair_bias,
    dir_w,
    text_len,
    owner_order,
    pair_index,
    cot_out,
    cot_logits,
):
    docs = text_len.shape[0]
    slots = hidden_in.shape[0] // docs
    width = hidden_in.shape[1]
    segs = slots - TEXT
    seg_rows = roi.shape[0]
    n_dp = lax.axis_size("dp")
    all_rows = seg_rows * n_dp
    half, half_seg = TEXT // 2, segs // 2
    m = lax.axis_index("mp")
    c = m % 2
    dp = lax.axis_index("dp")
    shifts = (dp % 2, dp // 2 % 2)
    place = jnp.stack([c, *shifts]).astype(jnp.int32)
    part = w_qkv.shape[2]
    from_sib = lambda x: swap(x, "mp", 1)
    from_x = lambda x: swap(x, "mp", 2)
    later = lambda w, after: lax.optimization_barrier((w, after))[0]

    def near(k, *arrays):
        parts = []
        for w in arrays:
            size = w.shape[0] // 2
            parts.append(lax.dynamic_slice_in_dim(w, shifts[k] * size, size, 0))
        return from_x(jnp.concatenate(parts, axis=0))

    second = jnp.arange(2, dtype=jnp.int32)[:, None] == 1

    def merge(one, two, count):
        gap = one[0:1] - two[0:1]
        both = one + two
        return jnp.where(second, both + gap * gap * (0.5 * seg_rows * count), 0.5 * both)

    own = (w_out, w_in, w_back)
    close_in = near(0, w_out, w_in)
    close_back = near(1, w_back)
    own_sib = tuple(from_sib(w) for w in own)
    bias_sib, bias_x = from_sib(bias_in), from_x(bias_in)
    bias_xsib = from_sib(bias_x)
    stats = butterfly(local_stats(roi), merge)
    stats, bias_rows = lax.optimization_barrier(
        (stats, (bias_in, bias_sib, bias_x, bias_xsib))
    )
    qkv, lse, both_seg, both_txt, x_seg, x_txt = attn_fwd(
        all_rows, place, text_len, hidden_in, roi, stats, bn_gain, bn_bias, w_qkv, bias_qv
    )

    close, own_sib, both_seg, both_txt = lax.optimization_barrier(
        ((close_in, close_back), own_sib, both_seg, both_txt)
    )
    far = (swap(close[0], "dp", 1), swap(close[1], "dp", 2))
    far_seg, far_txt = from_x(both_seg), from_x(both_txt)
    close_sib = tuple(from_sib(w) for w in close)
    both_sib = (from_sib(both_seg), from_sib(both_txt))
    far, far_seg, close_sib, both_sib = lax.optimization_barrier(
        (far, far_seg, close_sib, both_sib)
    )
    far_sib = tuple(from_sib(w) for w in far)
    weights = ((w_out, own_sib[0]),) + tuple(
        (own[1 + k], own_sib[1 + k], close[k], far[k], close_sib[k], far_sib[k]) for k in range(2)
    )
    ctx_seg = (both_seg, both_sib[0], far_seg, from_sib(far_seg))
    vec = (bias_out, ln1_gain, ln1_bias, bias_back, ln2_gain, ln2_bias)
    mine_rows = docs * (half + half_seg)
    txt_rows = docs * half
    seg = ffn(
        place, vec, bias_rows, weights, docs * half_seg, txt_rows, mine_rows, None,
        ctx=ctx_seg, xres=x_seg,
    )

    far_txt = later(far_txt, seg["out"])
    ctx_txt = (both_txt, both_sib[1], far_txt, from_sib(far_txt))

    txt = {name: seg[name] for name in ("h1", "act0", "act1")}
    txt_sums, gwo = [], []

    def text(doc, *first):
        done = ffn(
            place, vec, bias_rows, weights, half, 0, mine_rows, None,
            ctx=ctx_txt, xres=first[0], gout=cot_out, into=txt, start=doc, count=1,
        )
        txt_sums.append(done.pop("sums"))
        gwo.append(done.pop("gwo"))
        txt.update(done)

    share = width // lax.axis_size("mp")
    cols = lambda x, who: lax.dynamic_slice_in_dim(x, who * share, share, 1)
    mine, theirs = cols(seg["out"], m), from_sib(cols(seg["out"], m ^ 1))
    by_core = lambda a, b: (jnp.where(c == 0, a, b), jnp.where(c == 0, b, a))
    columns = jnp.stack(
        [p.reshape(docs, half_seg, share) for p in by_core(mine, theirs)], axis=1
    ).reshape(seg_rows, share)
    ordering = owner_order[0]
    swap_rows = lambda x: lax.all_to_all(x, "dp", split_axis=0, concat_axis=0, tiled=True)
    ordered, x_txt = lax.optimization_barrier((jnp.take(columns, ordering, axis=0), x_txt))
    received = swap_rows(ordered)
    text(0, x_txt)
    received, x_txt = lax.optimization_barrier((received, later(x_txt, txt_sums[0])))
    candidates = jnp.arange(seg_rows, dtype=jnp.int32)[None, :]
    pick_left = (pair_index[:, 0:1] == candidates).astype(F32)
    pick_right = (pair_index[:, 1:2] == candidates).astype(F32)
    sides = jnp.concatenate([product(pick_left, received), product(pick_right, received)], axis=1)
    pair_w2 = pair_w.reshape(2 * share, width)
    pair_part = product(sides, pair_w2)
    pair_part = pair_part + from_sib(pair_part)
    pairs_half = pair_part.shape[0] // 2
    piece = lax.dynamic_slice_in_dim(pair_part, c * pairs_half, pairs_half, 0)
    piece, x_txt = lax.optimization_barrier((piece, x_txt))
    other = from_x(piece)
    if docs > 1:
        text(1, x_txt)
    piece, x_txt = lax.optimization_barrier((piece + later(other, txt_sums[-1]), x_txt))
    pair_pre = jnp.concatenate(by_core(piece, from_sib(piece)), axis=0) + pair_bias
    root = 0.5 * (1.0 + lax.erf(pair_pre * ROOT_HALF))
    pair_act = pair_pre * root
    logits = product(pair_act, dir_w)
    grad_dir_w = product(cot_logits, pair_act, ((0,), (0,)))
    grad_pair_pre = product(cot_logits, dir_w, ((1,), (1,))) * (
        root + pair_pre * jnp.exp(-0.5 * pair_pre * pair_pre) * DENSITY
    )
    grad_pair_bias = jnp.sum(grad_pair_pre, axis=0)
    grad_pair_w = product(sides, grad_pair_pre, ((0,), (0,)))
    grad_sides = product(grad_pair_pre, pair_w2, ((1,), (1,)))
    grad_received = product(pick_left, grad_sides[:, :share], ((0,), (0,))) + product(
        pick_right, grad_sides[:, share:], ((0,), (0,))
    )
    grad_received, x_txt = lax.optimization_barrier((grad_received, x_txt))
    grad_sent = swap_rows(grad_received)
    for doc in range(2, docs):
        text(doc, x_txt)
    grad_sent = later(grad_sent, txt_sums[-1])
    back_order = jnp.zeros_like(ordering).at[ordering].set(jnp.arange(seg_rows, dtype=jnp.int32))
    grad_cols = jnp.take(grad_sent, back_order, axis=0).reshape(docs, 2, half_seg, share)
    rows_of = lambda who: lax.dynamic_index_in_dim(grad_cols, who, 1, keepdims=False).reshape(
        docs * half_seg, share
    )
    grad_mine, grad_theirs = rows_of(c), from_sib(rows_of(1 - c))
    chip_cols = jnp.concatenate(by_core(grad_mine, grad_theirs), axis=1)
    far_cols = from_x(chip_cols)
    low_x = m < 2
    grad_seg = jnp.concatenate(
        [jnp.where(low_x, chip_cols, far_cols), jnp.where(low_x, far_cols, chip_cols)], axis=1
    )
    cot_seg = lax.dynamic_slice_in_dim(
        cot_out.reshape(docs, slots, width), TEXT + c * half_seg, half_seg, 1
    ).reshape(docs * half_seg, width)
    output = join_rows(
        docs, segs, place, seg["out"], txt["out"],
        from_sib(seg["out"]), from_sib(later(txt["out"], grad_cols)),
    )
    grad_seg, output = lax.optimization_barrier((grad_seg, output))
    back = ffn(
        place, vec, bias_rows, weights, docs * half_seg, txt_rows, mine_rows,
        [seg[name] for name in ("n1", "f1", "n2", "f2", "slope")],
        ctx=ctx_seg, gout=cot_seg + grad_seg,
        into={name: txt[name] for name in ("gs", "gi0", "gi1", "gf")},
    )

    tall = ((0,), (0,))
    sib_back = from_sib(product(txt["act1"], back["gs"], tall))
    sib_in = from_sib(product(txt["h1"], back["gi1"], tall))
    grad_back_own = product(txt["act0"], back["gs"], tall) + sib_back
    grad_in_own = product(txt["h1"], back["gi0"], tall) + sib_in
    gf_txt, gf_seg = back["gf"][:txt_rows], back["gf"][txt_rows:]
    gwo = sum(gwo) + back["gwo"]
    grad_out_own = gwo[:part] + from_sib(gwo[part:])

    steps = Steps()
    steps.add("in_out", ring(jnp.concatenate([grad_in_own, grad_out_own], axis=0), 1, (width, part)))
    back_pair = jnp.concatenate([grad_back_own, grad_pair_w], axis=0)
    steps.add("back_pair", ring(back_pair, -1, (width, 2 * share)))
    mine = (back["gb"], txt["gb"])
    theirs = tuple(from_sib(g) for g in mine)
    w_sum = jnp.zeros((3 * part, width), F32)
    b_sum = jnp.zeros((1, 3 * part), F32)
    gx = []
    for doc in range(docs):

        def scores(b_sum, doc=doc):
            return attn_bwd(
                doc, place, text_len, qkv, lse, (both_seg, both_txt), mine, theirs, b_sum
            )

        def weights_of(gq, w_sum, doc=doc):
            return qkv_bwd(
                all_rows, doc, docs, place, hidden_in, roi, stats, bn_gain, bn_bias, w_qkv, gq, w_sum
            )

        gq, b_sum = steps.run(scores, (b_sum,))
        gx_mine, gx_theirs, w_sum = steps.run(weights_of, (gq, w_sum))
        chip_sum = gx_mine + from_sib(gx_theirs)
        gx.append((chip_sum, from_x(chip_sum)))
    cut = w_sum.shape[0] * 5 // 9
    steps.add("qkv_low", halving(w_sum[:cut], 0))
    steps.add("qkv_high", halving(w_sum[cut:], 1))
    gh_mine, gh_theirs = [], []
    for doc in range(docs):
        first = jnp.concatenate(
            [gf_seg[doc * half_seg : (doc + 1) * half_seg], gf_txt[doc * half : (doc + 1) * half]],
            axis=0,
        )
        if doc:
            steps.run()
        (far,) = steps.run(lambda x: (x,), (gx[doc][1],))
        gh_mine.append(first + (gx[doc][0] + far))
        gh_theirs.append(from_sib(gh_mine[-1]))
    (gh_theirs[-1],) = steps.run(lambda x: (x,), (gh_theirs[-1],))
    grad_hidden, bn_sums = final_rows(all_rows, segs, place, gh_mine, gh_theirs, roi, stats)

    rows = sum(txt_sums) + back["sums"]
    rows = jnp.concatenate([rows[:6], rows[6:7]]) + from_sib(jnp.concatenate([rows[:6], rows[7:8]]))
    pad = lambda v: jnp.pad(v, (0, width - v.shape[0]))[None]
    vectors = jnp.concatenate(
        [
            rows,
            grad_pair_bias[None],
            grad_dir_w,
            pad(b_sum[0, :part]),
            pad(b_sum[0, 2 * part :]),
            bn_sums[0:2],
        ],
        axis=0,
    )
    steps.add("vectors", cube(vectors))
    steps.finish()
    vectors, in_out, back_pair, low, high = (
        steps.results[name] for name in ("vectors", "in_out", "back_pair", "qkv_low", "qkv_high")
    )
    sum_qkv = jnp.concatenate([low, high], axis=0)
    n_dirs = dir_w.shape[1]
    sum_dir_w = vectors[8 : 8 + n_dirs].T
    tail = vectors[8 + n_dirs :]
    sum_bias_qv = tail[0:2, :part]
    grad_bn_bias, grad_bn_gain = tail[2], tail[3]
    grad_roi_out = grad_hidden.reshape(docs, slots, width)[:, TEXT:].reshape(seg_rows, width)
    roi_factor = lax.rsqrt(stats[1] / all_rows + EPSILON)
    roi_normed = (roi - stats[0]) * roi_factor
    grad_roi = (
        bn_gain
        * roi_factor
        * (grad_roi_out - grad_bn_bias / all_rows - roi_normed * grad_bn_gain / all_rows)
    )
    return (
        output,
        logits,
        grad_hidden,
        grad_roi,
        grad_bn_gain,
        grad_bn_bias,
        jnp.transpose(sum_qkv.reshape(3, part, width), (0, 2, 1)),
        sum_bias_qv,
        in_out[1],
        vectors[5],
        vectors[3],
        vectors[4],
        in_out[0],
        vectors[6],
        back_pair[0],
        vectors[2],
        vectors[0],
        vectors[1],
        back_pair[1].reshape(2, share, width),
        vectors[7],
        sum_dir_w,
    )


def solution(mesh):
    placed = (
        P("dp", None),
        P("dp", None),
        P(),
        P(),
        P(None, None, "mp"),
        P(None, "mp"),
        P("mp", None),
        P(),
        P(),
        P(),
        P(None, "mp"),
        P("mp"),
        P("mp", None),
        P(),
        P(),
        P(),
        P(None, "mp", None),
        P(),
        P(),
        P("dp"),
        P("dp", None),
        P("dp", None),
        P("dp", None),
        P("dp", None),
    )
    return jax.shard_map(
        per_device,
        mesh=mesh,
        in_specs=placed,
        out_specs=(
            P("dp", None),
            P("dp", None),
            P("dp", None),
            P("dp", None),
            P(),
            P(),
            P(None, None, "mp"),
            P(None, "mp"),
            P("mp", None),
            P(),
            P(),
            P(),
            P(None, "mp"),
            P("mp"),
            P("mp", None),
            P(),
            P(),
            P(),
            P(None, "mp", None),
            P(),
            P(),
        ),
        check_vma=False,
    )
```

```python
import functools

import jax
import jax.numpy as jnp
from jax import lax
from jax.experimental import pallas as pl
from jax.experimental.pallas import tpu as pltpu
from jax.sharding import PartitionSpec as P

HEAD_DIM = 64
TEXT = 512
EPSILON = 1e-05
NEGATIVE = -1e30
ROOT_HALF = 0.7071067811865476
DENSITY = 0.3989422804014327
HIGH = lax.Precision.HIGH
QUERY_STEP = 256
VMEM_LIMIT = 60 << 20
F32 = jnp.float32
BF16 = jnp.bfloat16


def product(operand, other, dims=((1,), (0,))):
    return lax.dot_general(
        operand, other, (dims, ((), ())), precision=HIGH, preferred_element_type=F32
    )


def halves(x):
    hi = x.astype(BF16)
    return hi, (x - hi.astype(F32)).astype(BF16)


def dot(a, b, dims=((1,), (0,))):
    return lax.dot_general(a, b, (dims, ((), ())), preferred_element_type=F32)


ROWS_BY_ROWS = ((1,), (1,))
COLS_BY_COLS = ((0,), (0,))


def dot3_apart(a, b, dims=((1,), (0,))):
    return dot(a[0], b[0], dims) + dot(a[1], b[0], dims) + dot(a[0], b[1], dims)


def dot3(a, b, dims=((1,), (0,))):
    ka, kb = dims[0][0], dims[1][0]
    return dot(jnp.concatenate([a[0], a[1], a[0]], ka), jnp.concatenate([b[0], b[0], b[1]], kb), dims)


def gelu_parts(v):
    phi = 0.5 + 0.5 * lax.erf(v * ROOT_HALF)
    return v * phi, phi + v * jnp.exp(-0.5 * v * v) * DENSITY


def normalize_rows(y):
    center = y - jnp.mean(y, axis=-1, keepdims=True)
    factor = lax.rsqrt(jnp.mean(center * center, axis=-1, keepdims=True) + EPSILON)
    return center * factor, factor


def normalize_rows_back(upstream, normed, factor):
    return factor * (
        upstream
        - jnp.mean(upstream, axis=-1, keepdims=True)
        - normed * jnp.mean(upstream * normed, axis=-1, keepdims=True)
    )


def colsum(x):
    return jnp.sum(x, axis=0, keepdims=True)


def lane_is(rows, width, lane):
    return lax.broadcasted_iota(jnp.int32, (rows, width), 1) == lane


def cost(products, moved):
    return pl.CostEstimate(flops=6 * products, bytes_accessed=moved, transcendentals=0)


def smem():
    return pl.BlockSpec(memory_space=pltpu.SMEM)


def whole(shape):
    return pl.BlockSpec(shape, lambda *_: (0,) * len(shape), pipeline_mode=pl.Buffered(1))


def sds(*shape):
    return jax.ShapeDtypeStruct(shape, F32)


def batch_normed(roi, stats, rows):
    return (roi - stats[0:1]) * lax.rsqrt(stats[1:2] / rows + EPSILON)


def segment_rows(roi, stats, rows, gain, shift):
    return batch_normed(roi[...], stats, rows) * gain[...][None, :] + shift[...][None, :]


def side_rows(ref, side, half, half_seg):
    return (
        ref.at[pl.ds(pl.multiple_of(TEXT + side * half_seg, half_seg), half_seg)],
        ref.at[pl.ds(pl.multiple_of(side * half, half), half)],
    )


def split_qkv(w, w_hi, w_lo):
    part = w.shape[2]
    for i in range(3):
        lanes = slice(i * part, (i + 1) * part)
        w_hi[:, lanes], w_lo[:, lanes] = halves(w[i])


def attn_fwd_kernel(all_rows, *refs):
    place, lens, hid, roi, stats, gain, shift, w, bias = refs[:9]
    qkv, lse, both_seg, both_txt, xm_seg, xm_txt = refs[9:15]
    w_hi, w_lo, x_seg, ctx, ctx_t = refs[15:]
    doc = pl.program_id(0)
    c = place[0]
    width = w.shape[2]
    heads = width // HEAD_DIM
    slots = hid.shape[0]
    half, half_seg = TEXT // 2, (slots - TEXT) // 2

    @pl.when(doc == 0)
    def _():
        split_qkv(w, w_hi, w_lo)

    x_seg[...] = hid[TEXT:, :] + segment_rows(roi, stats, all_rows, gain, shift)
    wide = (w_hi[...], w_lo[...])
    added = jnp.concatenate([bias[0:1, :], jnp.zeros((1, width), F32), bias[1:2, :]], axis=1)
    for start in (0, half):
        qkv[start : start + half, :] = dot3(halves(hid[start : start + half, :]), wide) + added
    qkv[TEXT:, :] = dot3(halves(x_seg[...]), wide) + added

    position = lax.broadcasted_iota(jnp.int32, (slots, HEAD_DIM), 0)
    first = lane_is(slots, HEAD_DIM, 0)
    dead = (position >= lens[doc]) & (position < TEXT)
    key_extra = jnp.where(first & dead, NEGATIVE, 0.0).astype(BF16)
    ones = jnp.where(first, 1.0, 0.0).astype(BF16)
    one_rows = jnp.ones((16, slots), BF16)
    values = jnp.transpose(qkv[:, 2 * width :])
    for h in range(heads):
        at = h * HEAD_DIM
        q_hi, q_lo = halves(qkv[:, at : at + HEAD_DIM] * HEAD_DIM**-0.5)
        k_hi, k_lo = halves(qkv[:, width + at : width + at + HEAD_DIM])
        v_two = jnp.concatenate([*halves(values[at : at + HEAD_DIM, :]), one_rows], axis=0)
        q_pack = jnp.concatenate([q_hi, q_lo, q_hi, ones], axis=1)
        k_pack = jnp.concatenate([k_hi, k_hi, k_lo, key_extra], axis=1)
        for start in range(0, slots, QUERY_STEP):
            cols = slice(start, min(slots, start + QUERY_STEP))
            scores = dot(k_pack, q_pack[cols], ROWS_BY_ROWS)
            top = jnp.max(scores, axis=0, keepdims=True)
            p_hi, p_lo = halves(jnp.exp(scores - top))
            mixed = dot(v_two, p_hi) + dot(v_two, p_lo)
            total = mixed[2 * HEAD_DIM : 2 * HEAD_DIM + 1]
            ctx_t[at : at + HEAD_DIM, cols] = (
                mixed[:HEAD_DIM] + mixed[HEAD_DIM : 2 * HEAD_DIM]
            ) / total
            lse[h : h + 1, cols] = top + jnp.log(total)
    ctx[...] = jnp.transpose(ctx_t[...])
    for lanes, side in ((slice(0, width), c), (slice(width, 2 * width), 1 - c)):
        at_seg, at_txt = side_rows(ctx, side, half, half_seg)
        both_seg[:, lanes] = at_seg[...]
        both_txt[:, lanes] = at_txt[...]
    xm_seg[...] = x_seg[pl.ds(pl.multiple_of(c * half_seg, half_seg), half_seg), :]
    xm_txt[...] = hid[pl.ds(pl.multiple_of(c * half, half), half), :]


def by_doc(rows, lanes):
    return pl.BlockSpec((rows, lanes), lambda d: (d, 0))


def attn_fwd(all_rows, place, lens, hidden, roi, stats, gain, shift, w, bias):
    docs = lens.shape[0]
    slots, width = hidden.shape[0] // docs, hidden.shape[1]
    segs = slots - TEXT
    part = w.shape[2]
    out_rows = [
        (slots, 3 * part),
        (8, slots),
        (segs // 2, 2 * part),
        (TEXT // 2, 2 * part),
        (segs // 2, width),
        (TEXT // 2, width),
    ]
    return pl.pallas_call(
        functools.partial(attn_fwd_kernel, all_rows),
        grid=(docs,),
        in_specs=[smem(), smem(), by_doc(slots, width), by_doc(segs, width)]
        + [whole(a.shape) for a in (stats, gain, shift, w, bias)],
        out_specs=[by_doc(*s) for s in out_rows],
        out_shape=[sds(docs * s[0], s[1]) for s in out_rows],
        scratch_shapes=[
            pltpu.VMEM((width, 3 * part), BF16),
            pltpu.VMEM((width, 3 * part), BF16),
            pltpu.VMEM((segs, width), F32),
            pltpu.VMEM((slots, part), F32),
            pltpu.VMEM((part, slots), F32),
        ],
        compiler_params=pltpu.CompilerParams(vmem_limit_bytes=VMEM_LIMIT),
        cost_estimate=cost(docs * slots, slots),
        name="attn_fwd",
    )(place, lens, hidden, roi, stats, gain, shift, w, bias)


def attn_bwd_kernel(doc, *refs):
    place, lens, qkv, lse, ctx_seg, ctx_txt, gm_seg, gm_txt, gt_seg, gt_txt, b_sum = refs[:11]
    gq, b_out, o_all, g_all, gq_t = refs[11:]
    c = place[0]
    width = qkv.shape[1] // 3
    heads = width // HEAD_DIM
    slots = qkv.shape[0]
    half, half_seg = TEXT // 2, (slots - TEXT) // 2
    near, far = slice(0, width), slice(width, 2 * width)
    for dst, mine, theirs in (
        (o_all, (ctx_seg, ctx_txt), (ctx_seg, ctx_txt)),
        (g_all, (gm_seg, gm_txt), (gt_seg, gt_txt)),
    ):
        for side, sources, lanes in ((c, mine, near), (1 - c, theirs, far)):
            for place_at, source in zip(side_rows(dst, side, half, half_seg), sources):
                place_at[...] = source[:, lanes]

    position = lax.broadcasted_iota(jnp.int32, (slots, HEAD_DIM), 0)
    first = lane_is(slots, HEAD_DIM, 0)
    dead = (position >= lens[doc]) & (position < TEXT)
    key_extra = jnp.where(first & dead, NEGATIVE, 0.0).astype(BF16)
    ones = jnp.where(first, 1.0, 0.0).astype(BF16)
    none = jnp.zeros_like(ones)
    head_of = lax.broadcasted_iota(jnp.int32, (16, width), 1) // HEAD_DIM
    pick_head = jnp.where(
        head_of == lax.broadcasted_iota(jnp.int32, (16, width), 0), 1.0, 0.0
    ).astype(BF16)
    scale = HEAD_DIM**-0.5
    product_hi, product_lo = halves(g_all[...] * o_all[...])
    inner = dot(pick_head, product_hi, ROWS_BY_ROWS) + dot(pick_head, product_lo, ROWS_BY_ROWS)
    keys_t = jnp.transpose(qkv[:, width : 2 * width])
    for h in range(heads):
        at = h * HEAD_DIM
        q_hi, q_lo = halves(qkv[:, at : at + HEAD_DIM] * scale)
        k_hi, k_lo = halves(qkv[:, width + at : width + at + HEAD_DIM])
        v_hi, v_lo = halves(qkv[:, 2 * width + at : 2 * width + at + HEAD_DIM])
        g_hi, g_lo = halves(g_all[:, at : at + HEAD_DIM])
        k_rows = jnp.concatenate(halves(keys_t[at : at + HEAD_DIM, :]), axis=0)
        q_pack = jnp.concatenate([q_hi, q_lo, q_hi, ones], axis=1)
        k_pack = jnp.concatenate([k_hi, k_hi, k_lo, key_extra], axis=1)
        g_pack = jnp.concatenate([g_hi, g_lo, g_hi, none], axis=1)
        v_pack = jnp.concatenate([v_hi, v_hi, v_lo, none], axis=1)
        q_two = jnp.concatenate([q_hi, q_lo], axis=1)
        g_two = jnp.concatenate([g_hi, g_lo], axis=1)
        weights = jnp.exp(dot(k_pack, q_pack, ROWS_BY_ROWS) - lse[h : h + 1, :])
        grads = weights * (dot(v_pack, g_pack, ROWS_BY_ROWS) - inner[h : h + 1, :])
        w_two = halves(weights)
        s_two = halves(grads)
        grad_v = dot(w_two[0], g_two) + dot(w_two[1], g_two)
        grad_k = dot(s_two[0], q_two) + dot(s_two[1], q_two)
        grad_q = dot(k_rows, s_two[0]) + dot(k_rows, s_two[1])
        gq[:, width + at : width + at + HEAD_DIM] = grad_k[:, :HEAD_DIM] + grad_k[:, HEAD_DIM:]
        gq[:, 2 * width + at : 2 * width + at + HEAD_DIM] = (
            grad_v[:, :HEAD_DIM] + grad_v[:, HEAD_DIM:]
        )
        gq_t[at : at + HEAD_DIM, :] = (grad_q[:HEAD_DIM] + grad_q[HEAD_DIM:]) * scale
    gq[:, :width] = jnp.transpose(gq_t[...])
    b_out[...] = b_sum[...] + colsum(gq[...])


def attn_bwd(doc, place, lens, qkv, lse, ctx, mine, theirs, b_sum):
    docs = lens.shape[0]
    slots, cols = qkv.shape[0] // docs, qkv.shape[1]
    segs = slots - TEXT
    part = cols // 3
    of_doc = lambda rows, lanes: pl.BlockSpec((rows, lanes), lambda i: (doc, 0))
    rows = [of_doc(segs // 2, 2 * part), of_doc(TEXT // 2, 2 * part)]
    return pl.pallas_call(
        functools.partial(attn_bwd_kernel, doc),
        grid=(1,),
        in_specs=[smem(), smem(), of_doc(slots, cols), of_doc(8, slots)] + rows * 3 + [whole((1, cols))],
        out_specs=[whole((slots, cols)), whole((1, cols))],
        out_shape=[sds(slots, cols), sds(1, cols)],
        scratch_shapes=[
            pltpu.VMEM((slots, part), F32),
            pltpu.VMEM((slots, part), F32),
            pltpu.VMEM((part, slots), F32),
        ],
        compiler_params=pltpu.CompilerParams(vmem_limit_bytes=32 << 20),
        cost_estimate=cost(slots * part * 16 * slots, 8 * slots * cols),
        name="attn_bwd",
    )(place, lens, qkv, lse, *ctx, *mine, *theirs, b_sum)


def qkv_bwd_kernel(all_rows, *refs):
    place, hid, roi, stats, gain, shift, w, gq, w_sum = refs[:9]
    gx_mine, gx_theirs, w_out = refs[9:12]
    w_hi, w_lo, x_all, gx = refs[12:]
    c = place[0]
    slots = hid.shape[0]
    half, half_seg = TEXT // 2, (slots - TEXT) // 2
    split_qkv(w, w_hi, w_lo)
    x_all[:TEXT, :] = hid[:TEXT, :]
    x_all[TEXT:, :] = hid[TEXT:, :] + segment_rows(roi, stats, all_rows, gain, shift)
    wide = (w_hi[...], w_lo[...])
    for start in range(0, slots, 320):
        rows = slice(start, min(slots, start + 320))
        gx[rows, :] = dot3_apart(halves(gq[rows, :]), wide, ROWS_BY_ROWS)
    w_out[...] = w_sum[...] + dot3_apart(halves(gq[...]), halves(x_all[...]), COLS_BY_COLS)
    for dst, side in ((gx_mine, c), (gx_theirs, 1 - c)):
        at_seg, at_txt = side_rows(gx, side, half, half_seg)
        dst[:half_seg, :] = at_seg[...]
        dst[half_seg:, :] = at_txt[...]


def qkv_bwd(all_rows, doc, docs, place, hidden, roi, stats, gain, shift, w, gq, w_sum):
    slots, width = hidden.shape[0] // docs, hidden.shape[1]
    cols = gq.shape[1]
    of_doc = lambda rows, lanes: pl.BlockSpec((rows, lanes), lambda i: (doc, 0))
    return pl.pallas_call(
        functools.partial(qkv_bwd_kernel, all_rows),
        grid=(1,),
        in_specs=[smem(), of_doc(slots, width), of_doc(slots - TEXT, width)]
        + [whole(a.shape) for a in (stats, gain, shift, w, gq, w_sum)],
        out_specs=[whole((slots // 2, width)), whole((slots // 2, width)), whole((cols, width))],
        out_shape=[sds(slots // 2, width), sds(slots // 2, width), sds(cols, width)],
        scratch_shapes=[
            pltpu.VMEM((width, cols), BF16),
            pltpu.VMEM((width, cols), BF16),
            pltpu.VMEM((slots, width), F32),
            pltpu.VMEM((slots, width), F32),
        ],
        compiler_params=pltpu.CompilerParams(vmem_limit_bytes=32 << 20),
        cost_estimate=cost(slots * cols * 2 * width, 12 * slots * width),
        name="qkv_bwd",
    )(place, hidden, roi, stats, gain, shift, w, gq, w_sum)


VECTORS = ("bias_out", "ln1_gain", "ln1_bias", "bias_back", "ln2_gain", "ln2_bias")
TILES = 4
PIECE_SHARDS = (0, 1, 2, 2, 3, 3)


def piece_place(i, rows, shift):
    if i < 2:
        return 0
    half = rows // 2
    return pl.multiple_of((shift if i % 2 == 0 else 1 - shift) * half, half)


def ffn_kernel(forward, backward, names, *refs):
    ref = dict(zip(names, refs))
    place, stage, sems = ref["place"], ref["stage"], ref["sems"]
    wts, acc, a_hi, a_lo = ref["wts"], ref["acc"], ref["a_hi"], ref["a_lo"]
    wo = ref["wo"]
    resident = wts.shape[0] == TILES
    c = place[0]
    shifts = {"wo": place[1], "wi": place[1], "wb": place[2]}
    width = acc.shape[1]
    rows = acc.shape[0]
    part = wo.shape[1] // 4
    row = lambda name: ref[name][...][None, :]

    def two_shards(one, two):
        lane = lax.broadcasted_iota(jnp.int32, (rows, 2 * part), 1)
        return jnp.where(lane < part, ref[one][...], ref[two][...])

    def copies(tile):
        found = []
        for i in range(6):
            if PIECE_SHARDS[i] == tile:
                for k, kind in enumerate(("wi", "wb")):
                    piece = ref[f"{kind}{i}"]
                    if kind == "wi" and i > 1:
                        piece = piece.at[pl.ds(part // 2, width // 2)]
                    at = pl.ds(piece_place(i, width, shifts[kind]), piece.shape[0])
                    where = stage.at[tile % 2, k, at, :]
                    found.append(
                        pltpu.make_async_copy(piece, where, sems.at[tile % 2, len(found)])
                    )
        return found

    def start_tile(tile):
        for copy in copies(tile):
            copy.start()

    slot_of = lambda tile: tile if resident else tile % 2

    def ready(tile):
        for copy in copies(tile):
            copy.wait()
        slot = slot_of(tile)
        wts[slot, 0], wts[slot, 1] = halves(stage[tile % 2, 0])
        wts[slot, 2], wts[slot, 3] = halves(stage[tile % 2, 1])
        if tile + 2 < TILES:
            start_tile(tile + 2)

    def load_wo(count):
        for i in range(count):
            at = PIECE_SHARDS[i] * part + piece_place(i, part, shifts["wo"])
            where = pl.ds(at, ref[f"wo{i}"].shape[0])
            wo[0, where, :], wo[1, where, :] = halves(ref[f"wo{i}"][...])

    def run_forward(loading):
        y = ref["xres"][...] + row("bias_out")
        for one, two, at in (
            ("ctx_own", "ctx_sib", slice(0, 2 * part)),
            ("ctx_far", "ctx_farsib", slice(2 * part, 4 * part)),
        ):
            y = y + dot3(halves(two_shards(one, two)), (wo[0, at, :], wo[1, at, :]))
        normed, factor = normalize_rows(y)
        ref["n1"][...] = normed
        ref["f1"][...] = jnp.broadcast_to(factor, (rows, 128))
        h = normed * row("ln1_gain") + row("ln1_bias")
        ref["h1"][...] = h
        a_hi[...], a_lo[...] = halves(h)
        acc[...] = h + row("bias_back")
        for t in range(TILES):
            if loading and t == 0:
                ready(0)
            if loading and t + 1 < TILES:
                ready(t + 1)
            slot = slot_of(t)
            pre = dot3((a_hi[...], a_lo[...]), (wts[slot, 0], wts[slot, 1]))
            value, rise = gelu_parts(pre + row(f"bias_in{t}"))
            ref["slope"][t] = rise
            if t < 2:
                ref[f"act{t}"][...] = value
            acc[...] += dot3(halves(value), (wts[slot, 2], wts[slot, 3]))
        normed, factor = normalize_rows(acc[...])
        ref["n2"][...] = normed
        ref["f2"][...] = jnp.broadcast_to(factor, (rows, 128))
        ref["out"][...] = normed * row("ln2_gain") + row("ln2_bias")

    def run_backward(loading):
        sums = ref["sums"]
        if forward:
            g = ref["gout"][pl.ds(pl.multiple_of(c * rows, rows), rows), :]
        else:
            g = ref["gout"][...]
        n2 = ref["n2"][...]
        sums[0:1, :] += colsum(g * n2)
        sums[1:2, :] += colsum(g)
        back = normalize_rows_back(g * row("ln2_gain"), n2, ref["f2"][:, 0:1])
        sums[2:3, :] += colsum(back)
        ref["gs"][...] = back
        acc[...] = back
        a_hi[...], a_lo[...] = halves(back)
        for t in range(TILES):
            if loading and t == 0:
                ready(0)
            if loading and t + 1 < TILES:
                ready(t + 1)
            slot = slot_of(t)
            grad = dot3((a_hi[...], a_lo[...]), (wts[slot, 2], wts[slot, 3]), ROWS_BY_ROWS)
            grad = grad * ref["slope"][t]
            if t < 2:
                ref[f"gi{t}"][...] = grad
                sums[6 + t : 7 + t, :] += colsum(grad)
            acc[...] += dot3(halves(grad), (wts[slot, 0], wts[slot, 1]), ROWS_BY_ROWS)
        g, n1 = acc[...], ref["n1"][...]
        sums[3:4, :] += colsum(g * n1)
        sums[4:5, :] += colsum(g)
        back = normalize_rows_back(g * row("ln1_gain"), n1, ref["f1"][:, 0:1])
        sums[5:6, :] += colsum(back)
        ref["gf"][...] = back
        two = halves(back)
        at = slice(0, 2 * part)
        ref["gb"][...] = dot3(two, (wo[0, at, :], wo[1, at, :]), ROWS_BY_ROWS)
        ref["gwo"][...] = dot3_apart(halves(two_shards("ctx_own", "ctx_sib")), two, COLS_BY_COLS)

    def begin():
        start_tile(0)
        start_tile(1)
        load_wo(6 if forward else 2)
        if backward:
            ref["sums"][...] = jnp.zeros_like(ref["sums"])

    if forward and backward:

        @pl.when(pl.program_id(0) == 0)
        def _():
            begin()
            run_forward(True)
            run_backward(False)

        @pl.when(pl.program_id(0) > 0)
        def _():
            run_forward(False)
            run_backward(False)
    else:
        begin()
        if forward:
            run_forward(True)
        if backward:
            run_backward(True)


def ffn(place, vectors, bias_in, weights, block, offset, total, saved, *, ctx=None, xres=None, gout=None, into=None, start=0, count=None):
    forward, backward = xres is not None, gout is not None
    both = forward and backward
    width = vectors[0].shape[0]
    rows = ctx[0].shape[0]
    blocks = rows // block
    part = width // 4
    w_out, w_in, w_back = weights
    first = offset // block + start
    local = lambda lanes: pl.BlockSpec((block, lanes), lambda r: (start + r, 0))
    shared = pl.BlockSpec((block, width), lambda r: (first + r, 0))
    anywhere = pl.BlockSpec(memory_space=pltpu.HBM)
    names, specs, args = [], [], []

    def take(name, spec, arg):
        names.append(name)
        specs.append(spec)
        args.append(arg)

    take("place", smem(), place)
    for name, a in zip(VECTORS, vectors):
        take(name, whole(a.shape), a)
    for name, a in zip(("ctx_own", "ctx_sib", "ctx_far", "ctx_farsib"), ctx):
        take(name, local(a.shape[1]), a)
    if forward:
        for t in range(TILES):
            take(f"bias_in{t}", whole(bias_in[t].shape), bias_in[t])
        take("xres", local(width), xres)
    if backward:
        if both:
            slots = gout.shape[0] // blocks
            take("gout", pl.BlockSpec((slots, width), lambda r: (start + r, 0)), gout)
        else:
            take("gout", local(width), gout)
    kept = (
        ("n1", (block, width)),
        ("f1", (block, 128)),
        ("n2", (block, width)),
        ("f2", (block, 128)),
        ("slope", (TILES, block, width)),
    )
    if backward and not forward:
        for (name, shape), a in zip(kept, saved):
            take(name, whole(shape), a)
    for i in range(6 if forward else 2):
        piece, height = (w_out[i], part) if i < 2 else (w_in[i], part // 2)
        take(f"wo{i}", whole((height, width)), piece)
    for i in range(6):
        take(f"wi{i}", anywhere, w_in[i])
        take(f"wb{i}", anywhere, w_back[i])
    outs = []
    if forward:
        outs += [("out", local(width), sds(rows, width))]
        outs += [(n, shared, sds(total, width)) for n in ("h1", "act0", "act1")]
        if not backward:
            outs += [(name, whole(shape), sds(*shape)) for name, shape in kept]
    if backward:
        outs += [(n, shared, sds(total, width)) for n in ("gs", "gi0", "gi1", "gf")]
        outs += [("gb", local(2 * part), sds(rows, 2 * part))]
        outs += [("gwo", whole((2 * part, width)), sds(2 * part, width))]
        outs += [("sums", whole((8, width)), sds(8, width))]
    aliases = {}
    if into:
        for k, (name, _, _) in enumerate(outs):
            if name in into:
                aliases[len(args)] = k
                take(name + "_into", anywhere, into[name])
    scratch = [
        ("stage", pltpu.VMEM((2, 2, width, width), F32)),
        ("sems", pltpu.SemaphoreType.DMA((2, 4))),
        ("wts", pltpu.VMEM((TILES if both else 2, 4, width, width), BF16)),
        ("wo", pltpu.VMEM((2, width, width), BF16)),
        ("acc", pltpu.VMEM((block, width), F32)),
        ("a_hi", pltpu.VMEM((block, width), BF16)),
        ("a_lo", pltpu.VMEM((block, width), BF16)),
    ]
    if both:
        scratch += [(name, pltpu.VMEM(shape, F32)) for name, shape in kept]
    all_names = names + [o[0] for o in outs] + [s[0] for s in scratch]
    passes = (3 if both else 1) * 8
    result = pl.pallas_call(
        functools.partial(ffn_kernel, forward, backward, all_names),
        grid=(count or blocks,),
        in_specs=specs,
        out_specs=[o[1] for o in outs],
        out_shape=[o[2] for o in outs],
        scratch_shapes=[s[1] for s in scratch],
        input_output_aliases=aliases,
        compiler_params=pltpu.CompilerParams(vmem_limit_bytes=VMEM_LIMIT),
        cost_estimate=cost(
            (count or blocks) * block * width * width * (16 if both else 8) + 4 * width**3,
            60 * block * width,
        ),
        name="ffn_" + "fwd" * forward + "bwd" * backward,
    )(*args)
    return {o[0]: r for o, r in zip(outs, result)}


def join_kernel(docs, segs, place, ms, mt, ts, tt, out):
    c = place[0]
    half, half_seg = TEXT // 2, segs // 2
    for seg, txt, side in ((ms, mt, c), (ts, tt, 1 - c)):
        at_seg, at_txt = side_rows(out, side, half, half_seg)
        at_seg[...] = seg[...]
        at_txt[...] = txt[...]


def join_rows(docs, segs, place, ms, mt, ts, tt):
    width = ms.shape[1]
    slots = TEXT + segs
    return pl.pallas_call(
        functools.partial(join_kernel, docs, segs),
        grid=(docs,),
        in_specs=[smem()] + [by_doc(segs // 2, width), by_doc(TEXT // 2, width)] * 2,
        out_specs=by_doc(slots, width),
        out_shape=sds(docs * slots, width),
        cost_estimate=cost(0, 8 * docs * slots * width),
        compiler_params=pltpu.CompilerParams(vmem_limit_bytes=VMEM_LIMIT),
        name="join_rows",
    )(place, ms, mt, ts, tt)


def final_kernel(docs, segs, all_rows, *refs):
    place = refs[0]
    mine, theirs = refs[1 : 1 + docs], refs[1 + docs : 1 + 2 * docs]
    roi, stats, out, sums = refs[1 + 2 * docs :]
    d = pl.program_id(0)
    c = place[0]
    half, half_seg = TEXT // 2, segs // 2

    @pl.when(d == 0)
    def _():
        sums[...] = jnp.zeros_like(sums)

    for i in range(docs):

        @pl.when(d == i)
        def _():
            for source, side in ((mine[i], c), (theirs[i], 1 - c)):
                at_seg, at_txt = side_rows(out, side, half, half_seg)
                at_seg[...] = source[:half_seg, :]
                at_txt[...] = source[half_seg:, :]

    g = out[TEXT:, :]
    sums[0:1, :] += colsum(g)
    sums[1:2, :] += colsum(g * batch_normed(roi[...], stats, all_rows))


def final_rows(all_rows, segs, place, mine, theirs, roi, stats):
    docs = len(mine)
    width = roi.shape[1]
    slots = TEXT + segs
    return pl.pallas_call(
        functools.partial(final_kernel, docs, segs, all_rows),
        grid=(docs,),
        in_specs=[smem()]
        + [whole((slots // 2, width))] * (2 * docs)
        + [by_doc(segs, width), whole(stats.shape)],
        out_specs=[by_doc(slots, width), pl.BlockSpec((8, width), lambda d: (0, 0))],
        out_shape=[sds(docs * slots, width), sds(8, width)],
        compiler_params=pltpu.CompilerParams(vmem_limit_bytes=VMEM_LIMIT),
        cost_estimate=cost(0, 20 * docs * slots * width),
        name="final_rows",
    )(place, *mine, *theirs, roi, stats)


def stats_kernel(roi, stats):
    x = roi[...]
    mean = jnp.mean(x, axis=0, keepdims=True)
    stats[0:1, :] = mean
    stats[1:2, :] = colsum((x - mean) * (x - mean))


def local_stats(roi):
    width = roi.shape[1]
    return pl.pallas_call(
        stats_kernel, out_shape=sds(2, width), name="local_stats"
    )(roi)


def swap(x, axis, bit):
    n = lax.axis_size(axis)
    return lax.ppermute(x, axis, [(i, i ^ bit) for i in range(n)])


def butterfly(x, merge):
    bit = 1
    while bit < lax.axis_size("dp"):
        x = merge(x, swap(x, "dp", bit), bit)
        bit *= 2
    return x


def ring(part, sign, cuts):
    n = lax.axis_size("dp")
    order = list(range(0, n, 2)) + list(range(n - 1, 0, -2))
    pairs = [(order[k], order[(k + sign) % n]) for k in range(n)]
    me = lax.axis_index("dp")
    place = sign * jnp.where(me % 2 == 0, me // 2, n - 1 - me // 2)
    size = part.shape[0] // n
    at = lambda k: ((place - k) % n) * size
    held = lax.dynamic_slice_in_dim(part, at(0), size, 0)
    for step in range(1, n):
        got = yield held, "dp", pairs
        held = got + lax.dynamic_slice_in_dim(part, at(step), size, 0)
    pieces = [held]
    for step in range(n - 1):
        held = yield held, "dp", pairs
        pieces.append(held)
    if size % 8 == 0:
        where = jnp.stack([at(k - 1) for k in range(n)]).astype(jnp.int32)
        return assemble(where, pieces, cuts)
    total = part
    for k, piece in enumerate(pieces):
        total = lax.dynamic_update_slice_in_dim(total, piece, at(k - 1), 0)
    return [total[sum(cuts[:i]) : sum(cuts[: i + 1])] for i in range(len(cuts))]


def assemble_kernel(count, where, *refs):
    outs, total = refs[count:-1], refs[-1]
    for k, piece in enumerate(refs[:count]):
        total[pl.ds(pl.multiple_of(where[k], 8), piece.shape[0]), :] = piece[...]
    at = 0
    for out in outs:
        out[...] = total[at : at + out.shape[0], :]
        at += out.shape[0]


def assemble(where, pieces, cuts):
    size, width = pieces[0].shape
    return pl.pallas_call(
        functools.partial(assemble_kernel, len(pieces)),
        in_specs=[smem()] + [pl.BlockSpec(memory_space=pltpu.VMEM)] * len(pieces),
        out_specs=[pl.BlockSpec(memory_space=pltpu.VMEM)] * len(cuts),
        out_shape=[sds(rows, width) for rows in cuts],
        scratch_shapes=[pltpu.VMEM((size * len(pieces), width), F32)],
        compiler_params=pltpu.CompilerParams(vmem_limit_bytes=VMEM_LIMIT),
        cost_estimate=cost(0, 8 * size * len(pieces) * width),
        name="assemble",
    )(where, *pieces)


def halving(part, turn):
    n = lax.axis_size("dp")
    bits = list(range(n.bit_length() - 1))
    bits = bits[turn:] + bits[:turn]
    me = lax.axis_index("dp")
    pairs = lambda bit: [(i, i ^ (1 << bit)) for i in range(n)]
    for bit in bits:
        upper = (me >> bit) % 2
        half = part.shape[0] // 2
        keep, give = (lax.dynamic_slice_in_dim(part, k * half, half, 0) for k in (upper, 1 - upper))
        part = keep + (yield give, "dp", pairs(bit))
    for bit in bits[::-1]:
        upper = (me >> bit) % 2 == 1
        other = yield part, "dp", pairs(bit)
        part = jnp.concatenate(
            [jnp.where(upper, other, part), jnp.where(upper, part, other)], axis=0
        )
    return part


def cube(x):
    n = lax.axis_size("dp")
    bit = 1
    while bit < n:
        x = x + (yield x, "dp", [(i, i ^ bit) for i in range(n)])
        bit *= 2
    return x


class Steps:
    def __init__(self):
        self.active, self.results = {}, {}

    def add(self, name, moves):
        self.active[name] = (moves, next(moves))

    def run(self, work=None, inputs=()):
        names = list(self.active)
        sends = [self.active[name][1][0] for name in names]
        sends, inputs = lax.optimization_barrier((sends, tuple(inputs)))
        got = [lax.ppermute(x, *self.active[name][1][1:]) for name, x in zip(names, sends)]
        done = work(*inputs) if work else ()
        got, done = lax.optimization_barrier((got, done))
        for name, x in zip(names, got):
            moves = self.active.pop(name)[0]
            try:
                self.active[name] = (moves, moves.send(x))
            except StopIteration as stop:
                self.results[name] = stop.value
        return done

    def finish(self):
        while self.active:
            self.run()


def per_device(
    hidden_in,
    roi,
    bn_gain,
    bn_bias,
    w_qkv,
    bias_qv,
    w_out,
    bias_out,
    ln1_gain,
    ln1_bias,
    w_in,
    bias_in,
    w_back,
    bias_back,
    ln2_gain,
    ln2_bias,
    pair_w,
    pair_bias,
    dir_w,
    text_len,
    owner_order,
    pair_index,
    cot_out,
    cot_logits,
):
    docs = text_len.shape[0]
    slots = hidden_in.shape[0] // docs
    width = hidden_in.shape[1]
    segs = slots - TEXT
    seg_rows = roi.shape[0]
    n_dp = lax.axis_size("dp")
    all_rows = seg_rows * n_dp
    half, half_seg = TEXT // 2, segs // 2
    m = lax.axis_index("mp")
    c = m % 2
    dp = lax.axis_index("dp")
    shifts = (dp % 2, dp // 2 % 2)
    place = jnp.stack([c, *shifts]).astype(jnp.int32)
    part = w_qkv.shape[2]
    from_sib = lambda x: swap(x, "mp", 1)
    from_x = lambda x: swap(x, "mp", 2)
    later = lambda w, after: lax.optimization_barrier((w, after))[0]

    def near(k, *arrays):
        parts = []
        for w in arrays:
            size = w.shape[0] // 2
            parts.append(lax.dynamic_slice_in_dim(w, shifts[k] * size, size, 0))
        return from_x(jnp.concatenate(parts, axis=0))

    second = jnp.arange(2, dtype=jnp.int32)[:, None] == 1

    def merge(one, two, count):
        gap = one[0:1] - two[0:1]
        both = one + two
        return jnp.where(second, both + gap * gap * (0.5 * seg_rows * count), 0.5 * both)

    own = (w_out, w_in, w_back)
    close_in = near(0, w_out, w_in)
    close_back = near(1, w_back)
    own_sib = tuple(from_sib(w) for w in own)
    bias_sib, bias_x = from_sib(bias_in), from_x(bias_in)
    bias_xsib = from_sib(bias_x)
    stats = butterfly(local_stats(roi), merge)
    stats, bias_rows = lax.optimization_barrier(
        (stats, (bias_in, bias_sib, bias_x, bias_xsib))
    )
    qkv, lse, both_seg, both_txt, x_seg, x_txt = attn_fwd(
        all_rows, place, text_len, hidden_in, roi, stats, bn_gain, bn_bias, w_qkv, bias_qv
    )

    close, own_sib, both_seg, both_txt = lax.optimization_barrier(
        ((close_in, close_back), own_sib, both_seg, both_txt)
    )
    far = (swap(close[0], "dp", 1), swap(close[1], "dp", 2))
    far_seg, far_txt = from_x(both_seg), from_x(both_txt)
    close_sib = tuple(from_sib(w) for w in close)
    both_sib = (from_sib(both_seg), from_sib(both_txt))
    far, far_seg, close_sib, both_sib = lax.optimization_barrier(
        (far, far_seg, close_sib, both_sib)
    )
    far_sib = tuple(from_sib(w) for w in far)
    weights = ((w_out, own_sib[0]),) + tuple(
        (own[1 + k], own_sib[1 + k], close[k], far[k], close_sib[k], far_sib[k]) for k in range(2)
    )
    ctx_seg = (both_seg, both_sib[0], far_seg, from_sib(far_seg))
    vec = (bias_out, ln1_gain, ln1_bias, bias_back, ln2_gain, ln2_bias)
    mine_rows = docs * (half + half_seg)
    txt_rows = docs * half
    seg = ffn(
        place, vec, bias_rows, weights, docs * half_seg, txt_rows, mine_rows, None,
        ctx=ctx_seg, xres=x_seg,
    )

    far_txt = later(far_txt, seg["out"])
    ctx_txt = (both_txt, both_sib[1], far_txt, from_sib(far_txt))

    txt = {name: seg[name] for name in ("h1", "act0", "act1")}
    txt_sums, gwo = [], []

    def text(doc, *first):
        done = ffn(
            place, vec, bias_rows, weights, half, 0, mine_rows, None,
            ctx=ctx_txt, xres=first[0], gout=cot_out, into=txt, start=doc, count=1,
        )
        txt_sums.append(done.pop("sums"))
        gwo.append(done.pop("gwo"))
        txt.update(done)

    share = width // lax.axis_size("mp")
    cols = lambda x, who: lax.dynamic_slice_in_dim(x, who * share, share, 1)
    mine, theirs = cols(seg["out"], m), from_sib(cols(seg["out"], m ^ 1))
    by_core = lambda a, b: (jnp.where(c == 0, a, b), jnp.where(c == 0, b, a))
    columns = jnp.stack(
        [p.reshape(docs, half_seg, share) for p in by_core(mine, theirs)], axis=1
    ).reshape(seg_rows, share)
    ordering = owner_order[0]
    swap_rows = lambda x: lax.all_to_all(x, "dp", split_axis=0, concat_axis=0, tiled=True)
    ordered, x_txt = lax.optimization_barrier((jnp.take(columns, ordering, axis=0), x_txt))
    received = swap_rows(ordered)
    text(0, x_txt)
    received, x_txt = lax.optimization_barrier((received, later(x_txt, txt_sums[0])))
    candidates = jnp.arange(seg_rows, dtype=jnp.int32)[None, :]
    pick_left = (pair_index[:, 0:1] == candidates).astype(F32)
    pick_right = (pair_index[:, 1:2] == candidates).astype(F32)
    sides = jnp.concatenate([product(pick_left, received), product(pick_right, received)], axis=1)
    pair_w2 = pair_w.reshape(2 * share, width)
    pair_part = product(sides, pair_w2)
    pair_part = pair_part + from_sib(pair_part)
    pairs_half = pair_part.shape[0] // 2
    piece = lax.dynamic_slice_in_dim(pair_part, c * pairs_half, pairs_half, 0)
    piece, x_txt = lax.optimization_barrier((piece, x_txt))
    other = from_x(piece)
    if docs > 1:
        text(1, x_txt)
    piece, x_txt = lax.optimization_barrier((piece + later(other, txt_sums[-1]), x_txt))
    pair_pre = jnp.concatenate(by_core(piece, from_sib(piece)), axis=0) + pair_bias
    root = 0.5 * (1.0 + lax.erf(pair_pre * ROOT_HALF))
    pair_act = pair_pre * root
    logits = product(pair_act, dir_w)
    grad_dir_w = product(cot_logits, pair_act, ((0,), (0,)))
    grad_pair_pre = product(cot_logits, dir_w, ((1,), (1,))) * (
        root + pair_pre * jnp.exp(-0.5 * pair_pre * pair_pre) * DENSITY
    )
    grad_pair_bias = jnp.sum(grad_pair_pre, axis=0)
    grad_pair_w = product(sides, grad_pair_pre, ((0,), (0,)))
    grad_sides = product(grad_pair_pre, pair_w2, ((1,), (1,)))
    grad_received = product(pick_left, grad_sides[:, :share], ((0,), (0,))) + product(
        pick_right, grad_sides[:, share:], ((0,), (0,))
    )
    grad_received, x_txt = lax.optimization_barrier((grad_received, x_txt))
    grad_sent = swap_rows(grad_received)
    for doc in range(2, docs):
        text(doc, x_txt)
    grad_sent = later(grad_sent, txt_sums[-1])
    back_order = jnp.zeros_like(ordering).at[ordering].set(jnp.arange(seg_rows, dtype=jnp.int32))
    grad_cols = jnp.take(grad_sent, back_order, axis=0).reshape(docs, 2, half_seg, share)
    rows_of = lambda who: lax.dynamic_index_in_dim(grad_cols, who, 1, keepdims=False).reshape(
        docs * half_seg, share
    )
    grad_mine, grad_theirs = rows_of(c), from_sib(rows_of(1 - c))
    chip_cols = jnp.concatenate(by_core(grad_mine, grad_theirs), axis=1)
    far_cols = from_x(chip_cols)
    low_x = m < 2
    grad_seg = jnp.concatenate(
        [jnp.where(low_x, chip_cols, far_cols), jnp.where(low_x, far_cols, chip_cols)], axis=1
    )
    cot_seg = lax.dynamic_slice_in_dim(
        cot_out.reshape(docs, slots, width), TEXT + c * half_seg, half_seg, 1
    ).reshape(docs * half_seg, width)
    output = join_rows(
        docs, segs, place, seg["out"], txt["out"],
        from_sib(seg["out"]), from_sib(later(txt["out"], grad_cols)),
    )
    grad_seg, output = lax.optimization_barrier((grad_seg, output))
    back = ffn(
        place, vec, bias_rows, weights, docs * half_seg, txt_rows, mine_rows,
        [seg[name] for name in ("n1", "f1", "n2", "f2", "slope")],
        ctx=ctx_seg, gout=cot_seg + grad_seg,
        into={name: txt[name] for name in ("gs", "gi0", "gi1", "gf")},
    )

    tall = ((0,), (0,))
    sib_back = from_sib(product(txt["act1"], back["gs"], tall))
    sib_in = from_sib(product(txt["h1"], back["gi1"], tall))
    grad_back_own = product(txt["act0"], back["gs"], tall) + sib_back
    grad_in_own = product(txt["h1"], back["gi0"], tall) + sib_in
    gf_txt, gf_seg = back["gf"][:txt_rows], back["gf"][txt_rows:]
    gwo = sum(gwo) + back["gwo"]
    grad_out_own = gwo[:part] + from_sib(gwo[part:])

    steps = Steps()
    steps.add("in_out", ring(jnp.concatenate([grad_in_own, grad_out_own], axis=0), 1, (width, part)))
    back_pair = jnp.concatenate([grad_back_own, grad_pair_w], axis=0)
    steps.add("back_pair", ring(back_pair, -1, (width, 2 * share)))
    mine = (back["gb"], txt["gb"])
    theirs = tuple(from_sib(g) for g in mine)
    w_sum = jnp.zeros((3 * part, width), F32)
    b_sum = jnp.zeros((1, 3 * part), F32)
    gx = []
    for doc in range(docs):

        def scores(b_sum, doc=doc):
            return attn_bwd(
                doc, place, text_len, qkv, lse, (both_seg, both_txt), mine, theirs, b_sum
            )

        def weights_of(gq, w_sum, doc=doc):
            return qkv_bwd(
                all_rows, doc, docs, place, hidden_in, roi, stats, bn_gain, bn_bias, w_qkv, gq, w_sum
            )

        gq, b_sum = steps.run(scores, (b_sum,))
        gx_mine, gx_theirs, w_sum = steps.run(weights_of, (gq, w_sum))
        chip_sum = gx_mine + from_sib(gx_theirs)
        gx.append((chip_sum, from_x(chip_sum)))
    cut = w_sum.shape[0] * 5 // 9
    qkv_steps = Steps()
    qkv_steps.add("qkv_low", halving(w_sum[:cut], 0))
    qkv_steps.add("qkv_high", halving(w_sum[cut:], 1))
    qkv_steps.finish()
    gh_mine, gh_theirs = [], []
    for doc in range(docs):
        first = jnp.concatenate(
            [gf_seg[doc * half_seg : (doc + 1) * half_seg], gf_txt[doc * half : (doc + 1) * half]],
            axis=0,
        )
        if doc:
            steps.run()
        (far,) = steps.run(lambda x: (x,), (gx[doc][1],))
        gh_mine.append(first + (gx[doc][0] + far))
        gh_theirs.append(from_sib(gh_mine[-1]))
    (gh_theirs[-1],) = steps.run(lambda x: (x,), (gh_theirs[-1],))
    grad_hidden, bn_sums = final_rows(all_rows, segs, place, gh_mine, gh_theirs, roi, stats)

    rows = sum(txt_sums) + back["sums"]
    rows = jnp.concatenate([rows[:6], rows[6:7]]) + from_sib(jnp.concatenate([rows[:6], rows[7:8]]))
    pad = lambda v: jnp.pad(v, (0, width - v.shape[0]))[None]
    vectors = jnp.concatenate(
        [
            rows,
            grad_pair_bias[None],
            grad_dir_w,
            pad(b_sum[0, :part]),
            pad(b_sum[0, 2 * part :]),
            bn_sums[0:2],
        ],
        axis=0,
    )
    steps.add("vectors", cube(vectors))
    steps.finish()
    steps.results.update(qkv_steps.results)
    vectors, in_out, back_pair, low, high = (
        steps.results[name] for name in ("vectors", "in_out", "back_pair", "qkv_low", "qkv_high")
    )
    sum_qkv = jnp.concatenate([low, high], axis=0)
    n_dirs = dir_w.shape[1]
    sum_dir_w = vectors[8 : 8 + n_dirs].T
    tail = vectors[8 + n_dirs :]
    sum_bias_qv = tail[0:2, :part]
    grad_bn_bias, grad_bn_gain = tail[2], tail[3]
    grad_roi_out = grad_hidden.reshape(docs, slots, width)[:, TEXT:].reshape(seg_rows, width)
    roi_factor = lax.rsqrt(stats[1] / all_rows + EPSILON)
    roi_normed = (roi - stats[0]) * roi_factor
    grad_roi = (
        bn_gain
        * roi_factor
        * (grad_roi_out - grad_bn_bias / all_rows - roi_normed * grad_bn_gain / all_rows)
    )
    return (
        output,
        logits,
        grad_hidden,
        grad_roi,
        grad_bn_gain,
        grad_bn_bias,
        jnp.transpose(sum_qkv.reshape(3, part, width), (0, 2, 1)),
        sum_bias_qv,
        in_out[1],
        vectors[5],
        vectors[3],
        vectors[4],
        in_out[0],
        vectors[6],
        back_pair[0],
        vectors[2],
        vectors[0],
        vectors[1],
        back_pair[1].reshape(2, share, width),
        vectors[7],
        sum_dir_w,
    )


def solution(mesh):
    placed = (
        P("dp", None),
        P("dp", None),
        P(),
        P(),
        P(None, None, "mp"),
        P(None, "mp"),
        P("mp", None),
        P(),
        P(),
        P(),
        P(None, "mp"),
        P("mp"),
        P("mp", None),
        P(),
        P(),
        P(),
        P(None, "mp", None),
        P(),
        P(),
        P("dp"),
        P("dp", None),
        P("dp", None),
        P("dp", None),
        P("dp", None),
    )
    return jax.shard_map(
        per_device,
        mesh=mesh,
        in_specs=placed,
        out_specs=(
            P("dp", None),
            P("dp", None),
            P("dp", None),
            P("dp", None),
            P(),
            P(),
            P(None, None, "mp"),
            P(None, "mp"),
            P("mp", None),
            P(),
            P(),
            P(),
            P(None, "mp"),
            P("mp"),
            P("mp", None),
            P(),
            P(),
            P(),
            P(None, "mp", None),
            P(),
            P(),
        ),
        check_vma=False,
    )
```

```python
import functools

import jax
import jax.numpy as jnp
from jax import lax
from jax.experimental import pallas as pl
from jax.experimental.pallas import tpu as pltpu
from jax.sharding import PartitionSpec as P

HEAD_DIM = 64
TEXT = 512
EPSILON = 1e-05
NEGATIVE = -1e30
ROOT_HALF = 0.7071067811865476
DENSITY = 0.3989422804014327
HIGH = lax.Precision.HIGH
QUERY_STEP = 256
VMEM_LIMIT = 60 << 20
F32 = jnp.float32
BF16 = jnp.bfloat16


def product(operand, other, dims=((1,), (0,))):
    return lax.dot_general(
        operand, other, (dims, ((), ())), precision=HIGH, preferred_element_type=F32
    )


def halves(x):
    hi = x.astype(BF16)
    return hi, (x - hi.astype(F32)).astype(BF16)


def dot(a, b, dims=((1,), (0,))):
    return lax.dot_general(a, b, (dims, ((), ())), preferred_element_type=F32)


ROWS_BY_ROWS = ((1,), (1,))
COLS_BY_COLS = ((0,), (0,))


def dot3_apart(a, b, dims=((1,), (0,))):
    return dot(a[0], b[0], dims) + dot(a[1], b[0], dims) + dot(a[0], b[1], dims)


def dot3(a, b, dims=((1,), (0,))):
    ka, kb = dims[0][0], dims[1][0]
    return dot(jnp.concatenate([a[0], a[1], a[0]], ka), jnp.concatenate([b[0], b[0], b[1]], kb), dims)


def gelu_parts(v):
    phi = 0.5 + 0.5 * lax.erf(v * ROOT_HALF)
    return v * phi, phi + v * jnp.exp(-0.5 * v * v) * DENSITY


def normalize_rows(y):
    center = y - jnp.mean(y, axis=-1, keepdims=True)
    factor = lax.rsqrt(jnp.mean(center * center, axis=-1, keepdims=True) + EPSILON)
    return center * factor, factor


def normalize_rows_back(upstream, normed, factor):
    return factor * (
        upstream
        - jnp.mean(upstream, axis=-1, keepdims=True)
        - normed * jnp.mean(upstream * normed, axis=-1, keepdims=True)
    )


def colsum(x):
    return jnp.sum(x, axis=0, keepdims=True)


def lane_is(rows, width, lane):
    return lax.broadcasted_iota(jnp.int32, (rows, width), 1) == lane


def cost(products, moved):
    return pl.CostEstimate(flops=6 * products, bytes_accessed=moved, transcendentals=0)


def smem():
    return pl.BlockSpec(memory_space=pltpu.SMEM)


def whole(shape):
    return pl.BlockSpec(shape, lambda *_: (0,) * len(shape), pipeline_mode=pl.Buffered(1))


def sds(*shape):
    return jax.ShapeDtypeStruct(shape, F32)


def batch_normed(roi, stats, rows):
    return (roi - stats[0:1]) * lax.rsqrt(stats[1:2] / rows + EPSILON)


def segment_rows(roi, stats, rows, gain, shift):
    return batch_normed(roi[...], stats, rows) * gain[...][None, :] + shift[...][None, :]


def side_rows(ref, side, half, half_seg):
    return (
        ref.at[pl.ds(pl.multiple_of(TEXT + side * half_seg, half_seg), half_seg)],
        ref.at[pl.ds(pl.multiple_of(side * half, half), half)],
    )


def split_qkv(w, w_hi, w_lo):
    part = w.shape[2]
    for i in range(3):
        lanes = slice(i * part, (i + 1) * part)
        w_hi[:, lanes], w_lo[:, lanes] = halves(w[i])


def attn_fwd_kernel(all_rows, *refs):
    place, lens, hid, roi, stats, gain, shift, w, bias = refs[:9]
    qkv, lse, both_seg, both_txt, xm_seg, xm_txt = refs[9:15]
    w_hi, w_lo, x_seg, ctx, ctx_t = refs[15:]
    doc = pl.program_id(0)
    c = place[0]
    width = w.shape[2]
    heads = width // HEAD_DIM
    slots = hid.shape[0]
    half, half_seg = TEXT // 2, (slots - TEXT) // 2

    @pl.when(doc == 0)
    def _():
        split_qkv(w, w_hi, w_lo)

    x_seg[...] = hid[TEXT:, :] + segment_rows(roi, stats, all_rows, gain, shift)
    wide = (w_hi[...], w_lo[...])
    added = jnp.concatenate([bias[0:1, :], jnp.zeros((1, width), F32), bias[1:2, :]], axis=1)
    for start in (0, half):
        qkv[start : start + half, :] = dot3(halves(hid[start : start + half, :]), wide) + added
    qkv[TEXT:, :] = dot3(halves(x_seg[...]), wide) + added

    position = lax.broadcasted_iota(jnp.int32, (slots, HEAD_DIM), 0)
    first = lane_is(slots, HEAD_DIM, 0)
    dead = (position >= lens[doc]) & (position < TEXT)
    key_extra = jnp.where(first & dead, NEGATIVE, 0.0).astype(BF16)
    ones = jnp.where(first, 1.0, 0.0).astype(BF16)
    one_rows = jnp.ones((16, slots), BF16)
    values = jnp.transpose(qkv[:, 2 * width :])
    for h in range(heads):
        at = h * HEAD_DIM
        q_hi, q_lo = halves(qkv[:, at : at + HEAD_DIM] * HEAD_DIM**-0.5)
        k_hi, k_lo = halves(qkv[:, width + at : width + at + HEAD_DIM])
        v_two = jnp.concatenate([*halves(values[at : at + HEAD_DIM, :]), one_rows], axis=0)
        q_pack = jnp.concatenate([q_hi, q_lo, q_hi, ones], axis=1)
        k_pack = jnp.concatenate([k_hi, k_hi, k_lo, key_extra], axis=1)
        for start in range(0, slots, QUERY_STEP):
            cols = slice(start, min(slots, start + QUERY_STEP))
            scores = dot(k_pack, q_pack[cols], ROWS_BY_ROWS)
            top = jnp.max(scores, axis=0, keepdims=True)
            p_hi, p_lo = halves(jnp.exp(scores - top))
            mixed = dot(v_two, p_hi) + dot(v_two, p_lo)
            total = mixed[2 * HEAD_DIM : 2 * HEAD_DIM + 1]
            ctx_t[at : at + HEAD_DIM, cols] = (
                mixed[:HEAD_DIM] + mixed[HEAD_DIM : 2 * HEAD_DIM]
            ) / total
            lse[h : h + 1, cols] = top + jnp.log(total)
    ctx[...] = jnp.transpose(ctx_t[...])
    for lanes, side in ((slice(0, width), c), (slice(width, 2 * width), 1 - c)):
        at_seg, at_txt = side_rows(ctx, side, half, half_seg)
        both_seg[:, lanes] = at_seg[...]
        both_txt[:, lanes] = at_txt[...]
    xm_seg[...] = x_seg[pl.ds(pl.multiple_of(c * half_seg, half_seg), half_seg), :]
    xm_txt[...] = hid[pl.ds(pl.multiple_of(c * half, half), half), :]


def by_doc(rows, lanes):
    return pl.BlockSpec((rows, lanes), lambda d: (d, 0))


def attn_fwd(all_rows, place, lens, hidden, roi, stats, gain, shift, w, bias):
    docs = lens.shape[0]
    slots, width = hidden.shape[0] // docs, hidden.shape[1]
    segs = slots - TEXT
    part = w.shape[2]
    out_rows = [
        (slots, 3 * part),
        (8, slots),
        (segs // 2, 2 * part),
        (TEXT // 2, 2 * part),
        (segs // 2, width),
        (TEXT // 2, width),
    ]
    return pl.pallas_call(
        functools.partial(attn_fwd_kernel, all_rows),
        grid=(docs,),
        in_specs=[smem(), smem(), by_doc(slots, width), by_doc(segs, width)]
        + [whole(a.shape) for a in (stats, gain, shift, w, bias)],
        out_specs=[by_doc(*s) for s in out_rows],
        out_shape=[sds(docs * s[0], s[1]) for s in out_rows],
        scratch_shapes=[
            pltpu.VMEM((width, 3 * part), BF16),
            pltpu.VMEM((width, 3 * part), BF16),
            pltpu.VMEM((segs, width), F32),
            pltpu.VMEM((slots, part), F32),
            pltpu.VMEM((part, slots), F32),
        ],
        compiler_params=pltpu.CompilerParams(vmem_limit_bytes=VMEM_LIMIT),
        cost_estimate=cost(docs * slots, slots),
        name="attn_fwd",
    )(place, lens, hidden, roi, stats, gain, shift, w, bias)


def attn_bwd_kernel(doc, *refs):
    place, lens, qkv, lse, ctx_seg, ctx_txt, gm_seg, gm_txt, gt_seg, gt_txt, b_sum = refs[:11]
    gq, b_out, o_all, g_all, gq_t = refs[11:]
    c = place[0]
    width = qkv.shape[1] // 3
    heads = width // HEAD_DIM
    slots = qkv.shape[0]
    half, half_seg = TEXT // 2, (slots - TEXT) // 2
    near, far = slice(0, width), slice(width, 2 * width)
    for dst, mine, theirs in (
        (o_all, (ctx_seg, ctx_txt), (ctx_seg, ctx_txt)),
        (g_all, (gm_seg, gm_txt), (gt_seg, gt_txt)),
    ):
        for side, sources, lanes in ((c, mine, near), (1 - c, theirs, far)):
            for place_at, source in zip(side_rows(dst, side, half, half_seg), sources):
                place_at[...] = source[:, lanes]

    position = lax.broadcasted_iota(jnp.int32, (slots, HEAD_DIM), 0)
    first = lane_is(slots, HEAD_DIM, 0)
    dead = (position >= lens[doc]) & (position < TEXT)
    key_extra = jnp.where(first & dead, NEGATIVE, 0.0).astype(BF16)
    ones = jnp.where(first, 1.0, 0.0).astype(BF16)
    none = jnp.zeros_like(ones)
    head_of = lax.broadcasted_iota(jnp.int32, (16, width), 1) // HEAD_DIM
    pick_head = jnp.where(
        head_of == lax.broadcasted_iota(jnp.int32, (16, width), 0), 1.0, 0.0
    ).astype(BF16)
    scale = HEAD_DIM**-0.5
    product_hi, product_lo = halves(g_all[...] * o_all[...])
    inner = dot(pick_head, product_hi, ROWS_BY_ROWS) + dot(pick_head, product_lo, ROWS_BY_ROWS)
    keys_t = jnp.transpose(qkv[:, width : 2 * width])
    for h in range(heads):
        at = h * HEAD_DIM
        q_hi, q_lo = halves(qkv[:, at : at + HEAD_DIM] * scale)
        k_hi, k_lo = halves(qkv[:, width + at : width + at + HEAD_DIM])
        v_hi, v_lo = halves(qkv[:, 2 * width + at : 2 * width + at + HEAD_DIM])
        g_hi, g_lo = halves(g_all[:, at : at + HEAD_DIM])
        k_rows = jnp.concatenate(halves(keys_t[at : at + HEAD_DIM, :]), axis=0)
        q_pack = jnp.concatenate([q_hi, q_lo, q_hi, ones], axis=1)
        k_pack = jnp.concatenate([k_hi, k_hi, k_lo, key_extra], axis=1)
        g_pack = jnp.concatenate([g_hi, g_lo, g_hi, none], axis=1)
        v_pack = jnp.concatenate([v_hi, v_hi, v_lo, none], axis=1)
        q_two = jnp.concatenate([q_hi, q_lo], axis=1)
        g_two = jnp.concatenate([g_hi, g_lo], axis=1)
        weights = jnp.exp(dot(k_pack, q_pack, ROWS_BY_ROWS) - lse[h : h + 1, :])
        grads = weights * (dot(v_pack, g_pack, ROWS_BY_ROWS) - inner[h : h + 1, :])
        w_two = halves(weights)
        s_two = halves(grads)
        grad_v = dot(w_two[0], g_two) + dot(w_two[1], g_two)
        grad_k = dot(s_two[0], q_two) + dot(s_two[1], q_two)
        grad_q = dot(k_rows, s_two[0]) + dot(k_rows, s_two[1])
        gq[:, width + at : width + at + HEAD_DIM] = grad_k[:, :HEAD_DIM] + grad_k[:, HEAD_DIM:]
        gq[:, 2 * width + at : 2 * width + at + HEAD_DIM] = (
            grad_v[:, :HEAD_DIM] + grad_v[:, HEAD_DIM:]
        )
        gq_t[at : at + HEAD_DIM, :] = (grad_q[:HEAD_DIM] + grad_q[HEAD_DIM:]) * scale
    gq[:, :width] = jnp.transpose(gq_t[...])
    b_out[...] = b_sum[...] + colsum(gq[...])


def attn_bwd(doc, place, lens, qkv, lse, ctx, mine, theirs, b_sum):
    docs = lens.shape[0]
    slots, cols = qkv.shape[0] // docs, qkv.shape[1]
    segs = slots - TEXT
    part = cols // 3
    of_doc = lambda rows, lanes: pl.BlockSpec((rows, lanes), lambda i: (doc, 0))
    rows = [of_doc(segs // 2, 2 * part), of_doc(TEXT // 2, 2 * part)]
    return pl.pallas_call(
        functools.partial(attn_bwd_kernel, doc),
        grid=(1,),
        in_specs=[smem(), smem(), of_doc(slots, cols), of_doc(8, slots)] + rows * 3 + [whole((1, cols))],
        out_specs=[whole((slots, cols)), whole((1, cols))],
        out_shape=[sds(slots, cols), sds(1, cols)],
        scratch_shapes=[
            pltpu.VMEM((slots, part), F32),
            pltpu.VMEM((slots, part), F32),
            pltpu.VMEM((part, slots), F32),
        ],
        compiler_params=pltpu.CompilerParams(vmem_limit_bytes=32 << 20),
        cost_estimate=cost(slots * part * 16 * slots, 8 * slots * cols),
        name="attn_bwd",
    )(place, lens, qkv, lse, *ctx, *mine, *theirs, b_sum)


def qkv_bwd_kernel(all_rows, *refs):
    place, hid, roi, stats, gain, shift, w, gq, w_sum = refs[:9]
    gx_mine, gx_theirs, w_out = refs[9:12]
    w_hi, w_lo, x_all, gx = refs[12:]
    c = place[0]
    slots = hid.shape[0]
    half, half_seg = TEXT // 2, (slots - TEXT) // 2
    split_qkv(w, w_hi, w_lo)
    x_all[:TEXT, :] = hid[:TEXT, :]
    x_all[TEXT:, :] = hid[TEXT:, :] + segment_rows(roi, stats, all_rows, gain, shift)
    wide = (w_hi[...], w_lo[...])
    for start in range(0, slots, 320):
        rows = slice(start, min(slots, start + 320))
        gx[rows, :] = dot3_apart(halves(gq[rows, :]), wide, ROWS_BY_ROWS)
    w_out[...] = w_sum[...] + dot3_apart(halves(gq[...]), halves(x_all[...]), COLS_BY_COLS)
    for dst, side in ((gx_mine, c), (gx_theirs, 1 - c)):
        at_seg, at_txt = side_rows(gx, side, half, half_seg)
        dst[:half_seg, :] = at_seg[...]
        dst[half_seg:, :] = at_txt[...]


def qkv_bwd(all_rows, doc, docs, place, hidden, roi, stats, gain, shift, w, gq, w_sum):
    slots, width = hidden.shape[0] // docs, hidden.shape[1]
    cols = gq.shape[1]
    of_doc = lambda rows, lanes: pl.BlockSpec((rows, lanes), lambda i: (doc, 0))
    return pl.pallas_call(
        functools.partial(qkv_bwd_kernel, all_rows),
        grid=(1,),
        in_specs=[smem(), of_doc(slots, width), of_doc(slots - TEXT, width)]
        + [whole(a.shape) for a in (stats, gain, shift, w, gq, w_sum)],
        out_specs=[whole((slots // 2, width)), whole((slots // 2, width)), whole((cols, width))],
        out_shape=[sds(slots // 2, width), sds(slots // 2, width), sds(cols, width)],
        scratch_shapes=[
            pltpu.VMEM((width, cols), BF16),
            pltpu.VMEM((width, cols), BF16),
            pltpu.VMEM((slots, width), F32),
            pltpu.VMEM((slots, width), F32),
        ],
        compiler_params=pltpu.CompilerParams(vmem_limit_bytes=32 << 20),
        cost_estimate=cost(slots * cols * 2 * width, 12 * slots * width),
        name="qkv_bwd",
    )(place, hidden, roi, stats, gain, shift, w, gq, w_sum)


VECTORS = ("bias_out", "ln1_gain", "ln1_bias", "bias_back", "ln2_gain", "ln2_bias")
TILES = 4
PIECE_SHARDS = (0, 1, 2, 2, 3, 3)


def piece_place(i, rows, shift):
    if i < 2:
        return 0
    half = rows // 2
    return pl.multiple_of((shift if i % 2 == 0 else 1 - shift) * half, half)


def ffn_kernel(forward, backward, names, *refs):
    ref = dict(zip(names, refs))
    place, stage, sems = ref["place"], ref["stage"], ref["sems"]
    wts, acc, a_hi, a_lo = ref["wts"], ref["acc"], ref["a_hi"], ref["a_lo"]
    wo = ref["wo"]
    resident = wts.shape[0] == TILES
    c = place[0]
    shifts = {"wo": place[1], "wi": place[1], "wb": place[2]}
    width = acc.shape[1]
    rows = acc.shape[0]
    part = wo.shape[1] // 4
    row = lambda name: ref[name][...][None, :]

    def two_shards(one, two):
        lane = lax.broadcasted_iota(jnp.int32, (rows, 2 * part), 1)
        return jnp.where(lane < part, ref[one][...], ref[two][...])

    def copies(tile):
        found = []
        for i in range(6):
            if PIECE_SHARDS[i] == tile:
                for k, kind in enumerate(("wi", "wb")):
                    piece = ref[f"{kind}{i}"]
                    if kind == "wi" and i > 1:
                        piece = piece.at[pl.ds(part // 2, width // 2)]
                    at = pl.ds(piece_place(i, width, shifts[kind]), piece.shape[0])
                    where = stage.at[tile % 2, k, at, :]
                    found.append(
                        pltpu.make_async_copy(piece, where, sems.at[tile % 2, len(found)])
                    )
        return found

    def start_tile(tile):
        for copy in copies(tile):
            copy.start()

    slot_of = lambda tile: tile if resident else tile % 2

    def ready(tile):
        for copy in copies(tile):
            copy.wait()
        slot = slot_of(tile)
        wts[slot, 0], wts[slot, 1] = halves(stage[tile % 2, 0])
        wts[slot, 2], wts[slot, 3] = halves(stage[tile % 2, 1])
        if tile + 2 < TILES:
            start_tile(tile + 2)

    def load_wo(count):
        for i in range(count):
            at = PIECE_SHARDS[i] * part + piece_place(i, part, shifts["wo"])
            where = pl.ds(at, ref[f"wo{i}"].shape[0])
            wo[0, where, :], wo[1, where, :] = halves(ref[f"wo{i}"][...])

    def run_forward(loading):
        y = ref["xres"][...] + row("bias_out")
        for one, two, at in (
            ("ctx_own", "ctx_sib", slice(0, 2 * part)),
            ("ctx_far", "ctx_farsib", slice(2 * part, 4 * part)),
        ):
            y = y + dot3(halves(two_shards(one, two)), (wo[0, at, :], wo[1, at, :]))
        normed, factor = normalize_rows(y)
        ref["n1"][...] = normed
        ref["f1"][...] = jnp.broadcast_to(factor, (rows, 128))
        h = normed * row("ln1_gain") + row("ln1_bias")
        ref["h1"][...] = h
        a_hi[...], a_lo[...] = halves(h)
        acc[...] = h + row("bias_back")
        for t in range(TILES):
            if loading and t == 0:
                ready(0)
            if loading and t + 1 < TILES:
                ready(t + 1)
            slot = slot_of(t)
            pre = dot3((a_hi[...], a_lo[...]), (wts[slot, 0], wts[slot, 1]))
            value, rise = gelu_parts(pre + row(f"bias_in{t}"))
            ref["slope"][t] = rise
            if t < 2:
                ref[f"act{t}"][...] = value
            acc[...] += dot3(halves(value), (wts[slot, 2], wts[slot, 3]))
        normed, factor = normalize_rows(acc[...])
        ref["n2"][...] = normed
        ref["f2"][...] = jnp.broadcast_to(factor, (rows, 128))
        ref["out"][...] = normed * row("ln2_gain") + row("ln2_bias")

    def run_backward(loading):
        sums = ref["sums"]
        if forward:
            g = ref["gout"][pl.ds(pl.multiple_of(c * rows, rows), rows), :]
        else:
            g = ref["gout"][...]
        n2 = ref["n2"][...]
        sums[0:1, :] += colsum(g * n2)
        sums[1:2, :] += colsum(g)
        back = normalize_rows_back(g * row("ln2_gain"), n2, ref["f2"][:, 0:1])
        sums[2:3, :] += colsum(back)
        ref["gs"][...] = back
        acc[...] = back
        a_hi[...], a_lo[...] = halves(back)
        for t in range(TILES):
            if loading and t == 0:
                ready(0)
            if loading and t + 1 < TILES:
                ready(t + 1)
            slot = slot_of(t)
            grad = dot3((a_hi[...], a_lo[...]), (wts[slot, 2], wts[slot, 3]), ROWS_BY_ROWS)
            grad = grad * ref["slope"][t]
            if t < 2:
                ref[f"gi{t}"][...] = grad
                sums[6 + t : 7 + t, :] += colsum(grad)
            acc[...] += dot3(halves(grad), (wts[slot, 0], wts[slot, 1]), ROWS_BY_ROWS)
        g, n1 = acc[...], ref["n1"][...]
        sums[3:4, :] += colsum(g * n1)
        sums[4:5, :] += colsum(g)
        back = normalize_rows_back(g * row("ln1_gain"), n1, ref["f1"][:, 0:1])
        sums[5:6, :] += colsum(back)
        ref["gf"][...] = back
        two = halves(back)
        at = slice(0, 2 * part)
        ref["gb"][...] = dot3(two, (wo[0, at, :], wo[1, at, :]), ROWS_BY_ROWS)
        ref["gwo"][...] = dot3_apart(halves(two_shards("ctx_own", "ctx_sib")), two, COLS_BY_COLS)

    def begin():
        start_tile(0)
        start_tile(1)
        load_wo(6 if forward else 2)
        if backward:
            ref["sums"][...] = jnp.zeros_like(ref["sums"])

    if forward and backward:

        @pl.when(pl.program_id(0) == 0)
        def _():
            begin()
            run_forward(True)
            run_backward(False)

        @pl.when(pl.program_id(0) > 0)
        def _():
            run_forward(False)
            run_backward(False)
    else:
        begin()
        if forward:
            run_forward(True)
        if backward:
            run_backward(True)


def ffn(place, vectors, bias_in, weights, block, offset, total, saved, *, ctx=None, xres=None, gout=None, into=None, start=0, count=None):
    forward, backward = xres is not None, gout is not None
    both = forward and backward
    width = vectors[0].shape[0]
    rows = ctx[0].shape[0]
    blocks = rows // block
    part = width // 4
    w_out, w_in, w_back = weights
    first = offset // block + start
    local = lambda lanes: pl.BlockSpec((block, lanes), lambda r: (start + r, 0))
    shared = pl.BlockSpec((block, width), lambda r: (first + r, 0))
    anywhere = pl.BlockSpec(memory_space=pltpu.HBM)
    names, specs, args = [], [], []

    def take(name, spec, arg):
        names.append(name)
        specs.append(spec)
        args.append(arg)

    take("place", smem(), place)
    for name, a in zip(VECTORS, vectors):
        take(name, whole(a.shape), a)
    for name, a in zip(("ctx_own", "ctx_sib", "ctx_far", "ctx_farsib"), ctx):
        take(name, local(a.shape[1]), a)
    if forward:
        for t in range(TILES):
            take(f"bias_in{t}", whole(bias_in[t].shape), bias_in[t])
        take("xres", local(width), xres)
    if backward:
        if both:
            slots = gout.shape[0] // blocks
            take("gout", pl.BlockSpec((slots, width), lambda r: (start + r, 0)), gout)
        else:
            take("gout", local(width), gout)
    kept = (
        ("n1", (block, width)),
        ("f1", (block, 128)),
        ("n2", (block, width)),
        ("f2", (block, 128)),
        ("slope", (TILES, block, width)),
    )
    if backward and not forward:
        for (name, shape), a in zip(kept, saved):
            take(name, whole(shape), a)
    for i in range(6 if forward else 2):
        piece, height = (w_out[i], part) if i < 2 else (w_in[i], part // 2)
        take(f"wo{i}", whole((height, width)), piece)
    for i in range(6):
        take(f"wi{i}", anywhere, w_in[i])
        take(f"wb{i}", anywhere, w_back[i])
    outs = []
    if forward:
        outs += [("out", local(width), sds(rows, width))]
        outs += [(n, shared, sds(total, width)) for n in ("h1", "act0", "act1")]
        if not backward:
            outs += [(name, whole(shape), sds(*shape)) for name, shape in kept]
    if backward:
        outs += [(n, shared, sds(total, width)) for n in ("gs", "gi0", "gi1", "gf")]
        outs += [("gb", local(2 * part), sds(rows, 2 * part))]
        outs += [("gwo", whole((2 * part, width)), sds(2 * part, width))]
        outs += [("sums", whole((8, width)), sds(8, width))]
    aliases = {}
    if into:
        for k, (name, _, _) in enumerate(outs):
            if name in into:
                aliases[len(args)] = k
                take(name + "_into", anywhere, into[name])
    scratch = [
        ("stage", pltpu.VMEM((2, 2, width, width), F32)),
        ("sems", pltpu.SemaphoreType.DMA((2, 4))),
        ("wts", pltpu.VMEM((TILES if both else 2, 4, width, width), BF16)),
        ("wo", pltpu.VMEM((2, width, width), BF16)),
        ("acc", pltpu.VMEM((block, width), F32)),
        ("a_hi", pltpu.VMEM((block, width), BF16)),
        ("a_lo", pltpu.VMEM((block, width), BF16)),
    ]
    if both:
        scratch += [(name, pltpu.VMEM(shape, F32)) for name, shape in kept]
    all_names = names + [o[0] for o in outs] + [s[0] for s in scratch]
    passes = (3 if both else 1) * 8
    result = pl.pallas_call(
        functools.partial(ffn_kernel, forward, backward, all_names),
        grid=(count or blocks,),
        in_specs=specs,
        out_specs=[o[1] for o in outs],
        out_shape=[o[2] for o in outs],
        scratch_shapes=[s[1] for s in scratch],
        input_output_aliases=aliases,
        compiler_params=pltpu.CompilerParams(vmem_limit_bytes=VMEM_LIMIT),
        cost_estimate=cost(
            (count or blocks) * block * width * width * (16 if both else 8) + 4 * width**3,
            60 * block * width,
        ),
        name="ffn_" + "fwd" * forward + "bwd" * backward,
    )(*args)
    return {o[0]: r for o, r in zip(outs, result)}


def join_kernel(docs, segs, place, ms, mt, ts, tt, out):
    c = place[0]
    half, half_seg = TEXT // 2, segs // 2
    for seg, txt, side in ((ms, mt, c), (ts, tt, 1 - c)):
        at_seg, at_txt = side_rows(out, side, half, half_seg)
        at_seg[...] = seg[...]
        at_txt[...] = txt[...]


def join_rows(docs, segs, place, ms, mt, ts, tt):
    width = ms.shape[1]
    slots = TEXT + segs
    return pl.pallas_call(
        functools.partial(join_kernel, docs, segs),
        grid=(docs,),
        in_specs=[smem()] + [by_doc(segs // 2, width), by_doc(TEXT // 2, width)] * 2,
        out_specs=by_doc(slots, width),
        out_shape=sds(docs * slots, width),
        cost_estimate=cost(0, 8 * docs * slots * width),
        compiler_params=pltpu.CompilerParams(vmem_limit_bytes=VMEM_LIMIT),
        name="join_rows",
    )(place, ms, mt, ts, tt)


def final_kernel(docs, segs, all_rows, *refs):
    place = refs[0]
    mine, theirs = refs[1 : 1 + docs], refs[1 + docs : 1 + 2 * docs]
    roi, stats, out, sums = refs[1 + 2 * docs :]
    d = pl.program_id(0)
    c = place[0]
    half, half_seg = TEXT // 2, segs // 2

    @pl.when(d == 0)
    def _():
        sums[...] = jnp.zeros_like(sums)

    for i in range(docs):

        @pl.when(d == i)
        def _():
            for source, side in ((mine[i], c), (theirs[i], 1 - c)):
                at_seg, at_txt = side_rows(out, side, half, half_seg)
                at_seg[...] = source[:half_seg, :]
                at_txt[...] = source[half_seg:, :]

    g = out[TEXT:, :]
    sums[0:1, :] += colsum(g)
    sums[1:2, :] += colsum(g * batch_normed(roi[...], stats, all_rows))


def final_rows(all_rows, segs, place, mine, theirs, roi, stats):
    docs = len(mine)
    width = roi.shape[1]
    slots = TEXT + segs
    return pl.pallas_call(
        functools.partial(final_kernel, docs, segs, all_rows),
        grid=(docs,),
        in_specs=[smem()]
        + [whole((slots // 2, width))] * (2 * docs)
        + [by_doc(segs, width), whole(stats.shape)],
        out_specs=[by_doc(slots, width), pl.BlockSpec((8, width), lambda d: (0, 0))],
        out_shape=[sds(docs * slots, width), sds(8, width)],
        compiler_params=pltpu.CompilerParams(vmem_limit_bytes=VMEM_LIMIT),
        cost_estimate=cost(0, 20 * docs * slots * width),
        name="final_rows",
    )(place, *mine, *theirs, roi, stats)


def stats_kernel(roi, stats):
    x = roi[...]
    mean = jnp.mean(x, axis=0, keepdims=True)
    stats[0:1, :] = mean
    stats[1:2, :] = colsum((x - mean) * (x - mean))


def local_stats(roi):
    width = roi.shape[1]
    return pl.pallas_call(
        stats_kernel, out_shape=sds(2, width), name="local_stats"
    )(roi)


def swap(x, axis, bit):
    n = lax.axis_size(axis)
    return lax.ppermute(x, axis, [(i, i ^ bit) for i in range(n)])


def butterfly(x, merge):
    bit = 1
    while bit < lax.axis_size("dp"):
        x = merge(x, swap(x, "dp", bit), bit)
        bit *= 2
    return x


def ring(part, sign, cuts):
    n = lax.axis_size("dp")
    order = list(range(0, n, 2)) + list(range(n - 1, 0, -2))
    pairs = [(order[k], order[(k + sign) % n]) for k in range(n)]
    me = lax.axis_index("dp")
    place = sign * jnp.where(me % 2 == 0, me // 2, n - 1 - me // 2)
    size = part.shape[0] // n
    at = lambda k: ((place - k) % n) * size
    held = lax.dynamic_slice_in_dim(part, at(0), size, 0)
    for step in range(1, n):
        got = yield held, "dp", pairs
        held = got + lax.dynamic_slice_in_dim(part, at(step), size, 0)
    pieces = [held]
    for step in range(n - 1):
        held = yield held, "dp", pairs
        pieces.append(held)
    if size % 8 == 0:
        where = jnp.stack([at(k - 1) for k in range(n)]).astype(jnp.int32)
        return assemble(where, pieces, cuts)
    total = part
    for k, piece in enumerate(pieces):
        total = lax.dynamic_update_slice_in_dim(total, piece, at(k - 1), 0)
    return [total[sum(cuts[:i]) : sum(cuts[: i + 1])] for i in range(len(cuts))]


def assemble_kernel(count, where, *refs):
    outs, total = refs[count:-1], refs[-1]
    for k, piece in enumerate(refs[:count]):
        total[pl.ds(pl.multiple_of(where[k], 8), piece.shape[0]), :] = piece[...]
    at = 0
    for out in outs:
        out[...] = total[at : at + out.shape[0], :]
        at += out.shape[0]


def assemble(where, pieces, cuts):
    size, width = pieces[0].shape
    return pl.pallas_call(
        functools.partial(assemble_kernel, len(pieces)),
        in_specs=[smem()] + [pl.BlockSpec(memory_space=pltpu.VMEM)] * len(pieces),
        out_specs=[pl.BlockSpec(memory_space=pltpu.VMEM)] * len(cuts),
        out_shape=[sds(rows, width) for rows in cuts],
        scratch_shapes=[pltpu.VMEM((size * len(pieces), width), F32)],
        compiler_params=pltpu.CompilerParams(vmem_limit_bytes=VMEM_LIMIT),
        cost_estimate=cost(0, 8 * size * len(pieces) * width),
        name="assemble",
    )(where, *pieces)


def halving(part, turn):
    n = lax.axis_size("dp")
    bits = list(range(n.bit_length() - 1))
    bits = bits[turn:] + bits[:turn]
    me = lax.axis_index("dp")
    pairs = lambda bit: [(i, i ^ (1 << bit)) for i in range(n)]
    for bit in bits:
        upper = (me >> bit) % 2
        half = part.shape[0] // 2
        keep, give = (lax.dynamic_slice_in_dim(part, k * half, half, 0) for k in (upper, 1 - upper))
        part = keep + (yield give, "dp", pairs(bit))
    for bit in bits[::-1]:
        upper = (me >> bit) % 2 == 1
        other = yield part, "dp", pairs(bit)
        part = jnp.concatenate(
            [jnp.where(upper, other, part), jnp.where(upper, part, other)], axis=0
        )
    return part


def cube(x):
    n = lax.axis_size("dp")
    bit = 1
    while bit < n:
        x = x + (yield x, "dp", [(i, i ^ bit) for i in range(n)])
        bit *= 2
    return x


class Steps:
    def __init__(self):
        self.active, self.results = {}, {}

    def add(self, name, moves):
        self.active[name] = (moves, next(moves))

    def run(self, work=None, inputs=()):
        names = list(self.active)
        sends = [self.active[name][1][0] for name in names]
        sends, inputs = lax.optimization_barrier((sends, tuple(inputs)))
        got = [lax.ppermute(x, *self.active[name][1][1:]) for name, x in zip(names, sends)]
        done = work(*inputs) if work else ()
        got, done = lax.optimization_barrier((got, done))
        for name, x in zip(names, got):
            moves = self.active.pop(name)[0]
            try:
                self.active[name] = (moves, moves.send(x))
            except StopIteration as stop:
                self.results[name] = stop.value
        return done

    def finish(self):
        while self.active:
            self.run()


def per_device(
    hidden_in,
    roi,
    bn_gain,
    bn_bias,
    w_qkv,
    bias_qv,
    w_out,
    bias_out,
    ln1_gain,
    ln1_bias,
    w_in,
    bias_in,
    w_back,
    bias_back,
    ln2_gain,
    ln2_bias,
    pair_w,
    pair_bias,
    dir_w,
    text_len,
    owner_order,
    pair_index,
    cot_out,
    cot_logits,
):
    docs = text_len.shape[0]
    slots = hidden_in.shape[0] // docs
    width = hidden_in.shape[1]
    segs = slots - TEXT
    seg_rows = roi.shape[0]
    n_dp = lax.axis_size("dp")
    all_rows = seg_rows * n_dp
    half, half_seg = TEXT // 2, segs // 2
    m = lax.axis_index("mp")
    c = m % 2
    dp = lax.axis_index("dp")
    shifts = (dp % 2, dp // 2 % 2)
    place = jnp.stack([c, *shifts]).astype(jnp.int32)
    part = w_qkv.shape[2]
    from_sib = lambda x: swap(x, "mp", 1)
    from_x = lambda x: swap(x, "mp", 2)
    later = lambda w, after: lax.optimization_barrier((w, after))[0]

    def near(k, *arrays):
        parts = []
        for w in arrays:
            size = w.shape[0] // 2
            parts.append(lax.dynamic_slice_in_dim(w, shifts[k] * size, size, 0))
        return from_x(jnp.concatenate(parts, axis=0))

    second = jnp.arange(2, dtype=jnp.int32)[:, None] == 1

    def merge(one, two, count):
        gap = one[0:1] - two[0:1]
        both = one + two
        return jnp.where(second, both + gap * gap * (0.5 * seg_rows * count), 0.5 * both)

    own = (w_out, w_in, w_back)
    close_in = near(0, w_out, w_in)
    close_back = near(1, w_back)
    own_sib = tuple(from_sib(w) for w in own)
    bias_sib, bias_x = from_sib(bias_in), from_x(bias_in)
    bias_xsib = from_sib(bias_x)
    stats = butterfly(local_stats(roi), merge)
    stats, bias_rows = lax.optimization_barrier(
        (stats, (bias_in, bias_sib, bias_x, bias_xsib))
    )
    qkv, lse, both_seg, both_txt, x_seg, x_txt = attn_fwd(
        all_rows, place, text_len, hidden_in, roi, stats, bn_gain, bn_bias, w_qkv, bias_qv
    )

    close, own_sib, both_seg, both_txt = lax.optimization_barrier(
        ((close_in, close_back), own_sib, both_seg, both_txt)
    )
    far = (swap(close[0], "dp", 1), swap(close[1], "dp", 2))
    far_seg, far_txt = from_x(both_seg), from_x(both_txt)
    close_sib = tuple(from_sib(w) for w in close)
    both_sib = (from_sib(both_seg), from_sib(both_txt))
    far, far_seg, close_sib, both_sib = lax.optimization_barrier(
        (far, far_seg, close_sib, both_sib)
    )
    far_sib = tuple(from_sib(w) for w in far)
    weights = ((w_out, own_sib[0]),) + tuple(
        (own[1 + k], own_sib[1 + k], close[k], far[k], close_sib[k], far_sib[k]) for k in range(2)
    )
    ctx_seg = (both_seg, both_sib[0], far_seg, from_sib(far_seg))
    vec = (bias_out, ln1_gain, ln1_bias, bias_back, ln2_gain, ln2_bias)
    mine_rows = docs * (half + half_seg)
    txt_rows = docs * half
    seg = ffn(
        place, vec, bias_rows, weights, docs * half_seg, txt_rows, mine_rows, None,
        ctx=ctx_seg, xres=x_seg,
    )

    far_txt = later(far_txt, seg["out"])
    ctx_txt = (both_txt, both_sib[1], far_txt, from_sib(far_txt))

    txt = {name: seg[name] for name in ("h1", "act0", "act1")}
    txt_sums, gwo = [], []

    def text(doc, *first):
        done = ffn(
            place, vec, bias_rows, weights, half, 0, mine_rows, None,
            ctx=ctx_txt, xres=first[0], gout=cot_out, into=txt, start=doc, count=1,
        )
        txt_sums.append(done.pop("sums"))
        gwo.append(done.pop("gwo"))
        txt.update(done)

    share = width // lax.axis_size("mp")
    cols = lambda x, who: lax.dynamic_slice_in_dim(x, who * share, share, 1)
    mine, theirs = cols(seg["out"], m), from_sib(cols(seg["out"], m ^ 1))
    by_core = lambda a, b: (jnp.where(c == 0, a, b), jnp.where(c == 0, b, a))
    columns = jnp.stack(
        [p.reshape(docs, half_seg, share) for p in by_core(mine, theirs)], axis=1
    ).reshape(seg_rows, share)
    ordering = owner_order[0]
    swap_rows = lambda x: lax.all_to_all(x, "dp", split_axis=0, concat_axis=0, tiled=True)
    ordered, x_txt = lax.optimization_barrier((jnp.take(columns, ordering, axis=0), x_txt))
    received = swap_rows(ordered)
    text(0, x_txt)
    received, x_txt = lax.optimization_barrier((received, later(x_txt, txt_sums[0])))
    candidates = jnp.arange(seg_rows, dtype=jnp.int32)[None, :]
    pick_left = (pair_index[:, 0:1] == candidates).astype(F32)
    pick_right = (pair_index[:, 1:2] == candidates).astype(F32)
    sides = jnp.concatenate([product(pick_left, received), product(pick_right, received)], axis=1)
    pair_w2 = pair_w.reshape(2 * share, width)
    pair_part = product(sides, pair_w2)
    pair_part = pair_part + from_sib(pair_part)
    pairs_half = pair_part.shape[0] // 2
    piece = lax.dynamic_slice_in_dim(pair_part, c * pairs_half, pairs_half, 0)
    piece, x_txt = lax.optimization_barrier((piece, x_txt))
    other = from_x(piece)
    if docs > 1:
        text(1, x_txt)
    piece, x_txt = lax.optimization_barrier((piece + later(other, txt_sums[-1]), x_txt))
    pair_pre = jnp.concatenate(by_core(piece, from_sib(piece)), axis=0) + pair_bias
    root = 0.5 * (1.0 + lax.erf(pair_pre * ROOT_HALF))
    pair_act = pair_pre * root
    logits = product(pair_act, dir_w)
    grad_dir_w = product(cot_logits, pair_act, ((0,), (0,)))
    grad_pair_pre = product(cot_logits, dir_w, ((1,), (1,))) * (
        root + pair_pre * jnp.exp(-0.5 * pair_pre * pair_pre) * DENSITY
    )
    grad_pair_bias = jnp.sum(grad_pair_pre, axis=0)
    grad_pair_w = product(sides, grad_pair_pre, ((0,), (0,)))
    grad_sides = product(grad_pair_pre, pair_w2, ((1,), (1,)))
    grad_received = product(pick_left, grad_sides[:, :share], ((0,), (0,))) + product(
        pick_right, grad_sides[:, share:], ((0,), (0,))
    )
    grad_received, x_txt = lax.optimization_barrier((grad_received, x_txt))
    grad_sent = swap_rows(grad_received)
    for doc in range(2, docs):
        text(doc, x_txt)
    grad_sent = later(grad_sent, txt_sums[-1])
    back_order = jnp.zeros_like(ordering).at[ordering].set(jnp.arange(seg_rows, dtype=jnp.int32))
    grad_cols = jnp.take(grad_sent, back_order, axis=0).reshape(docs, 2, half_seg, share)
    rows_of = lambda who: lax.dynamic_index_in_dim(grad_cols, who, 1, keepdims=False).reshape(
        docs * half_seg, share
    )
    grad_mine, grad_theirs = rows_of(c), from_sib(rows_of(1 - c))
    chip_cols = jnp.concatenate(by_core(grad_mine, grad_theirs), axis=1)
    far_cols = from_x(chip_cols)
    low_x = m < 2
    grad_seg = jnp.concatenate(
        [jnp.where(low_x, chip_cols, far_cols), jnp.where(low_x, far_cols, chip_cols)], axis=1
    )
    cot_seg = lax.dynamic_slice_in_dim(
        cot_out.reshape(docs, slots, width), TEXT + c * half_seg, half_seg, 1
    ).reshape(docs * half_seg, width)
    output = join_rows(
        docs, segs, place, seg["out"], txt["out"],
        from_sib(seg["out"]), from_sib(later(txt["out"], grad_cols)),
    )
    grad_seg, output = lax.optimization_barrier((grad_seg, output))
    back = ffn(
        place, vec, bias_rows, weights, docs * half_seg, txt_rows, mine_rows,
        [seg[name] for name in ("n1", "f1", "n2", "f2", "slope")],
        ctx=ctx_seg, gout=cot_seg + grad_seg,
        into={name: txt[name] for name in ("gs", "gi0", "gi1", "gf")},
    )

    tall = ((0,), (0,))
    sib_back = from_sib(product(txt["act1"], back["gs"], tall))
    sib_in = from_sib(product(txt["h1"], back["gi1"], tall))
    grad_back_own = product(txt["act0"], back["gs"], tall) + sib_back
    grad_in_own = product(txt["h1"], back["gi0"], tall) + sib_in
    gf_txt, gf_seg = back["gf"][:txt_rows], back["gf"][txt_rows:]
    gwo = sum(gwo) + back["gwo"]
    grad_out_own = gwo[:part] + from_sib(gwo[part:])

    steps = Steps()
    steps.add("in_out", ring(jnp.concatenate([grad_in_own, grad_out_own], axis=0), 1, (width, part)))
    back_pair = jnp.concatenate([grad_back_own, grad_pair_w], axis=0)
    steps.add("back_pair", ring(back_pair, -1, (width, 2 * share)))
    mine = (back["gb"], txt["gb"])
    theirs = tuple(from_sib(g) for g in mine)
    w_sum = jnp.zeros((3 * part, width), F32)
    b_sum = jnp.zeros((1, 3 * part), F32)
    gx, gh_mine, gh_theirs = [], [], []

    def finish_rows(doc, chip_sum, far):
        first = jnp.concatenate(
            [gf_seg[doc * half_seg : (doc + 1) * half_seg], gf_txt[doc * half : (doc + 1) * half]],
            axis=0,
        )
        gh_mine.append(first + (chip_sum + far))
        gh_theirs.append(from_sib(gh_mine[-1]))

    for doc in range(docs):

        def scores(b_sum, doc=doc):
            return attn_bwd(
                doc, place, text_len, qkv, lse, (both_seg, both_txt), mine, theirs, b_sum
            )

        def weights_of(gq, w_sum, doc=doc):
            grads = qkv_bwd(
                all_rows, doc, docs, place, hidden_in, roi, stats, bn_gain, bn_bias, w_qkv, gq, w_sum
            )
            return (*grads, *(far for _, far in gx[-1:]))

        gq, b_sum = steps.run(scores, (b_sum,))
        gx_mine, gx_theirs, w_sum, *far = steps.run(weights_of, (gq, w_sum))
        if far:
            finish_rows(doc - 1, gx[-1][0], far[0])
        chip_sum = gx_mine + from_sib(gx_theirs)
        gx.append((chip_sum, from_x(chip_sum)))
    cut = w_sum.shape[0] * 5 // 9
    qkv_steps = Steps()
    qkv_steps.add("qkv_low", halving(w_sum[:cut], 0))
    qkv_steps.add("qkv_high", halving(w_sum[cut:], 1))
    qkv_steps.finish()
    steps.run()
    (far,) = steps.run(lambda: (gx[-1][1],))
    finish_rows(docs - 1, gx[-1][0], far)
    (gh_theirs[-1],) = steps.run(lambda: (gh_theirs[-1],))
    grad_hidden, bn_sums = final_rows(all_rows, segs, place, gh_mine, gh_theirs, roi, stats)

    rows = sum(txt_sums) + back["sums"]
    rows = jnp.concatenate([rows[:6], rows[6:7]]) + from_sib(jnp.concatenate([rows[:6], rows[7:8]]))
    pad = lambda v: jnp.pad(v, (0, width - v.shape[0]))[None]
    vectors = jnp.concatenate(
        [
            rows,
            grad_pair_bias[None],
            grad_dir_w,
            pad(b_sum[0, :part]),
            pad(b_sum[0, 2 * part :]),
            bn_sums[0:2],
        ],
        axis=0,
    )
    steps.add("vectors", cube(vectors))
    steps.finish()
    steps.results.update(qkv_steps.results)
    vectors, in_out, back_pair, low, high = (
        steps.results[name] for name in ("vectors", "in_out", "back_pair", "qkv_low", "qkv_high")
    )
    sum_qkv = jnp.concatenate([low, high], axis=0)
    n_dirs = dir_w.shape[1]
    sum_dir_w = vectors[8 : 8 + n_dirs].T
    tail = vectors[8 + n_dirs :]
    sum_bias_qv = tail[0:2, :part]
    grad_bn_bias, grad_bn_gain = tail[2], tail[3]
    grad_roi_out = grad_hidden.reshape(docs, slots, width)[:, TEXT:].reshape(seg_rows, width)
    roi_factor = lax.rsqrt(stats[1] / all_rows + EPSILON)
    roi_normed = (roi - stats[0]) * roi_factor
    grad_roi = (
        bn_gain
        * roi_factor
        * (grad_roi_out - grad_bn_bias / all_rows - roi_normed * grad_bn_gain / all_rows)
    )
    return (
        output,
        logits,
        grad_hidden,
        grad_roi,
        grad_bn_gain,
        grad_bn_bias,
        jnp.transpose(sum_qkv.reshape(3, part, width), (0, 2, 1)),
        sum_bias_qv,
        in_out[1],
        vectors[5],
        vectors[3],
        vectors[4],
        in_out[0],
        vectors[6],
        back_pair[0],
        vectors[2],
        vectors[0],
        vectors[1],
        back_pair[1].reshape(2, share, width),
        vectors[7],
        sum_dir_w,
    )


def solution(mesh):
    placed = (
        P("dp", None),
        P("dp", None),
        P(),
        P(),
        P(None, None, "mp"),
        P(None, "mp"),
        P("mp", None),
        P(),
        P(),
        P(),
        P(None, "mp"),
        P("mp"),
        P("mp", None),
        P(),
        P(),
        P(),
        P(None, "mp", None),
        P(),
        P(),
        P("dp"),
        P("dp", None),
        P("dp", None),
        P("dp", None),
        P("dp", None),
    )
    return jax.shard_map(
        per_device,
        mesh=mesh,
        in_specs=placed,
        out_specs=(
            P("dp", None),
            P("dp", None),
            P("dp", None),
            P("dp", None),
            P(),
            P(),
            P(None, None, "mp"),
            P(None, "mp"),
            P("mp", None),
            P(),
            P(),
            P(),
            P(None, "mp"),
            P("mp"),
            P("mp", None),
            P(),
            P(),
            P(),
            P(None, "mp", None),
            P(),
            P(),
        ),
        check_vma=False,
    )
```

```python
import functools

import jax
import jax.numpy as jnp
from jax import lax
from jax.experimental import pallas as pl
from jax.experimental.pallas import tpu as pltpu
from jax.sharding import PartitionSpec as P

HEAD_DIM = 64
TEXT = 512
EPSILON = 1e-05
NEGATIVE = -1e30
ROOT_HALF = 0.7071067811865476
DENSITY = 0.3989422804014327
HIGH = lax.Precision.HIGH
QUERY_STEP = 256
VMEM_LIMIT = 60 << 20
F32 = jnp.float32
BF16 = jnp.bfloat16


def product(operand, other, dims=((1,), (0,))):
    return lax.dot_general(
        operand, other, (dims, ((), ())), precision=HIGH, preferred_element_type=F32
    )


def halves(x):
    hi = x.astype(BF16)
    return hi, (x - hi.astype(F32)).astype(BF16)


def dot(a, b, dims=((1,), (0,))):
    return lax.dot_general(a, b, (dims, ((), ())), preferred_element_type=F32)


ROWS_BY_ROWS = ((1,), (1,))
COLS_BY_COLS = ((0,), (0,))


def dot3_apart(a, b, dims=((1,), (0,))):
    return dot(a[0], b[0], dims) + dot(a[1], b[0], dims) + dot(a[0], b[1], dims)


def dot3(a, b, dims=((1,), (0,))):
    ka, kb = dims[0][0], dims[1][0]
    return dot(jnp.concatenate([a[0], a[1], a[0]], ka), jnp.concatenate([b[0], b[0], b[1]], kb), dims)


def gelu_parts(v):
    phi = 0.5 + 0.5 * lax.erf(v * ROOT_HALF)
    return v * phi, phi + v * jnp.exp(-0.5 * v * v) * DENSITY


def normalize_rows(y):
    center = y - jnp.mean(y, axis=-1, keepdims=True)
    factor = lax.rsqrt(jnp.mean(center * center, axis=-1, keepdims=True) + EPSILON)
    return center * factor, factor


def normalize_rows_back(upstream, normed, factor):
    return factor * (
        upstream
        - jnp.mean(upstream, axis=-1, keepdims=True)
        - normed * jnp.mean(upstream * normed, axis=-1, keepdims=True)
    )


def colsum(x):
    return jnp.sum(x, axis=0, keepdims=True)


def lane_is(rows, width, lane):
    return lax.broadcasted_iota(jnp.int32, (rows, width), 1) == lane


def cost(products, moved):
    return pl.CostEstimate(flops=6 * products, bytes_accessed=moved, transcendentals=0)


def smem():
    return pl.BlockSpec(memory_space=pltpu.SMEM)


def whole(shape):
    return pl.BlockSpec(shape, lambda *_: (0,) * len(shape), pipeline_mode=pl.Buffered(1))


def sds(*shape):
    return jax.ShapeDtypeStruct(shape, F32)


def batch_normed(roi, stats, rows):
    return (roi - stats[0:1]) * lax.rsqrt(stats[1:2] / rows + EPSILON)


def segment_rows(roi, stats, rows, gain, shift):
    return batch_normed(roi[...], stats, rows) * gain[...][None, :] + shift[...][None, :]


def side_rows(ref, side, half, half_seg):
    return (
        ref.at[pl.ds(pl.multiple_of(TEXT + side * half_seg, half_seg), half_seg)],
        ref.at[pl.ds(pl.multiple_of(side * half, half), half)],
    )


def split_qkv(w, w_hi, w_lo):
    part = w.shape[2]
    for i in range(3):
        lanes = slice(i * part, (i + 1) * part)
        w_hi[:, lanes], w_lo[:, lanes] = halves(w[i])


def attn_fwd_kernel(all_rows, *refs):
    place, lens, hid, roi, stats, gain, shift, w, bias = refs[:9]
    qkv, lse, both_seg, both_txt, xm_seg, xm_txt = refs[9:15]
    w_hi, w_lo, x_seg, ctx, ctx_t = refs[15:]
    doc = pl.program_id(0)
    c = place[0]
    width = w.shape[2]
    heads = width // HEAD_DIM
    slots = hid.shape[0]
    half, half_seg = TEXT // 2, (slots - TEXT) // 2

    @pl.when(doc == 0)
    def _():
        split_qkv(w, w_hi, w_lo)

    x_seg[...] = hid[TEXT:, :] + segment_rows(roi, stats, all_rows, gain, shift)
    wide = (w_hi[...], w_lo[...])
    added = jnp.concatenate([bias[0:1, :], jnp.zeros((1, width), F32), bias[1:2, :]], axis=1)
    for start in (0, half):
        qkv[start : start + half, :] = dot3(halves(hid[start : start + half, :]), wide) + added
    qkv[TEXT:, :] = dot3(halves(x_seg[...]), wide) + added

    position = lax.broadcasted_iota(jnp.int32, (slots, HEAD_DIM), 0)
    first = lane_is(slots, HEAD_DIM, 0)
    dead = (position >= lens[doc]) & (position < TEXT)
    key_extra = jnp.where(first & dead, NEGATIVE, 0.0).astype(BF16)
    ones = jnp.where(first, 1.0, 0.0).astype(BF16)
    one_rows = jnp.ones((16, slots), BF16)
    values = jnp.transpose(qkv[:, 2 * width :])
    for h in range(heads):
        at = h * HEAD_DIM
        q_hi, q_lo = halves(qkv[:, at : at + HEAD_DIM] * HEAD_DIM**-0.5)
        k_hi, k_lo = halves(qkv[:, width + at : width + at + HEAD_DIM])
        v_two = jnp.concatenate([*halves(values[at : at + HEAD_DIM, :]), one_rows], axis=0)
        q_pack = jnp.concatenate([q_hi, q_lo, q_hi, ones], axis=1)
        k_pack = jnp.concatenate([k_hi, k_hi, k_lo, key_extra], axis=1)
        for start in range(0, slots, QUERY_STEP):
            cols = slice(start, min(slots, start + QUERY_STEP))
            scores = dot(k_pack, q_pack[cols], ROWS_BY_ROWS)
            top = jnp.max(scores, axis=0, keepdims=True)
            p_hi, p_lo = halves(jnp.exp(scores - top))
            mixed = dot(v_two, p_hi) + dot(v_two, p_lo)
            total = mixed[2 * HEAD_DIM : 2 * HEAD_DIM + 1]
            ctx_t[at : at + HEAD_DIM, cols] = (
                mixed[:HEAD_DIM] + mixed[HEAD_DIM : 2 * HEAD_DIM]
            ) / total
            lse[h : h + 1, cols] = top + jnp.log(total)
    ctx[...] = jnp.transpose(ctx_t[...])
    for lanes, side in ((slice(0, width), c), (slice(width, 2 * width), 1 - c)):
        at_seg, at_txt = side_rows(ctx, side, half, half_seg)
        both_seg[:, lanes] = at_seg[...]
        both_txt[:, lanes] = at_txt[...]
    xm_seg[...] = x_seg[pl.ds(pl.multiple_of(c * half_seg, half_seg), half_seg), :]
    xm_txt[...] = hid[pl.ds(pl.multiple_of(c * half, half), half), :]


def by_doc(rows, lanes):
    return pl.BlockSpec((rows, lanes), lambda d: (d, 0))


def attn_fwd(all_rows, place, lens, hidden, roi, stats, gain, shift, w, bias):
    docs = lens.shape[0]
    slots, width = hidden.shape[0] // docs, hidden.shape[1]
    segs = slots - TEXT
    part = w.shape[2]
    out_rows = [
        (slots, 3 * part),
        (8, slots),
        (segs // 2, 2 * part),
        (TEXT // 2, 2 * part),
        (segs // 2, width),
        (TEXT // 2, width),
    ]
    return pl.pallas_call(
        functools.partial(attn_fwd_kernel, all_rows),
        grid=(docs,),
        in_specs=[smem(), smem(), by_doc(slots, width), by_doc(segs, width)]
        + [whole(a.shape) for a in (stats, gain, shift, w, bias)],
        out_specs=[by_doc(*s) for s in out_rows],
        out_shape=[sds(docs * s[0], s[1]) for s in out_rows],
        scratch_shapes=[
            pltpu.VMEM((width, 3 * part), BF16),
            pltpu.VMEM((width, 3 * part), BF16),
            pltpu.VMEM((segs, width), F32),
            pltpu.VMEM((slots, part), F32),
            pltpu.VMEM((part, slots), F32),
        ],
        compiler_params=pltpu.CompilerParams(vmem_limit_bytes=VMEM_LIMIT),
        cost_estimate=cost(docs * slots, slots),
        name="attn_fwd",
    )(place, lens, hidden, roi, stats, gain, shift, w, bias)


def attn_bwd_kernel(doc, *refs):
    place, lens, qkv, lse, ctx_seg, ctx_txt, gm_seg, gm_txt, gt_seg, gt_txt, b_sum = refs[:11]
    gq, b_out, o_all, g_all, gq_t = refs[11:]
    c = place[0]
    width = qkv.shape[1] // 3
    heads = width // HEAD_DIM
    slots = qkv.shape[0]
    half, half_seg = TEXT // 2, (slots - TEXT) // 2
    near, far = slice(0, width), slice(width, 2 * width)
    for dst, mine, theirs in (
        (o_all, (ctx_seg, ctx_txt), (ctx_seg, ctx_txt)),
        (g_all, (gm_seg, gm_txt), (gt_seg, gt_txt)),
    ):
        for side, sources, lanes in ((c, mine, near), (1 - c, theirs, far)):
            for place_at, source in zip(side_rows(dst, side, half, half_seg), sources):
                place_at[...] = source[:, lanes]

    position = lax.broadcasted_iota(jnp.int32, (slots, HEAD_DIM), 0)
    first = lane_is(slots, HEAD_DIM, 0)
    dead = (position >= lens[doc]) & (position < TEXT)
    key_extra = jnp.where(first & dead, NEGATIVE, 0.0).astype(BF16)
    ones = jnp.where(first, 1.0, 0.0).astype(BF16)
    none = jnp.zeros_like(ones)
    head_of = lax.broadcasted_iota(jnp.int32, (16, width), 1) // HEAD_DIM
    pick_head = jnp.where(
        head_of == lax.broadcasted_iota(jnp.int32, (16, width), 0), 1.0, 0.0
    ).astype(BF16)
    scale = HEAD_DIM**-0.5
    product_hi, product_lo = halves(g_all[...] * o_all[...])
    inner = dot(pick_head, product_hi, ROWS_BY_ROWS) + dot(pick_head, product_lo, ROWS_BY_ROWS)
    keys_t = jnp.transpose(qkv[:, width : 2 * width])
    for h in range(heads):
        at = h * HEAD_DIM
        q_hi, q_lo = halves(qkv[:, at : at + HEAD_DIM] * scale)
        k_hi, k_lo = halves(qkv[:, width + at : width + at + HEAD_DIM])
        v_hi, v_lo = halves(qkv[:, 2 * width + at : 2 * width + at + HEAD_DIM])
        g_hi, g_lo = halves(g_all[:, at : at + HEAD_DIM])
        k_rows = jnp.concatenate(halves(keys_t[at : at + HEAD_DIM, :]), axis=0)
        q_pack = jnp.concatenate([q_hi, q_lo, q_hi, ones], axis=1)
        k_pack = jnp.concatenate([k_hi, k_hi, k_lo, key_extra], axis=1)
        g_pack = jnp.concatenate([g_hi, g_lo, g_hi, none], axis=1)
        v_pack = jnp.concatenate([v_hi, v_hi, v_lo, none], axis=1)
        q_two = jnp.concatenate([q_hi, q_lo], axis=1)
        g_two = jnp.concatenate([g_hi, g_lo], axis=1)
        weights = jnp.exp(dot(k_pack, q_pack, ROWS_BY_ROWS) - lse[h : h + 1, :])
        grads = weights * (dot(v_pack, g_pack, ROWS_BY_ROWS) - inner[h : h + 1, :])
        w_two = halves(weights)
        s_two = halves(grads)
        grad_v = dot(w_two[0], g_two) + dot(w_two[1], g_two)
        grad_k = dot(s_two[0], q_two) + dot(s_two[1], q_two)
        grad_q = dot(k_rows, s_two[0]) + dot(k_rows, s_two[1])
        gq[:, width + at : width + at + HEAD_DIM] = grad_k[:, :HEAD_DIM] + grad_k[:, HEAD_DIM:]
        gq[:, 2 * width + at : 2 * width + at + HEAD_DIM] = (
            grad_v[:, :HEAD_DIM] + grad_v[:, HEAD_DIM:]
        )
        gq_t[at : at + HEAD_DIM, :] = (grad_q[:HEAD_DIM] + grad_q[HEAD_DIM:]) * scale
    gq[:, :width] = jnp.transpose(gq_t[...])
    b_out[...] = b_sum[...] + colsum(gq[...])


def attn_bwd(doc, place, lens, qkv, lse, ctx, mine, theirs, b_sum):
    docs = lens.shape[0]
    slots, cols = qkv.shape[0] // docs, qkv.shape[1]
    segs = slots - TEXT
    part = cols // 3
    of_doc = lambda rows, lanes: pl.BlockSpec((rows, lanes), lambda i: (doc, 0))
    rows = [of_doc(segs // 2, 2 * part), of_doc(TEXT // 2, 2 * part)]
    return pl.pallas_call(
        functools.partial(attn_bwd_kernel, doc),
        grid=(1,),
        in_specs=[smem(), smem(), of_doc(slots, cols), of_doc(8, slots)] + rows * 3 + [whole((1, cols))],
        out_specs=[whole((slots, cols)), whole((1, cols))],
        out_shape=[sds(slots, cols), sds(1, cols)],
        scratch_shapes=[
            pltpu.VMEM((slots, part), F32),
            pltpu.VMEM((slots, part), F32),
            pltpu.VMEM((part, slots), F32),
        ],
        compiler_params=pltpu.CompilerParams(vmem_limit_bytes=32 << 20),
        cost_estimate=cost(slots * part * 16 * slots, 8 * slots * cols),
        name="attn_bwd",
    )(place, lens, qkv, lse, *ctx, *mine, *theirs, b_sum)


def qkv_bwd_kernel(all_rows, *refs):
    place, hid, roi, stats, gain, shift, w, gq, w_sum = refs[:9]
    gx_mine, gx_theirs, w_out = refs[9:12]
    w_hi, w_lo, x_all, gx = refs[12:]
    c = place[0]
    slots = hid.shape[0]
    half, half_seg = TEXT // 2, (slots - TEXT) // 2
    split_qkv(w, w_hi, w_lo)
    x_all[:TEXT, :] = hid[:TEXT, :]
    x_all[TEXT:, :] = hid[TEXT:, :] + segment_rows(roi, stats, all_rows, gain, shift)
    wide = (w_hi[...], w_lo[...])
    for start in range(0, slots, 320):
        rows = slice(start, min(slots, start + 320))
        gx[rows, :] = dot3_apart(halves(gq[rows, :]), wide, ROWS_BY_ROWS)
    w_out[...] = w_sum[...] + dot3_apart(halves(gq[...]), halves(x_all[...]), COLS_BY_COLS)
    for dst, side in ((gx_mine, c), (gx_theirs, 1 - c)):
        at_seg, at_txt = side_rows(gx, side, half, half_seg)
        dst[:half_seg, :] = at_seg[...]
        dst[half_seg:, :] = at_txt[...]


def qkv_bwd(all_rows, doc, docs, place, hidden, roi, stats, gain, shift, w, gq, w_sum):
    slots, width = hidden.shape[0] // docs, hidden.shape[1]
    cols = gq.shape[1]
    of_doc = lambda rows, lanes: pl.BlockSpec((rows, lanes), lambda i: (doc, 0))
    return pl.pallas_call(
        functools.partial(qkv_bwd_kernel, all_rows),
        grid=(1,),
        in_specs=[smem(), of_doc(slots, width), of_doc(slots - TEXT, width)]
        + [whole(a.shape) for a in (stats, gain, shift, w, gq, w_sum)],
        out_specs=[whole((slots // 2, width)), whole((slots // 2, width)), whole((cols, width))],
        out_shape=[sds(slots // 2, width), sds(slots // 2, width), sds(cols, width)],
        scratch_shapes=[
            pltpu.VMEM((width, cols), BF16),
            pltpu.VMEM((width, cols), BF16),
            pltpu.VMEM((slots, width), F32),
            pltpu.VMEM((slots, width), F32),
        ],
        compiler_params=pltpu.CompilerParams(vmem_limit_bytes=32 << 20),
        cost_estimate=cost(slots * cols * 2 * width, 12 * slots * width),
        name="qkv_bwd",
    )(place, hidden, roi, stats, gain, shift, w, gq, w_sum)


VECTORS = ("bias_out", "ln1_gain", "ln1_bias", "bias_back", "ln2_gain", "ln2_bias")
TILES = 4
PIECE_SHARDS = (0, 1, 2, 2, 3, 3)


def piece_place(i, rows, shift):
    if i < 2:
        return 0
    half = rows // 2
    return pl.multiple_of((shift if i % 2 == 0 else 1 - shift) * half, half)


def ffn_kernel(forward, backward, names, *refs):
    ref = dict(zip(names, refs))
    place, stage, sems = ref["place"], ref["stage"], ref["sems"]
    wts, acc, a_hi, a_lo = ref["wts"], ref["acc"], ref["a_hi"], ref["a_lo"]
    wo = ref["wo"]
    resident = wts.shape[0] == TILES
    c = place[0]
    shifts = {"wo": place[1], "wi": place[1], "wb": place[2]}
    width = acc.shape[1]
    rows = acc.shape[0]
    part = wo.shape[1] // 4
    row = lambda name: ref[name][...][None, :]

    def two_shards(one, two):
        lane = lax.broadcasted_iota(jnp.int32, (rows, 2 * part), 1)
        return jnp.where(lane < part, ref[one][...], ref[two][...])

    def copies(tile):
        found = []
        for i in range(6):
            if PIECE_SHARDS[i] == tile:
                for k, kind in enumerate(("wi", "wb")):
                    piece = ref[f"{kind}{i}"]
                    if kind == "wi" and i > 1:
                        piece = piece.at[pl.ds(part // 2, width // 2)]
                    at = pl.ds(piece_place(i, width, shifts[kind]), piece.shape[0])
                    where = stage.at[tile % 2, k, at, :]
                    found.append(
                        pltpu.make_async_copy(piece, where, sems.at[tile % 2, len(found)])
                    )
        return found

    def start_tile(tile):
        for copy in copies(tile):
            copy.start()

    slot_of = lambda tile: tile if resident else tile % 2

    def ready(tile):
        for copy in copies(tile):
            copy.wait()
        slot = slot_of(tile)
        wts[slot, 0], wts[slot, 1] = halves(stage[tile % 2, 0])
        wts[slot, 2], wts[slot, 3] = halves(stage[tile % 2, 1])
        if tile + 2 < TILES:
            start_tile(tile + 2)

    def load_wo(count):
        for i in range(count):
            at = PIECE_SHARDS[i] * part + piece_place(i, part, shifts["wo"])
            where = pl.ds(at, ref[f"wo{i}"].shape[0])
            wo[0, where, :], wo[1, where, :] = halves(ref[f"wo{i}"][...])

    def run_forward(loading):
        y = ref["xres"][...] + row("bias_out")
        for one, two, at in (
            ("ctx_own", "ctx_sib", slice(0, 2 * part)),
            ("ctx_far", "ctx_farsib", slice(2 * part, 4 * part)),
        ):
            y = y + dot3(halves(two_shards(one, two)), (wo[0, at, :], wo[1, at, :]))
        normed, factor = normalize_rows(y)
        ref["n1"][...] = normed
        ref["f1"][...] = jnp.broadcast_to(factor, (rows, 128))
        h = normed * row("ln1_gain") + row("ln1_bias")
        ref["h1"][...] = h
        a_hi[...], a_lo[...] = halves(h)
        acc[...] = h + row("bias_back")
        for t in range(TILES):
            if loading and t == 0:
                ready(0)
            if loading and t + 1 < TILES:
                ready(t + 1)
            slot = slot_of(t)
            pre = dot3((a_hi[...], a_lo[...]), (wts[slot, 0], wts[slot, 1]))
            value, rise = gelu_parts(pre + row(f"bias_in{t}"))
            ref["slope"][t] = rise
            if t < 2:
                ref[f"act{t}"][...] = value
            acc[...] += dot3(halves(value), (wts[slot, 2], wts[slot, 3]))
        normed, factor = normalize_rows(acc[...])
        ref["n2"][...] = normed
        ref["f2"][...] = jnp.broadcast_to(factor, (rows, 128))
        ref["out"][...] = normed * row("ln2_gain") + row("ln2_bias")

    def run_backward(loading):
        sums = ref["sums"]
        if forward:
            g = ref["gout"][pl.ds(pl.multiple_of(c * rows, rows), rows), :]
        else:
            g = ref["gout"][...]
        n2 = ref["n2"][...]
        sums[0:1, :] += colsum(g * n2)
        sums[1:2, :] += colsum(g)
        back = normalize_rows_back(g * row("ln2_gain"), n2, ref["f2"][:, 0:1])
        sums[2:3, :] += colsum(back)
        ref["gs"][...] = back
        acc[...] = back
        a_hi[...], a_lo[...] = halves(back)
        for t in range(TILES):
            if loading and t == 0:
                ready(0)
            if loading and t + 1 < TILES:
                ready(t + 1)
            slot = slot_of(t)
            grad = dot3((a_hi[...], a_lo[...]), (wts[slot, 2], wts[slot, 3]), ROWS_BY_ROWS)
            grad = grad * ref["slope"][t]
            if t < 2:
                ref[f"gi{t}"][...] = grad
                sums[6 + t : 7 + t, :] += colsum(grad)
            acc[...] += dot3(halves(grad), (wts[slot, 0], wts[slot, 1]), ROWS_BY_ROWS)
        g, n1 = acc[...], ref["n1"][...]
        sums[3:4, :] += colsum(g * n1)
        sums[4:5, :] += colsum(g)
        back = normalize_rows_back(g * row("ln1_gain"), n1, ref["f1"][:, 0:1])
        sums[5:6, :] += colsum(back)
        ref["gf"][...] = back
        two = halves(back)
        at = slice(0, 2 * part)
        ref["gb"][...] = dot3(two, (wo[0, at, :], wo[1, at, :]), ROWS_BY_ROWS)
        ref["gwo"][...] = dot3_apart(halves(two_shards("ctx_own", "ctx_sib")), two, COLS_BY_COLS)

    def begin():
        start_tile(0)
        start_tile(1)
        load_wo(6 if forward else 2)
        if backward:
            ref["sums"][...] = jnp.zeros_like(ref["sums"])

    if forward and backward:

        @pl.when(pl.program_id(0) == 0)
        def _():
            begin()
            run_forward(True)
            run_backward(False)

        @pl.when(pl.program_id(0) > 0)
        def _():
            run_forward(False)
            run_backward(False)
    else:
        begin()
        if forward:
            run_forward(True)
        if backward:
            run_backward(True)


def ffn(place, vectors, bias_in, weights, block, offset, total, saved, *, ctx=None, xres=None, gout=None, into=None, start=0, count=None):
    forward, backward = xres is not None, gout is not None
    both = forward and backward
    width = vectors[0].shape[0]
    rows = ctx[0].shape[0]
    blocks = rows // block
    part = width // 4
    w_out, w_in, w_back = weights
    first = offset // block + start
    local = lambda lanes: pl.BlockSpec((block, lanes), lambda r: (start + r, 0))
    shared = pl.BlockSpec((block, width), lambda r: (first + r, 0))
    anywhere = pl.BlockSpec(memory_space=pltpu.HBM)
    names, specs, args = [], [], []

    def take(name, spec, arg):
        names.append(name)
        specs.append(spec)
        args.append(arg)

    take("place", smem(), place)
    for name, a in zip(VECTORS, vectors):
        take(name, whole(a.shape), a)
    for name, a in zip(("ctx_own", "ctx_sib", "ctx_far", "ctx_farsib"), ctx):
        take(name, local(a.shape[1]), a)
    if forward:
        for t in range(TILES):
            take(f"bias_in{t}", whole(bias_in[t].shape), bias_in[t])
        take("xres", local(width), xres)
    if backward:
        if both:
            slots = gout.shape[0] // blocks
            take("gout", pl.BlockSpec((slots, width), lambda r: (start + r, 0)), gout)
        else:
            take("gout", local(width), gout)
    kept = (
        ("n1", (block, width)),
        ("f1", (block, 128)),
        ("n2", (block, width)),
        ("f2", (block, 128)),
        ("slope", (TILES, block, width)),
    )
    if backward and not forward:
        for (name, shape), a in zip(kept, saved):
            take(name, whole(shape), a)
    for i in range(6 if forward else 2):
        piece, height = (w_out[i], part) if i < 2 else (w_in[i], part // 2)
        take(f"wo{i}", whole((height, width)), piece)
    for i in range(6):
        take(f"wi{i}", anywhere, w_in[i])
        take(f"wb{i}", anywhere, w_back[i])
    outs = []
    if forward:
        outs += [("out", local(width), sds(rows, width))]
        outs += [(n, shared, sds(total, width)) for n in ("h1", "act0", "act1")]
        if not backward:
            outs += [(name, whole(shape), sds(*shape)) for name, shape in kept]
    if backward:
        outs += [(n, shared, sds(total, width)) for n in ("gs", "gi0", "gi1", "gf")]
        outs += [("gb", local(2 * part), sds(rows, 2 * part))]
        outs += [("gwo", whole((2 * part, width)), sds(2 * part, width))]
        outs += [("sums", whole((8, width)), sds(8, width))]
    aliases = {}
    if into:
        for k, (name, _, _) in enumerate(outs):
            if name in into:
                aliases[len(args)] = k
                take(name + "_into", anywhere, into[name])
    scratch = [
        ("stage", pltpu.VMEM((2, 2, width, width), F32)),
        ("sems", pltpu.SemaphoreType.DMA((2, 4))),
        ("wts", pltpu.VMEM((TILES if both else 2, 4, width, width), BF16)),
        ("wo", pltpu.VMEM((2, width, width), BF16)),
        ("acc", pltpu.VMEM((block, width), F32)),
        ("a_hi", pltpu.VMEM((block, width), BF16)),
        ("a_lo", pltpu.VMEM((block, width), BF16)),
    ]
    if both:
        scratch += [(name, pltpu.VMEM(shape, F32)) for name, shape in kept]
    all_names = names + [o[0] for o in outs] + [s[0] for s in scratch]
    passes = (3 if both else 1) * 8
    result = pl.pallas_call(
        functools.partial(ffn_kernel, forward, backward, all_names),
        grid=(count or blocks,),
        in_specs=specs,
        out_specs=[o[1] for o in outs],
        out_shape=[o[2] for o in outs],
        scratch_shapes=[s[1] for s in scratch],
        input_output_aliases=aliases,
        compiler_params=pltpu.CompilerParams(vmem_limit_bytes=VMEM_LIMIT),
        cost_estimate=cost(
            (count or blocks) * block * width * width * (16 if both else 8) + 4 * width**3,
            60 * block * width,
        ),
        name="ffn_" + "fwd" * forward + "bwd" * backward,
    )(*args)
    return {o[0]: r for o, r in zip(outs, result)}


def join_kernel(docs, segs, place, ms, mt, ts, tt, out):
    c = place[0]
    half, half_seg = TEXT // 2, segs // 2
    for seg, txt, side in ((ms, mt, c), (ts, tt, 1 - c)):
        at_seg, at_txt = side_rows(out, side, half, half_seg)
        at_seg[...] = seg[...]
        at_txt[...] = txt[...]


def join_rows(docs, segs, place, ms, mt, ts, tt):
    width = ms.shape[1]
    slots = TEXT + segs
    return pl.pallas_call(
        functools.partial(join_kernel, docs, segs),
        grid=(docs,),
        in_specs=[smem()] + [by_doc(segs // 2, width), by_doc(TEXT // 2, width)] * 2,
        out_specs=by_doc(slots, width),
        out_shape=sds(docs * slots, width),
        cost_estimate=cost(0, 8 * docs * slots * width),
        compiler_params=pltpu.CompilerParams(vmem_limit_bytes=VMEM_LIMIT),
        name="join_rows",
    )(place, ms, mt, ts, tt)


def final_kernel(docs, segs, all_rows, *refs):
    place = refs[0]
    mine, theirs = refs[1 : 1 + docs], refs[1 + docs : 1 + 2 * docs]
    roi, stats, out, sums = refs[1 + 2 * docs :]
    d = pl.program_id(0)
    c = place[0]
    half, half_seg = TEXT // 2, segs // 2

    @pl.when(d == 0)
    def _():
        sums[...] = jnp.zeros_like(sums)

    for i in range(docs):

        @pl.when(d == i)
        def _():
            for source, side in ((mine[i], c), (theirs[i], 1 - c)):
                at_seg, at_txt = side_rows(out, side, half, half_seg)
                at_seg[...] = source[:half_seg, :]
                at_txt[...] = source[half_seg:, :]

    g = out[TEXT:, :]
    sums[0:1, :] += colsum(g)
    sums[1:2, :] += colsum(g * batch_normed(roi[...], stats, all_rows))


def final_rows(all_rows, segs, place, mine, theirs, roi, stats):
    docs = len(mine)
    width = roi.shape[1]
    slots = TEXT + segs
    return pl.pallas_call(
        functools.partial(final_kernel, docs, segs, all_rows),
        grid=(docs,),
        in_specs=[smem()]
        + [whole((slots // 2, width))] * (2 * docs)
        + [by_doc(segs, width), whole(stats.shape)],
        out_specs=[by_doc(slots, width), pl.BlockSpec((8, width), lambda d: (0, 0))],
        out_shape=[sds(docs * slots, width), sds(8, width)],
        compiler_params=pltpu.CompilerParams(vmem_limit_bytes=VMEM_LIMIT),
        cost_estimate=cost(0, 20 * docs * slots * width),
        name="final_rows",
    )(place, *mine, *theirs, roi, stats)


def stats_kernel(roi, stats):
    x = roi[...]
    mean = jnp.mean(x, axis=0, keepdims=True)
    stats[0:1, :] = mean
    stats[1:2, :] = colsum((x - mean) * (x - mean))


def local_stats(roi):
    width = roi.shape[1]
    return pl.pallas_call(
        stats_kernel, out_shape=sds(2, width), name="local_stats"
    )(roi)


def swap(x, axis, bit):
    n = lax.axis_size(axis)
    return lax.ppermute(x, axis, [(i, i ^ bit) for i in range(n)])


def butterfly(x, merge):
    bit = 1
    while bit < lax.axis_size("dp"):
        x = merge(x, swap(x, "dp", bit), bit)
        bit *= 2
    return x


def ring(part, sign, cuts):
    n = lax.axis_size("dp")
    order = list(range(0, n, 2)) + list(range(n - 1, 0, -2))
    pairs = [(order[k], order[(k + sign) % n]) for k in range(n)]
    me = lax.axis_index("dp")
    place = sign * jnp.where(me % 2 == 0, me // 2, n - 1 - me // 2)
    size = part.shape[0] // n
    at = lambda k: ((place - k) % n) * size
    held = lax.dynamic_slice_in_dim(part, at(0), size, 0)
    for step in range(1, n):
        got = yield held, "dp", pairs
        held = got + lax.dynamic_slice_in_dim(part, at(step), size, 0)
    pieces = [held]
    for step in range(n - 1):
        held = yield held, "dp", pairs
        pieces.append(held)
    if size % 8 == 0:
        where = jnp.stack([at(k - 1) for k in range(n)]).astype(jnp.int32)
        return assemble(where, pieces, cuts)
    total = part
    for k, piece in enumerate(pieces):
        total = lax.dynamic_update_slice_in_dim(total, piece, at(k - 1), 0)
    return [total[sum(cuts[:i]) : sum(cuts[: i + 1])] for i in range(len(cuts))]


def assemble_kernel(count, where, *refs):
    outs, total = refs[count:-1], refs[-1]
    for k, piece in enumerate(refs[:count]):
        total[pl.ds(pl.multiple_of(where[k], 8), piece.shape[0]), :] = piece[...]
    at = 0
    for out in outs:
        out[...] = total[at : at + out.shape[0], :]
        at += out.shape[0]


def assemble(where, pieces, cuts):
    size, width = pieces[0].shape
    return pl.pallas_call(
        functools.partial(assemble_kernel, len(pieces)),
        in_specs=[smem()] + [pl.BlockSpec(memory_space=pltpu.VMEM)] * len(pieces),
        out_specs=[pl.BlockSpec(memory_space=pltpu.VMEM)] * len(cuts),
        out_shape=[sds(rows, width) for rows in cuts],
        scratch_shapes=[pltpu.VMEM((size * len(pieces), width), F32)],
        compiler_params=pltpu.CompilerParams(vmem_limit_bytes=VMEM_LIMIT),
        cost_estimate=cost(0, 8 * size * len(pieces) * width),
        name="assemble",
    )(where, *pieces)


def halving(part, turn):
    n = lax.axis_size("dp")
    bits = list(range(n.bit_length() - 1))
    bits = bits[turn:] + bits[:turn]
    me = lax.axis_index("dp")
    pairs = lambda bit: [(i, i ^ (1 << bit)) for i in range(n)]
    for bit in bits:
        upper = (me >> bit) % 2
        half = part.shape[0] // 2
        keep, give = (lax.dynamic_slice_in_dim(part, k * half, half, 0) for k in (upper, 1 - upper))
        part = keep + (yield give, "dp", pairs(bit))
    for bit in bits[::-1]:
        upper = (me >> bit) % 2 == 1
        other = yield part, "dp", pairs(bit)
        part = jnp.concatenate(
            [jnp.where(upper, other, part), jnp.where(upper, part, other)], axis=0
        )
    return part


def cube(x):
    n = lax.axis_size("dp")
    bit = 1
    while bit < n:
        x = x + (yield x, "dp", [(i, i ^ bit) for i in range(n)])
        bit *= 2
    return x


class Steps:
    def __init__(self):
        self.active, self.results = {}, {}

    def add(self, name, moves):
        self.active[name] = (moves, next(moves))

    def run(self, work=None, inputs=()):
        names = list(self.active)
        sends = [self.active[name][1][0] for name in names]
        sends, inputs = lax.optimization_barrier((sends, tuple(inputs)))
        got = [lax.ppermute(x, *self.active[name][1][1:]) for name, x in zip(names, sends)]
        done = work(*inputs) if work else ()
        got, done = lax.optimization_barrier((got, done))
        for name, x in zip(names, got):
            moves = self.active.pop(name)[0]
            try:
                self.active[name] = (moves, moves.send(x))
            except StopIteration as stop:
                self.results[name] = stop.value
        return done

    def finish(self):
        while self.active:
            self.run()


def per_device(
    hidden_in,
    roi,
    bn_gain,
    bn_bias,
    w_qkv,
    bias_qv,
    w_out,
    bias_out,
    ln1_gain,
    ln1_bias,
    w_in,
    bias_in,
    w_back,
    bias_back,
    ln2_gain,
    ln2_bias,
    pair_w,
    pair_bias,
    dir_w,
    text_len,
    owner_order,
    pair_index,
    cot_out,
    cot_logits,
):
    docs = text_len.shape[0]
    slots = hidden_in.shape[0] // docs
    width = hidden_in.shape[1]
    segs = slots - TEXT
    seg_rows = roi.shape[0]
    n_dp = lax.axis_size("dp")
    all_rows = seg_rows * n_dp
    half, half_seg = TEXT // 2, segs // 2
    m = lax.axis_index("mp")
    c = m % 2
    dp = lax.axis_index("dp")
    shifts = (dp % 2, dp // 2 % 2)
    place = jnp.stack([c, *shifts]).astype(jnp.int32)
    part = w_qkv.shape[2]
    from_sib = lambda x: swap(x, "mp", 1)
    from_x = lambda x: swap(x, "mp", 2)
    later = lambda w, after: lax.optimization_barrier((w, after))[0]

    def near(k, *arrays):
        parts = []
        for w in arrays:
            size = w.shape[0] // 2
            parts.append(lax.dynamic_slice_in_dim(w, shifts[k] * size, size, 0))
        return from_x(jnp.concatenate(parts, axis=0))

    second = jnp.arange(2, dtype=jnp.int32)[:, None] == 1

    def merge(one, two, count):
        gap = one[0:1] - two[0:1]
        both = one + two
        return jnp.where(second, both + gap * gap * (0.5 * seg_rows * count), 0.5 * both)

    own = (w_out, w_in, w_back)
    close_in = near(0, w_out, w_in)
    close_back = near(1, w_back)
    own_sib = tuple(from_sib(w) for w in own)
    bias_sib, bias_x = from_sib(bias_in), from_x(bias_in)
    bias_xsib = from_sib(bias_x)
    stats = butterfly(local_stats(roi), merge)
    stats, bias_rows = lax.optimization_barrier(
        (stats, (bias_in, bias_sib, bias_x, bias_xsib))
    )
    qkv, lse, both_seg, both_txt, x_seg, x_txt = attn_fwd(
        all_rows, place, text_len, hidden_in, roi, stats, bn_gain, bn_bias, w_qkv, bias_qv
    )

    close, own_sib, both_seg, both_txt = lax.optimization_barrier(
        ((close_in, close_back), own_sib, both_seg, both_txt)
    )
    far = (swap(close[0], "dp", 1), swap(close[1], "dp", 2))
    far_seg, far_txt = from_x(both_seg), from_x(both_txt)
    close_sib = tuple(from_sib(w) for w in close)
    both_sib = (from_sib(both_seg), from_sib(both_txt))
    far, far_seg, close_sib, both_sib = lax.optimization_barrier(
        (far, far_seg, close_sib, both_sib)
    )
    far_sib = tuple(from_sib(w) for w in far)
    weights = ((w_out, own_sib[0]),) + tuple(
        (own[1 + k], own_sib[1 + k], close[k], far[k], close_sib[k], far_sib[k]) for k in range(2)
    )
    ctx_seg = (both_seg, both_sib[0], far_seg, from_sib(far_seg))
    vec = (bias_out, ln1_gain, ln1_bias, bias_back, ln2_gain, ln2_bias)
    mine_rows = docs * (half + half_seg)
    txt_rows = docs * half
    seg = ffn(
        place, vec, bias_rows, weights, docs * half_seg, txt_rows, mine_rows, None,
        ctx=ctx_seg, xres=x_seg,
    )

    far_txt = later(far_txt, seg["out"])
    ctx_txt = (both_txt, both_sib[1], far_txt, from_sib(far_txt))

    txt = {name: seg[name] for name in ("h1", "act0", "act1")}
    txt_sums, gwo = [], []

    def text(doc, *first):
        done = ffn(
            place, vec, bias_rows, weights, half, 0, mine_rows, None,
            ctx=ctx_txt, xres=first[0], gout=cot_out, into=txt, start=doc, count=1,
        )
        txt_sums.append(done.pop("sums"))
        gwo.append(done.pop("gwo"))
        txt.update(done)

    share = width // lax.axis_size("mp")
    cols = lambda x, who: lax.dynamic_slice_in_dim(x, who * share, share, 1)
    mine, theirs = cols(seg["out"], m), from_sib(cols(seg["out"], m ^ 1))
    by_core = lambda a, b: (jnp.where(c == 0, a, b), jnp.where(c == 0, b, a))
    columns = jnp.stack(
        [p.reshape(docs, half_seg, share) for p in by_core(mine, theirs)], axis=1
    ).reshape(seg_rows, share)
    ordering = owner_order[0]
    swap_rows = lambda x: lax.all_to_all(x, "dp", split_axis=0, concat_axis=0, tiled=True)
    ordered, x_txt = lax.optimization_barrier((jnp.take(columns, ordering, axis=0), x_txt))
    received = swap_rows(ordered)
    text(0, x_txt)
    received, x_txt = lax.optimization_barrier((received, later(x_txt, txt_sums[0])))
    candidates = jnp.arange(seg_rows, dtype=jnp.int32)[None, :]
    pick_left = (pair_index[:, 0:1] == candidates).astype(F32)
    pick_right = (pair_index[:, 1:2] == candidates).astype(F32)
    sides = jnp.concatenate([product(pick_left, received), product(pick_right, received)], axis=1)
    pair_w2 = pair_w.reshape(2 * share, width)
    pair_part = product(sides, pair_w2)
    pair_part = pair_part + from_sib(pair_part)
    pairs_half = pair_part.shape[0] // 2
    piece = lax.dynamic_slice_in_dim(pair_part, c * pairs_half, pairs_half, 0)
    piece, x_txt = lax.optimization_barrier((piece, x_txt))
    other = from_x(piece)
    if docs > 1:
        text(1, x_txt)
    piece, x_txt = lax.optimization_barrier((piece + later(other, txt_sums[-1]), x_txt))
    pair_pre = jnp.concatenate(by_core(piece, from_sib(piece)), axis=0) + pair_bias
    root = 0.5 * (1.0 + lax.erf(pair_pre * ROOT_HALF))
    pair_act = pair_pre * root
    logits = product(pair_act, dir_w)
    grad_dir_w = product(cot_logits, pair_act, ((0,), (0,)))
    grad_pair_pre = product(cot_logits, dir_w, ((1,), (1,))) * (
        root + pair_pre * jnp.exp(-0.5 * pair_pre * pair_pre) * DENSITY
    )
    grad_pair_bias = jnp.sum(grad_pair_pre, axis=0)
    grad_pair_w = product(sides, grad_pair_pre, ((0,), (0,)))
    grad_sides = product(grad_pair_pre, pair_w2, ((1,), (1,)))
    grad_received = product(pick_left, grad_sides[:, :share], ((0,), (0,))) + product(
        pick_right, grad_sides[:, share:], ((0,), (0,))
    )
    grad_received, x_txt = lax.optimization_barrier((grad_received, x_txt))
    grad_sent = swap_rows(grad_received)
    for doc in range(2, docs):
        text(doc, x_txt)
    grad_sent = later(grad_sent, txt_sums[-1])
    back_order = jnp.zeros_like(ordering).at[ordering].set(jnp.arange(seg_rows, dtype=jnp.int32))
    grad_cols = jnp.take(grad_sent, back_order, axis=0).reshape(docs, 2, half_seg, share)
    rows_of = lambda who: lax.dynamic_index_in_dim(grad_cols, who, 1, keepdims=False).reshape(
        docs * half_seg, share
    )
    grad_mine, grad_theirs = rows_of(c), from_sib(rows_of(1 - c))
    chip_cols = jnp.concatenate(by_core(grad_mine, grad_theirs), axis=1)
    far_cols = from_x(chip_cols)
    low_x = m < 2
    grad_seg = jnp.concatenate(
        [jnp.where(low_x, chip_cols, far_cols), jnp.where(low_x, far_cols, chip_cols)], axis=1
    )
    cot_seg = lax.dynamic_slice_in_dim(
        cot_out.reshape(docs, slots, width), TEXT + c * half_seg, half_seg, 1
    ).reshape(docs * half_seg, width)
    output = join_rows(
        docs, segs, place, seg["out"], txt["out"],
        from_sib(seg["out"]), from_sib(later(txt["out"], grad_cols)),
    )
    grad_seg, output = lax.optimization_barrier((grad_seg, output))
    back = ffn(
        place, vec, bias_rows, weights, docs * half_seg, txt_rows, mine_rows,
        [seg[name] for name in ("n1", "f1", "n2", "f2", "slope")],
        ctx=ctx_seg, gout=cot_seg + grad_seg,
        into={name: txt[name] for name in ("gs", "gi0", "gi1", "gf")},
    )

    tall = ((0,), (0,))
    sib_back = from_sib(product(txt["act1"], back["gs"], tall))
    sib_in = from_sib(product(txt["h1"], back["gi1"], tall))
    grad_back_own = product(txt["act0"], back["gs"], tall) + sib_back
    grad_in_own = product(txt["h1"], back["gi0"], tall) + sib_in
    gf_txt, gf_seg = back["gf"][:txt_rows], back["gf"][txt_rows:]
    gwo = sum(gwo) + back["gwo"]
    grad_out_own = gwo[:part] + from_sib(gwo[part:])

    steps = Steps()
    steps.add("in_out", ring(jnp.concatenate([grad_in_own, grad_out_own], axis=0), 1, (width, part)))
    back_pair = jnp.concatenate([grad_back_own, grad_pair_w], axis=0)
    steps.add("back_pair", ring(back_pair, -1, (width, 2 * share)))
    mine = (back["gb"], txt["gb"])
    theirs = tuple(from_sib(g) for g in mine)
    w_sum = jnp.zeros((3 * part, width), F32)
    b_sum = jnp.zeros((1, 3 * part), F32)
    gx = []
    for doc in range(docs):

        def scores(b_sum, doc=doc):
            return attn_bwd(
                doc, place, text_len, qkv, lse, (both_seg, both_txt), mine, theirs, b_sum
            )

        def weights_of(gq, w_sum, doc=doc):
            return qkv_bwd(
                all_rows, doc, docs, place, hidden_in, roi, stats, bn_gain, bn_bias, w_qkv, gq, w_sum
            )

        gq, b_sum = steps.run(scores, (b_sum,))
        gx_mine, gx_theirs, w_sum = steps.run(weights_of, (gq, w_sum))
        chip_sum = gx_mine + from_sib(gx_theirs)
        gx.append((chip_sum, from_x(chip_sum)))
    cut = w_sum.shape[0] * 5 // 9
    qkv_steps = Steps()
    qkv_steps.add("qkv_low", halving(w_sum[:cut], 0))
    qkv_steps.add("qkv_high", halving(w_sum[cut:], 1))
    qkv_steps.finish()
    gh_mine, gh_theirs = [], []
    for doc in range(docs):
        first = jnp.concatenate(
            [gf_seg[doc * half_seg : (doc + 1) * half_seg], gf_txt[doc * half : (doc + 1) * half]],
            axis=0,
        )
        if doc:
            steps.run()
        (far,) = steps.run(lambda doc=doc: (gx[doc][1],))
        gh_mine.append(first + (gx[doc][0] + far))
        gh_theirs.append(from_sib(gh_mine[-1]))
    (gh_theirs[-1],) = steps.run(lambda: (gh_theirs[-1],))
    grad_hidden, bn_sums = final_rows(all_rows, segs, place, gh_mine, gh_theirs, roi, stats)

    rows = sum(txt_sums) + back["sums"]
    rows = jnp.concatenate([rows[:6], rows[6:7]]) + from_sib(jnp.concatenate([rows[:6], rows[7:8]]))
    pad = lambda v: jnp.pad(v, (0, width - v.shape[0]))[None]
    vectors = jnp.concatenate(
        [
            rows,
            grad_pair_bias[None],
            grad_dir_w,
            pad(b_sum[0, :part]),
            pad(b_sum[0, 2 * part :]),
            bn_sums[0:2],
        ],
        axis=0,
    )
    steps.add("vectors", cube(vectors))
    steps.finish()
    steps.results.update(qkv_steps.results)
    vectors, in_out, back_pair, low, high = (
        steps.results[name] for name in ("vectors", "in_out", "back_pair", "qkv_low", "qkv_high")
    )
    sum_qkv = jnp.concatenate([low, high], axis=0)
    n_dirs = dir_w.shape[1]
    sum_dir_w = vectors[8 : 8 + n_dirs].T
    tail = vectors[8 + n_dirs :]
    sum_bias_qv = tail[0:2, :part]
    grad_bn_bias, grad_bn_gain = tail[2], tail[3]
    grad_roi_out = grad_hidden.reshape(docs, slots, width)[:, TEXT:].reshape(seg_rows, width)
    roi_factor = lax.rsqrt(stats[1] / all_rows + EPSILON)
    roi_normed = (roi - stats[0]) * roi_factor
    grad_roi = (
        bn_gain
        * roi_factor
        * (grad_roi_out - grad_bn_bias / all_rows - roi_normed * grad_bn_gain / all_rows)
    )
    return (
        output,
        logits,
        grad_hidden,
        grad_roi,
        grad_bn_gain,
        grad_bn_bias,
        jnp.transpose(sum_qkv.reshape(3, part, width), (0, 2, 1)),
        sum_bias_qv,
        in_out[1],
        vectors[5],
        vectors[3],
        vectors[4],
        in_out[0],
        vectors[6],
        back_pair[0],
        vectors[2],
        vectors[0],
        vectors[1],
        back_pair[1].reshape(2, share, width),
        vectors[7],
        sum_dir_w,
    )


def solution(mesh):
    placed = (
        P("dp", None),
        P("dp", None),
        P(),
        P(),
        P(None, None, "mp"),
        P(None, "mp"),
        P("mp", None),
        P(),
        P(),
        P(),
        P(None, "mp"),
        P("mp"),
        P("mp", None),
        P(),
        P(),
        P(),
        P(None, "mp", None),
        P(),
        P(),
        P("dp"),
        P("dp", None),
        P("dp", None),
        P("dp", None),
        P("dp", None),
    )
    return jax.shard_map(
        per_device,
        mesh=mesh,
        in_specs=placed,
        out_specs=(
            P("dp", None),
            P("dp", None),
            P("dp", None),
            P("dp", None),
            P(),
            P(),
            P(None, None, "mp"),
            P(None, "mp"),
            P("mp", None),
            P(),
            P(),
            P(),
            P(None, "mp"),
            P("mp"),
            P("mp", None),
            P(),
            P(),
            P(),
            P(None, "mp", None),
            P(),
            P(),
        ),
        check_vma=False,
    )
```
